512 devices in a mesh: rep: 32 (over z_lo, y), tp: 16 (over x, z_hi, core).
Axes of the slice: x: 4, y: 4, z: 16 (z_hi: 2, z_lo: 8; z = z_hi * 8 + z_lo), core: 2. Of those that a mesh axis runs over, the one named last changes fastest.
Arguments:
- queries: bfloat16 [4, 512, 8192], P(None, 'rep', 'tp'), may hold values from -240 to 240
- new_kv: bfloat16 [4, 512, 2048], P(None, 'rep', 'tp'), may hold values from -6 to 6
- kv_pool: bfloat16 [2048, 16, 16, 256], P('rep', 'tp'), may hold values from -6 to 6
- page_table: int32 [512, 8], P('rep'), may hold values from 0 to 63, as said below
- kv_lengths: int32 [512], replicated, may hold values from 1 to 128
- slot_source: int32 [512], replicated, may hold values from 0 to 511, as said below
- mamba_x: bfloat16 [4, 512, 16384], P(None, 'rep', 'tp'), may hold values from -6 to 6
- mamba_z: bfloat16 [4, 512, 16384], P(None, 'rep', 'tp'), may hold values from -6 to 6
- conv_state: bfloat16 [512, 3, 16384], P('rep', None, 'tp'), may hold values from -6 to 6
- ssm_state: float32 [512, 16, 16384], P('rep', None, 'tp'), may hold values from -6 to 6
- x_proj_weight: bfloat16 [544, 16384], P(None, 'tp'), may hold values from -0.046875 to 0.046875
- dt_proj_weight: bfloat16 [512, 16384], P(None, 'tp'), may hold values from -0.25 to 0.25
- dt_bias: float32 [16384], P('tp'), may hold values from -3 to 0.5
- a_rate: float32 [16, 16384], P(None, 'tp'), may hold values from 0.02 to 8
- skip_gain: float32 [16384], P('tp'), may hold values from 0.5 to 2
- conv_weight: float32 [4, 16384], P(None, 'tp'), may hold values from -3 to 3
- conv_bias: float32 [16384], P('tp'), may hold values from -3 to 3
- dt_gain: float32 [512], replicated, may hold values from 0.25 to 1.75
- b_gain: float32 [16], replicated, may hold values from 0.25 to 1.75
- c_gain: float32 [16], replicated, may hold values from 0.25 to 1.75
Outputs:
- attention_out: bfloat16 [4, 512, 8192], P(None, 'rep', 'tp')
- mixer_out: bfloat16 [4, 512, 16384], P(None, 'rep', 'tp')
The draws below stay inside these ranges and needn't reach their ends.
Inputs may be any that keep to these rules, and one draw needn't show every extreme that they name: `slot_source`: A permutation of the slots. In each group exactly 2 slots take a request from another group, from 2 different groups, and each group gives exactly 2 requests away; every other slot keeps its own request. `page_table`: within a group, the pool pages of all its requests' even pages are distinct, and so are those of the odd pages.
All inputs are finite; a program needn't handle non-finite values.
Results may differ from the reference program's by a relative error of at most 0.008.
Values may be sent and summed in bfloat16 or wider, within the bound.
A program may use at most 64 MiB of HBM per device.

```python
import math
from functools import partial
import jax
import jax.numpy as jnp
from jax import lax

REQS = 16
HEADS_DEV = 4
STATE = 16
DT_RANK = 512
CONV = 4
HEAD_DIM = 128
PAGE = 16
PAGES_REQ = 8
STEPS = 4
MOVE = 2
D_INNER = 16384
HEADS = 64
KV_HEADS = 8
N_REQ = 512
LMAX = 128
POOL = 64
POOL_ALL = 2048
N_REP = 32


def draw_slot_source(key, part):
    key = jax.random.fold_in(key, 11)
    relabel_key, offset_key, slot_key = jax.random.split(key, 3)
    relabel = jax.random.permutation(relabel_key, N_REP).astype(jnp.int32)
    position = jnp.argsort(relabel, stable=True).astype(jnp.int32)
    offsets = jax.random.permutation(offset_key, N_REP - 1)[:MOVE].astype(jnp.int32) + 1
    chosen = jax.vmap(lambda subkey: jax.random.permutation(subkey, REQS)[:MOVE])(jax.random.split(slot_key, N_REP)).astype(jnp.int32)
    groups = jnp.arange(N_REP, dtype=jnp.int32)
    source = jnp.arange(N_REP * REQS, dtype=jnp.int32)
    for move_index in range(MOVE):
        donors = relabel[(position + offsets[move_index]) % N_REP]
        source = source.at[groups * REQS + chosen[:, move_index]].set(donors * REQS + chosen[donors, move_index])
    return source


def draw_page_table(key, part):
    key = jax.random.fold_in(key, 12)
    per_parity = REQS * PAGES_REQ // 2
    orders = jax.vmap(lambda subkey: jax.random.permutation(subkey, per_parity))(jax.random.split(key, N_REP * 2)).astype(jnp.int32)
    orders = orders.reshape(N_REP, 2, REQS, PAGES_REQ // 2)
    return jnp.transpose(orders, (0, 2, 3, 1)).reshape(N_REP * REQS, PAGES_REQ)


def draw_kv_lengths(key, part):
    key = jax.random.fold_in(key, 13)
    length_key, load_key, longest_key = jax.random.split(key, 3)
    raw_lengths = jax.random.randint(length_key, (N_REP, REQS), 1, LMAX + 1, dtype=jnp.int32)
    shifts = jax.random.randint(load_key, (N_REP, 1), 0, 3, dtype=jnp.int32)
    lengths = jnp.maximum(jnp.right_shift(raw_lengths, shifts), 1).reshape(-1)
    longest = jax.random.randint(longest_key, (), 0, N_REP * REQS, dtype=jnp.int32)
    return lengths.at[longest].set(LMAX).astype(jnp.int32)


def draw_queries(key, part):
    key = jax.random.fold_in(key, 14)
    base_key = jax.random.fold_in(key, 0)
    values = jnp.clip(jax.random.normal(base_key, (STEPS, N_REQ, HEADS * HEAD_DIM), jnp.float32), -6.0, 6.0)
    return values.astype(jnp.bfloat16)


def shard_levels(own_key, shape, cuts, least, largest):
    def one(dim, parts):
        draws = jax.random.uniform(jax.random.fold_in(jax.random.fold_in(own_key, 6), dim), (parts,), jnp.float32, least / len(cuts), largest / len(cuts))
        return jnp.repeat(jnp.exp(draws), shape[dim] // parts).reshape((-1,) + (1,) * (len(shape) - dim - 1))

    loudness = one(*cuts[0])
    for cut in cuts[1:]:
        loudness = loudness * one(*cut)
    return loudness


def centred(rng, dims, width, limit, cuts=(), held_as=jnp.bfloat16):
    level = shard_levels(rng, dims, cuts, -0.22, 0.18) if cuts else 1.0
    values = jax.random.normal(rng, dims, jnp.float32) * width * level
    return jnp.minimum(jnp.maximum(values, -limit), limit).astype(held_as)


def setup_inputs(seed: int = 0) -> dict:
    seeds = jax.random.split(jax.random.key(seed), 21)
    return {
        "queries": draw_queries(jax.random.fold_in(seeds[20], 71), 0),
        "new_kv": centred(seeds[1], (STEPS, N_REQ, 2 * KV_HEADS * HEAD_DIM), 1.0, 6.0, ((1, 32), (2, 16))),
        "kv_pool": centred(seeds[2], (POOL_ALL, 2 * KV_HEADS, PAGE, 2 * HEAD_DIM), 1.0, 6.0, ((0, 32), (1, 16))),
        "page_table": draw_page_table(jax.random.fold_in(seeds[20], 71), 0),
        "kv_lengths": draw_kv_lengths(jax.random.fold_in(seeds[20], 71), 0),
        "slot_source": draw_slot_source(jax.random.fold_in(seeds[20], 71), 0),
        "mamba_x": centred(seeds[6], (STEPS, N_REQ, D_INNER), 1.0, 6.0, ((1, 32), (2, 16))),
        "mamba_z": centred(seeds[7], (STEPS, N_REQ, D_INNER), 1.0, 6.0, ((1, 32), (2, 16))),
        "conv_state": centred(seeds[8], (N_REQ, CONV - 1, D_INNER), 1.0, 6.0, ((0, 32), (2, 16))),
        "ssm_state": centred(seeds[9], (N_REQ, STATE, D_INNER), 1.0, 6.0, ((0, 32), (2, 16)), jnp.float32),
        "x_proj_weight": centred(seeds[10], (DT_RANK + 2 * STATE, D_INNER), D_INNER ** -0.5, 0.046875, ((1, 16),)),
        "dt_proj_weight": centred(seeds[11], (DT_RANK, D_INNER), DT_RANK ** -0.5, 0.25, ((1, 16),)),
        "dt_bias": jnp.clip(-3.0 + 3.5 * jax.random.uniform(seeds[12], (D_INNER,), jnp.float32) ** shard_levels(seeds[12], (D_INNER,), ((0, 16),), -0.2, 0.2), -3.0, 0.5),
        "a_rate": jnp.clip(jnp.exp(math.log(8.0) - 5.9914646 * jax.random.uniform(seeds[13], (STATE, D_INNER), jnp.float32) ** shard_levels(seeds[13], (STATE, D_INNER), ((1, 16),), -0.2, 0.2)), 0.02, 8.0),
        "skip_gain": jnp.clip(jnp.exp(math.log(2.0) - 1.3862944 * jax.random.uniform(seeds[14], (D_INNER,), jnp.float32) ** shard_levels(seeds[14], (D_INNER,), ((0, 16),), -0.2, 0.2)), 0.5, 2.0),
        "conv_weight": centred(seeds[15], (CONV, D_INNER), CONV ** -0.5, 3.0, ((1, 16),), jnp.float32),
        "conv_bias": centred(seeds[16], (D_INNER,), 0.5, 3.0, ((0, 16),), jnp.float32),
        "dt_gain": jnp.clip(1.0 + 0.15 * jax.random.normal(seeds[17], (DT_RANK,), jnp.float32), 0.25, 1.75),
        "b_gain": jnp.clip(1.0 + 0.15 * jax.random.normal(seeds[18], (STATE,), jnp.float32), 0.25, 1.75),
        "c_gain": jnp.clip(1.0 + 0.15 * jax.random.normal(seeds[19], (STATE,), jnp.float32), 0.25, 1.75),
    }


epsilon = 1e-06

def rms_scale(values, gain):
    return values * lax.rsqrt(lax.optimization_barrier(jnp.mean(values * values, axis=-1, keepdims=True)) + epsilon) * gain

def mixer_group(inputs, weights):
    x_steps, z_steps, conv_rows, scan_state = inputs
    x_proj_weight, dt_proj_weight, dt_bias, a_rate, skip_gain, conv_weight, conv_bias, dt_gain, b_gain, c_gain = weights
    outputs = []
    for step_idx in range(x_steps.shape[0]):
        window = jnp.concatenate([conv_rows, x_steps[step_idx][:, None, :]], axis=1)
        activ = jax.nn.silu(lax.optimization_barrier(jnp.sum(window.astype(jnp.float32) * conv_weight[None], axis=1)) + conv_bias)
        conv_rows = window[:, 1:, :]
        projected = jnp.dot(activ.astype(jnp.bfloat16), x_proj_weight.T, preferred_element_type=jnp.float32)
        dt_low = rms_scale(projected[:, :DT_RANK], dt_gain).astype(jnp.bfloat16)
        b_vector = rms_scale(projected[:, DT_RANK:DT_RANK + STATE], b_gain)
        c_vector = rms_scale(projected[:, DT_RANK + STATE:], c_gain)
        dt_step = jax.nn.softplus(jnp.dot(dt_low, dt_proj_weight, preferred_element_type=jnp.float32) + dt_bias)
        scan_state = jnp.exp(-dt_step[:, None, :] * a_rate[None]) * scan_state + dt_step[:, None, :] * b_vector[:, :, None] * activ[:, None, :]
        mixed = lax.optimization_barrier(jnp.sum(c_vector[:, :, None] * scan_state, axis=1)) + skip_gain * activ
        outputs.append((mixed * jax.nn.silu(z_steps[step_idx].astype(jnp.float32))).astype(jnp.bfloat16))
    return (jnp.stack(outputs), conv_rows, scan_state)

def mixer_phase(x_steps, z_steps, conv_rows, scan_state, weights):
    step_count = x_steps.shape[0]
    grouped = (jnp.moveaxis(x_steps.reshape(step_count, N_REP, REQS, -1), 1, 0), jnp.moveaxis(z_steps.reshape(step_count, N_REP, REQS, -1), 1, 0), conv_rows.reshape((N_REP, REQS) + conv_rows.shape[1:]), scan_state.reshape((N_REP, REQS) + scan_state.shape[1:]))
    outputs, conv_out, state_out = lax.map(partial(mixer_group, weights=weights), grouped)
    outputs = jnp.moveaxis(outputs, 0, 1).reshape(step_count, N_REQ, -1)
    return (outputs, conv_out.reshape(conv_rows.shape), state_out.reshape(scan_state.shape))

def attend(query_rows, key_rows, key_mask):
    keys = key_rows[..., :HEAD_DIM].astype(jnp.float32)
    values = key_rows[..., HEAD_DIM:].astype(jnp.float32)
    scores = jnp.einsum('snhd,nkd->snhk', query_rows.astype(jnp.float32), keys) / math.sqrt(HEAD_DIM)
    scores = jnp.where(key_mask[:, :, None, :], scores, -jnp.inf)
    weights = jax.nn.softmax(scores, axis=-1)
    return jnp.einsum('snhk,nkd->snhd', weights, values)

def step_mask(count, offset):
    allowed = jnp.arange(count)[None, :] <= offset + jnp.arange(2)[:, None]
    return jnp.broadcast_to(allowed[:, None, :], (2, N_REQ, count))

def head_group(head_index, queries, new_kv, kv_pool, page_table, kv_lengths, slot_source):
    owner = jnp.arange(N_REQ, dtype=jnp.int32) // REQS
    pool_rows = owner[:, None] * POOL + page_table
    tp_ranks = 2 * head_index + jnp.arange(PAGES_REQ, dtype=jnp.int32) % 2
    cache_rows = kv_pool[pool_rows, tp_ranks[None, :]].reshape(N_REQ, LMAX, 2 * HEAD_DIM)
    group_queries = lax.dynamic_slice_in_dim(queries.reshape(STEPS, N_REQ, HEADS, HEAD_DIM), head_index * 2 * HEADS_DEV, 2 * HEADS_DEV, 2)
    fresh_kv = lax.dynamic_index_in_dim(new_kv.reshape(STEPS, N_REQ, KV_HEADS, 2 * HEAD_DIM), head_index, 2, keepdims=False)
    positions = jnp.arange(LMAX)
    cache_mask = jnp.broadcast_to((positions[None, :] < kv_lengths[:, None])[None], (2, N_REQ, LMAX))
    extras = jnp.swapaxes(fresh_kv[0:2], 0, 1)
    first_out = attend(group_queries[0:2], jnp.concatenate([cache_rows, extras], axis=1), jnp.concatenate([cache_mask, step_mask(2, 0)], axis=-1))
    moved_cache = cache_rows[slot_source]
    moved_mask = jnp.broadcast_to((positions[None, :] < kv_lengths[slot_source][:, None])[None], (2, N_REQ, LMAX))
    moved_extras = jnp.concatenate([jnp.swapaxes(fresh_kv[0:2][:, slot_source], 0, 1), jnp.swapaxes(fresh_kv[2:4], 0, 1)], axis=1)
    second_out = attend(group_queries[2:4], jnp.concatenate([moved_cache, moved_extras], axis=1), jnp.concatenate([moved_mask, step_mask(4, 2)], axis=-1))
    return jnp.concatenate([first_out, second_out], axis=0)

def reference(queries, new_kv, kv_pool, page_table, kv_lengths, slot_source, mamba_x, mamba_z, conv_state, ssm_state, x_proj_weight, dt_proj_weight, dt_bias, a_rate, skip_gain, conv_weight, conv_bias, dt_gain, b_gain, c_gain):
    weights = (x_proj_weight, dt_proj_weight, dt_bias, a_rate, skip_gain, conv_weight, conv_bias, dt_gain, b_gain, c_gain)
    mixer_first, conv_mid, state_mid = mixer_phase(mamba_x[0:2], mamba_z[0:2], conv_state, ssm_state, weights)
    mixer_second, conv_end, state_end = mixer_phase(mamba_x[2:4], mamba_z[2:4], conv_mid[slot_source], state_mid[slot_source], weights)
    attention = lax.map(partial(head_group, queries=queries, new_kv=new_kv, kv_pool=kv_pool, page_table=page_table, kv_lengths=kv_lengths, slot_source=slot_source), jnp.arange(KV_HEADS, dtype=jnp.int32))
    attention_out = jnp.transpose(attention, (1, 2, 0, 3, 4)).reshape(STEPS, N_REQ, HEADS * HEAD_DIM).astype(jnp.bfloat16)
    return (attention_out, jnp.concatenate([mixer_first, mixer_second], axis=0))
```

```python
import functools

import jax
import jax.numpy as jnp
from jax import lax
from jax.experimental import pallas as pl
from jax.experimental.pallas import tpu as pltpu
from jax.sharding import PartitionSpec as P

F32 = jnp.float32
BF16 = jnp.bfloat16
I32 = jnp.int32
EPS = 1e-06
MASKED = -1e30
SCALE = 128**-0.5


def geometry(mesh):
    rep, tp = mesh.shape["rep"], mesh.shape["tp"]
    ny = 4 if rep >= 16 else 2
    return (rep // ny, ny, tp // 4)


def nn(a, b):
    return lax.dot_general(a, b, (((1,), (0,)), ((), ())), preferred_element_type=F32)


def nt(a, b):
    return lax.dot_general(a, b, (((1,), (1,)), ((), ())), preferred_element_type=F32)


def hot(cond):
    return jnp.where(cond, 1.0, 0.0).astype(BF16)


def iota(shape, dim):
    return lax.broadcasted_iota(I32, shape, dim)


def silu(v):
    return v / (1.0 + jnp.exp(-v))


def softplus(v):
    return jnp.maximum(v, 0.0) + jnp.log1p(jnp.exp(-jnp.abs(v)))


def attend(q_rows, keys, values, extra_keys, extra_values, bias, extra_bias):
    scores = nt(q_rows, keys) * SCALE + bias
    extra = nt(q_rows, extra_keys) * SCALE + extra_bias
    peak = jnp.maximum(
        jnp.max(scores, axis=1, keepdims=True), jnp.max(extra, axis=1, keepdims=True)
    )
    weight = jnp.exp(scores - peak)
    extra_weight = jnp.exp(extra - peak)
    total = jnp.sum(weight, axis=1, keepdims=True) + jnp.sum(extra_weight, axis=1, keepdims=True)
    out = nn(weight.astype(BF16), values) + nn(extra_weight.astype(BF16), extra_values)
    lane = iota((q_rows.shape[0], 128), 1)
    return out, jnp.where(lane < 64, peak, total)


def combine(near, far):
    near_peak, near_sum = near[:, 128:129], near[:, 192:193]
    far_peak, far_sum = far[:, 128:129], far[:, 192:193]
    peak = jnp.maximum(near_peak, far_peak)
    near_scale = jnp.exp(near_peak - peak)
    far_scale = jnp.exp(far_peak - peak)
    numer = near[:, :128] * near_scale + far[:, :128] * far_scale
    return numer / (near_sum * near_scale + far_sum * far_scale)


def tail_norm(tail):
    lane = iota(tail.shape, 1)
    square = tail * tail
    mean_b = jnp.sum(jnp.where(lane < 16, square, 0.0), axis=1, keepdims=True) / 16.0
    mean_c = jnp.sum(
        jnp.where((lane >= 16) & (lane < 32), square, 0.0), axis=1, keepdims=True
    ) / 16.0
    scale = jnp.where(lane < 16, lax.rsqrt(mean_b + EPS), lax.rsqrt(mean_c + EPS))
    return jnp.where(lane < 32, tail * scale, 0.0)


def by_quarter(blocks):
    quarter = iota(blocks[0].shape, 0) >> 2
    return jnp.where(
        quarter == 0,
        blocks[0],
        jnp.where(quarter == 1, blocks[1], jnp.where(quarter == 2, blocks[2], blocks[3])),
    )


def kernel(
    geo,
    src_s,
    src_ref,
    len_ref,
    page_ref,
    q_ref,
    nk_ref,
    x_ref,
    z_ref,
    conv_ref,
    dtb_ref,
    a_ref,
    skip_ref,
    cw_ref,
    cb_ref,
    dtg_ref,
    bg_ref,
    cg_ref,
    pool_hbm,
    ssm_hbm,
    xw_hbm,
    dw_hbm,
    attn_ref,
    mix_ref,
    pool,
    ssm,
    xw,
    dw,
    mid,
    act,
    dts,
    mixed,
    dtl,
    tails,
    gather_in,
    stage_y,
    land_y,
    land_o,
    q_other,
    nk_other,
    part,
    part_land,
    half_send,
    half_land,
    norm_send,
    norm_land,
    near,
    away,
    far,
    late_send,
    late_land,
    late_half,
    late_half_land,
    late_away,
    late_far,
    gather_out,
    stage_r,
    land_r,
    bias_ref,
    mask_ref,
    ssem,
    rsem,
    lsem,
):
    nz, ny, nx = geo
    no = 2 * nx
    rpo = 64 // no
    n = src_ref.shape[1]
    rep, tp = lax.axis_index("rep"), lax.axis_index("tp")
    zi, yi = rep // ny, rep % ny
    core, zh, xi = tp % 2, (tp // 2) % 2, tp // 4
    own = xi * 2 + core
    tp_other = tp + 1 - 2 * core
    tp_half = tp + 2 - 4 * zh

    def o_tp(d):
        o = (own + d) % no
        return (o // 2) * 4 + zh * 2 + o % 2

    def z_rep(d):
        return ((zi + d) % nz) * ny + yi

    def y_rep(e):
        return zi * ny + (yi + e) % ny

    partners = [(z_rep(d), tp) for d in range(1, nz)]
    partners += [(y_rep(e), tp) for e in range(1, ny)]
    partners += [(y_rep(e), tp_other) for e in range(1, ny)]
    partners += [(rep, o_tp(d)) for d in range(1, no)]
    partners += [(rep, tp_half)]
    barrier = pltpu.get_barrier_semaphore()
    for device in partners:
        pl.semaphore_signal(
            barrier, inc=1, device_id=device, device_id_type=pl.DeviceIdType.MESH
        )

    loads = []
    for k, (a, b) in enumerate(((xw_hbm, xw), (pool_hbm, pool), (dw_hbm, dw), (ssm_hbm, ssm))):
        load = pltpu.make_async_copy(a, b, lsem.at[k])
        load.start()
        loads.append(load)

    used = []

    def push(src, dst, device):
        k = len(used)
        copy = pltpu.make_async_remote_copy(
            src_ref=src,
            dst_ref=dst,
            send_sem=ssem.at[k],
            recv_sem=rsem.at[k],
            device_id=device,
            device_id_type=pl.DeviceIdType.MESH,
        )
        copy.start()
        used.append(copy)
        return copy

    src = src_ref[...]
    lane_n = iota((1, n), 1)
    foreign = src != lane_n
    foreign16 = jnp.broadcast_to(hot(foreign), (16, n))
    slot_pick = hot(iota((128, n), 1) == rep * 16 + (iota((128, n), 0) & 15))
    f128 = nt(foreign16, slot_pick)
    before = hot(
        (iota((128, 128), 0) < 16) & (iota((128, 128), 0) < (iota((128, 128), 1) & 15))
    )
    k128 = nn(f128.astype(BF16), before)
    row = iota((16, 128), 0)
    col = iota((16, 128), 1)
    rank = ((row >> 1) & 1).astype(F32)
    place = (f128 > 0.5) & (k128 == rank)
    pack = hot(place & ((row >> 2) == ((col >> 4) & 3)) & ((row & 1) == (col >> 6)))
    pick16 = hot(place & (col < 16))[:, :16]

    blocks = []
    nothing = jnp.zeros((16, 256), BF16)
    for s in (2, 3):
        x_s = x_ref[s]
        q_s = q_ref[s]
        nk_s = nk_ref[s]
        for b in range(4):
            side = (
                q_s[:, b * 256 : (b + 1) * 256]
                if b < 2
                else (jnp.concatenate([nk_s, nothing[:, :128]], axis=1) if b == 2 else nothing)
            )
            blocks.append(jnp.concatenate([x_s[:, b * 256 : (b + 1) * 256], side], axis=1))
    gather_in[0] = nn(pack, jnp.concatenate(blocks, axis=0)).astype(BF16)

    pl.semaphore_wait(barrier, len(partners))

    z_in = [push(gather_in.at[0], gather_in.at[d], (z_rep(d), tp)) for d in range(1, nz)]
    q_swap = push(q_ref, q_other, (rep, tp_other))
    nk_swap = push(nk_ref, nk_other, (rep, tp_other))

    conv = conv_ref[...].astype(F32)
    window = [conv[:, w, :] for w in range(3)] + [x_ref[s].astype(F32) for s in range(4)]
    conv_last = window[2].astype(BF16)
    cw = cw_ref[...]
    cb = cb_ref[...]
    activ = []
    for s in range(4):
        total = window[s] * cw[0:1]
        for w in range(1, 4):
            total = total + window[s + w] * cw[w : w + 1]
        activ.append(silu(total + cb))
        act[s] = activ[s]
    activ_b = jnp.concatenate([v.astype(BF16) for v in activ], axis=0)
    loads[0].wait()

    def project(rows):
        tail = jnp.concatenate([xw[512:544, :], jnp.zeros((96, 1024), BF16)], axis=0)
        return nt(rows, xw[0:512, :]), nt(rows, tail)

    main, tail = project(activ_b)
    for o in range(no):
        part[o, :, 0:512] = main[o * rpo : (o + 1) * rpo]
        part[o, :, 512:640] = tail[o * rpo : (o + 1) * rpo]
    part_out = [
        push(part.at[(own + d) % no], part_land.at[d], (rep, o_tp(d))) for d in range(1, no)
    ]

    same = iota((n, n), 0)
    lane_nn = iota((n, n), 1)
    rank16 = nn(foreign16, hot(((same >> 4) == (lane_nn >> 4)) & (same < lane_nn)))
    rank_there = nn(rank16.astype(BF16), hot(same == src))
    home = jnp.where(foreign, (lane_n >> 4) * 2 + rank16[0:1].astype(I32), -1)
    donor = jnp.where(foreign, (src >> 4) * 2 + rank_there[0:1].astype(I32), -1)
    to_row = iota((ny * 16, n), 0)
    to_code = (zi * ny + ((yi + (to_row >> 4)) & (ny - 1))) * 2 + ((to_row >> 1) & 1)
    from_row = iota((nz * 16, n), 0)
    from_code = (((zi - (from_row >> 4)) & (nz - 1)) * ny + yi) * 2 + ((from_row >> 1) & 1)
    r_ = iota((ny * 16, nz * 16), 0)
    c_ = iota((ny * 16, nz * 16), 1)
    alike = ((r_ >> 2) & 3 == (c_ >> 2) & 3) & ((r_ & 1) == (c_ & 1))
    select_in = hot(alike & (nt(hot(donor == to_code), hot(home == from_code)) > 0.5))
    select_out = hot(alike & (nt(hot(home == to_code), hot(donor == from_code)) > 0.5))

    own_lane = iota((16, n), 1) == rep * 16 + iota((16, n), 0)
    lengths = jnp.sum(jnp.where(own_lane, len_ref[...], 0), axis=1, keepdims=True)
    foreign_col = (
        jnp.sum(jnp.where(own_lane & foreign, 1.0, 0.0), axis=1, keepdims=True) > 0.5
    )
    table = page_ref[...]
    cache_lane = iota((16, 1024), 1)
    allowed = jnp.zeros((16, 1024), F32)
    for k in range(4):
        page = jnp.where(core == 0, table[:, 2 * k : 2 * k + 1], table[:, 2 * k + 1 : 2 * k + 2])
        limit = lengths - (2 * k + core) * 16
        allowed = jnp.where(
            ((cache_lane >> 4) == page) & ((cache_lane & 15) < limit), 1.0, allowed
        )
    mask_ref[...] = allowed.astype(BF16)
    bias_ref[...] = jnp.where(allowed > 0.5, 0.0, MASKED)

    for copy in z_in:
        copy.wait_recv()
    chosen = nn(select_in, gather_in[...].reshape(nz * 16, 512)).astype(BF16)
    for e in range(ny):
        stage_y[e] = chosen[e * 16 : (e + 1) * 16]
    land_y[0] = chosen[0:16]
    y_in = [push(stage_y.at[e], land_y.at[e], (y_rep(e), tp)) for e in range(1, ny)]
    y_in += [
        push(stage_y.at[e, :, 256:512], land_o.at[e], (y_rep(e), tp_other)) for e in range(ny)
    ]

    for copy in part_out:
        copy.wait_recv()
    summed = part[own]
    for d in range(1, no):
        summed = summed + part_land[d]
    blank = jnp.zeros((rpo, 128), F32)

    def pack_half(v):
        return jnp.concatenate(
            [
                jnp.concatenate([v[:, 0:256], v[:, 512:640]], axis=1),
                jnp.concatenate([v[:, 256:512], blank], axis=1),
            ],
            axis=0,
        ).astype(BF16)

    def unpack_half(v):
        v = v.astype(F32)
        return jnp.concatenate([v[:rpo, 0:256], v[rpo:, 0:256], v[:rpo, 256:384]], axis=1)

    half_send[...] = pack_half(summed)
    half = push(half_send, half_land, (rep, tp_half))

    loads[1].wait()
    q_swap.wait_recv()
    nk_swap.wait_recv()
    pages = pool[...].reshape(1024, 256)
    keys, values = pages[:, 0:128], pages[:, 128:256]
    pad64 = jnp.zeros((64, 128), BF16)
    new_keys = [nk_ref[s] for s in range(4)]
    new_values = [nk_other[s] for s in range(4)]
    extra_keys = jnp.concatenate(new_keys + [pad64], axis=0)
    extra_values = jnp.concatenate(new_values + [pad64], axis=0)
    row_q = iota((256, 128), 0)
    col_q = iota((256, 128), 1)
    extra_bias = jnp.where(
        ((row_q & 15) == (col_q & 15)) & ((col_q >> 4) <= (row_q >> 6)) & (core == 0), 0.0, MASKED
    )
    bias16 = bias_ref[...]
    bias = jnp.concatenate([bias16] * 16, axis=0)
    for source, target in ((q_other, away), (q_ref, near)):
        rows = jnp.concatenate(
            [source[s][:, h * 128 : (h + 1) * 128] for s in range(4) for h in range(4)], axis=0
        )
        out, stats = attend(rows, keys, values, extra_keys, extra_values, bias, extra_bias)
        target[:, 0:128] = out
        target[:, 128:256] = stats
        if target is away:
            partial = push(away, far, (rep, tp_other))

    for copy in y_in:
        copy.wait_recv()
    er = iota((128, ny * 16), 0)
    ec = iota((128, ny * 16), 1)
    wanted_step = jnp.where(er < 64, er & 1, 0)
    expand = hot(
        (((er >> 4) & 3) == ((ec >> 2) & 3))
        & (((er >> 1) & 1) == ((ec >> 1) & 1))
        & (wanted_step == (ec & 1))
    )
    arrived = nn(expand, land_y[...].reshape(ny * 16, 512))
    arrived_o = nn(expand[0:64], land_o[...].reshape(ny * 16, 256))
    x_now = jnp.concatenate([arrived[b * 16 : (b + 1) * 16, 0:256] for b in range(4)], axis=1)
    x_prev = jnp.concatenate(
        [arrived[64 + b * 16 : 64 + (b + 1) * 16, 0:256] for b in range(4)], axis=1
    )
    last_row = nn(pick16, conv_last)
    x_zero = nn(pick16, x_ref[0])
    x_one = nn(pick16, x_ref[1])
    odd = (iota((16, 1024), 0) & 1) == 1
    total = jnp.where(odd, x_zero, last_row) * cw[0:1]
    total = total + jnp.where(odd, x_one, x_zero) * cw[1:2]
    total = total + jnp.where(odd, x_prev, x_one) * cw[2:3]
    total = total + x_now * cw[3:4]
    late_act = silu(total + cb)
    main, tail = project(late_act.astype(BF16))
    late_own = jnp.concatenate(
        [by_quarter([main[:, b * 128 : (b + 1) * 128] for b in range(4)]), tail], axis=1
    )
    late_send[...] = late_own.astype(BF16)
    late_out = [push(late_send, late_land.at[d], (rep, o_tp(d))) for d in range(1, no)]

    half.wait_recv()
    summed = summed + unpack_half(half_land[...])
    main = summed[:, 0:512]
    mean = jnp.sum(main * main, axis=1, keepdims=True) / 512.0
    low = main * lax.rsqrt(mean + EPS) * dtg_ref[...]
    normed = jnp.concatenate([low, tail_norm(summed[:, 512:640])], axis=1)
    packed = pack_half(normed)
    norm_send[...] = packed
    norm_out = [push(norm_send, norm_land.at[d], (rep, o_tp(d))) for d in range(1, no)]

    def take(o, v):
        v = unpack_half(v)
        start = pl.multiple_of(o * rpo, rpo)
        dtl[pl.ds(start, rpo), :] = v[:, 0:512]
        tails[pl.ds(start, rpo), :] = v[:, 512:640]

    take(own, packed)

    q_late = jnp.concatenate(
        [
            v[(h // 2) * 16 : (h // 2) * 16 + 8, off + (h % 2) * 128 : off + (h % 2) * 128 + 128]
            for v, off in ((arrived, 256), (arrived_o, 0))
            for h in range(4)
        ],
        axis=0,
    ).astype(BF16)
    pad48 = jnp.zeros((48, 128), BF16)
    late_keys = jnp.concatenate(
        new_keys + [arrived[32:48, 256:384].astype(BF16), pad48], axis=0
    )
    late_values = jnp.concatenate(
        new_values + [arrived_o[32:48, 0:128].astype(BF16), pad48], axis=0
    )
    fits = (place & (col < 32)) | (
        (col >= 64)
        & (col < 68)
        & (((col >> 1) & 1) == ((row >> 1) & 1))
        & ((col & 1) <= (row & 1))
    )
    late_extra = jnp.where(fits & (core == 0), 0.0, MASKED)[0:8]
    late_bias = jnp.where(nn(pick16, mask_ref[...]) > 0.5, 0.0, MASKED)[0:8]
    out, stats = attend(
        q_late,
        keys,
        values,
        late_keys,
        late_values,
        jnp.concatenate([late_bias] * 8, axis=0),
        jnp.concatenate([late_extra] * 8, axis=0),
    )
    late_near = jnp.concatenate([out[0:32], stats[0:32]], axis=1)
    late_away[...] = jnp.concatenate([out[32:64], stats[32:64]], axis=1)
    late_partial = push(late_away, late_far, (rep, tp_other))

    for copy in late_out:
        copy.wait_recv()
    late_sum = late_own
    for d in range(1, no):
        late_sum = late_sum + late_land[d].astype(F32)
    late_half[...] = late_sum.astype(BF16)
    late_swap = push(late_half, late_half_land, (rep, tp_half))

    for d, copy in enumerate(norm_out, 1):
        copy.wait_recv()
        take((own - d + no) % no, norm_land[d])
    loads[2].wait()
    steps = softplus(nn(dtl[...].astype(BF16), dw[...]) + dtb_ref[...])
    for s in range(4):
        dts[s] = steps[s * 16 : (s + 1) * 16]
    eye = iota((16, 16), 0) == iota((16, 16), 1)
    b_gain = jnp.sum(jnp.where(eye, bg_ref[...], 0.0), axis=1, keepdims=True)
    c_gain = jnp.sum(jnp.where(eye, cg_ref[...], 0.0), axis=1, keepdims=True)
    skip = skip_ref[...]
    loads[3].wait()

    def columns(tail_row):
        b = jnp.sum(jnp.where(col == row, tail_row, 0.0), axis=1, keepdims=True) * b_gain
        c = jnp.sum(jnp.where(col == row + 16, tail_row, 0.0), axis=1, keepdims=True) * c_gain
        return b, c

    def advance(state, dt_row, act_row, tail_row):
        b, c = columns(tail_row)
        state = jnp.exp(-dt_row * a_ref[...]) * state + (dt_row * act_row) * b
        return state, jnp.sum(state * c, axis=0, keepdims=True) + skip * act_row

    def scan(first, held, keep):
        def body(i, carry):
            state = held[i]
            for s in (first, first + 1):
                state, out = advance(
                    state,
                    dts[s, pl.ds(i, 1), :],
                    act[s, pl.ds(i, 1), :],
                    tails[pl.ds(s * 16 + i, 1), :],
                )
                mixed[s, pl.ds(i, 1), :] = out
            if keep:
                mid[i] = state
            return carry

        lax.fori_loop(0, 16, body, 0)

    scan(0, ssm, True)

    late_swap.wait_recv()
    late_sum = late_sum + late_half_land[...].astype(F32)
    main = late_sum[:, 0:128]
    square = jnp.broadcast_to(jnp.sum(main * main, axis=1, keepdims=True), (16, 128))
    square = square + pltpu.roll(square, 8, 0)
    square = square + pltpu.roll(square, 4, 0)
    gain = dtg_ref[...]
    gains = by_quarter(
        [jnp.broadcast_to(gain[:, b * 128 : (b + 1) * 128], (16, 128)) for b in range(4)]
    )
    low = (main * lax.rsqrt(square / 512.0 + EPS) * gains).astype(BF16)
    wr = iota((64, 16), 0)
    wc = iota((64, 16), 1)
    spread = nn(hot(((wr >> 4) == (wc >> 2)) & ((wr & 3) == (wc & 3))), low)
    low = jnp.concatenate([spread[b * 16 : (b + 1) * 16] for b in range(4)], axis=1)
    late_dt = softplus(nn(low.astype(BF16), dw[...]) + dtb_ref[...])
    late_tail = tail_norm(late_sum[:, 128:256])

    base = rep * 16
    first = jnp.int32(-1)
    second = jnp.int32(0)
    for i in range(16):
        moves = src_s[base + i] != base + i
        second = jnp.where(moves & (first >= 0), i, second)
        first = jnp.where(moves & (first < 0), i, first)
    first = jnp.maximum(first, 0)
    rows = iota((16, 1024), 0) & 3
    late_mixed = jnp.zeros((16, 1024), F32)
    for r, slot in enumerate((first, second)):
        state = mid[slot]
        for s in range(2):
            m = r * 2 + s
            state, out = advance(
                state, late_dt[m : m + 1], late_act[m : m + 1], late_tail[m : m + 1]
            )
            late_mixed = jnp.where(rows == m, out, late_mixed)
    late_partial.wait_recv()
    heads = combine(late_near, late_far[...]).astype(BF16)
    hr = iota((16, 32), 0)
    hc = iota((16, 32), 1)
    heads = nn(hot(((hr >> 2) == (hc >> 3)) & ((hr & 3) == (hc & 7))), heads)
    quarter = by_quarter([late_mixed[:, b * 256 : (b + 1) * 256] for b in range(4)])
    gather_out[0] = jnp.concatenate([quarter, heads], axis=1).astype(BF16)
    z_out = [push(gather_out.at[0], gather_out.at[d], (z_rep(d), tp)) for d in range(1, nz)]

    scan(2, mid, False)
    partial.wait_recv()
    kept = []
    for s in range(4):
        block = combine(near[s * 64 : (s + 1) * 64, :], far[s * 64 : (s + 1) * 64, :])
        block = jnp.concatenate([block[h * 16 : (h + 1) * 16] for h in range(4)], axis=1)
        if s < 2:
            attn_ref[s] = block.astype(BF16)
            mix_ref[s] = (mixed[s] * silu(z_ref[s].astype(F32))).astype(BF16)
        else:
            kept.append(block)

    for copy in z_out:
        copy.wait_recv()
    chosen = nn(select_out, gather_out[...].reshape(nz * 16, 384)).astype(BF16)
    for e in range(ny):
        stage_r[e] = chosen[e * 16 : (e + 1) * 16]
    land_r[0] = chosen[0:16]
    y_out = [push(stage_r.at[e], land_r.at[e], (y_rep(e), tp)) for e in range(1, ny)]
    own_code = rep * 2 + ((iota((ny * 16, n), 0) >> 1) & 1)
    fr = iota((128, ny * 16), 0)
    fc = iota((128, ny * 16), 1)
    put = hot(
        (((fr >> 4) & 3) == ((fc >> 2) & 3))
        & ((fr >> 6) == (fc & 1))
        & (nt(slot_pick, hot(home == own_code)) > 0.5)
    )
    for copy in y_out:
        copy.wait_recv()
    returned = nn(put, land_r[...].reshape(ny * 16, 384))
    for s in (2, 3):
        pieces = [returned[(s - 2) * 64 + b * 16 : (s - 2) * 64 + b * 16 + 16] for b in range(4)]
        back = jnp.concatenate([v[:, 0:256] for v in pieces], axis=1)
        whole = jnp.where(foreign_col, back, mixed[s])
        mix_ref[s] = (whole * silu(z_ref[s].astype(F32))).astype(BF16)
        back = jnp.concatenate([v[:, 256:384] for v in pieces], axis=1)
        attn_ref[s] = jnp.where(foreign_col, back, kept[s - 2]).astype(BF16)

    for copy in used:
        copy.wait_send()


def shards(
    geo,
    queries,
    new_kv,
    kv_pool,
    page_table,
    kv_lengths,
    slot_source,
    mamba_x,
    mamba_z,
    conv_state,
    ssm_state,
    x_proj_weight,
    dt_proj_weight,
    dt_bias,
    a_rate,
    skip_gain,
    conv_weight,
    conv_bias,
    dt_gain,
    b_gain,
    c_gain,
):
    nz, ny, nx = geo
    no = 2 * nx
    rpo = 64 // no
    copies = (
        (nz - 1) + 2 + (no - 1) + (ny - 1) + ny + 1 + 1 + (no - 1) + (no - 1) + 1 + 1
        + (nz - 1) + (ny - 1)
    )
    vmem = pl.BlockSpec(memory_space=pltpu.VMEM)
    scratch = [
        pltpu.VMEM(kv_pool.shape, BF16),
        pltpu.VMEM(ssm_state.shape, F32),
        pltpu.VMEM(x_proj_weight.shape, BF16),
        pltpu.VMEM(dt_proj_weight.shape, BF16),
        pltpu.VMEM((16, 16, 1024), F32),
        pltpu.VMEM((4, 16, 1024), F32),
        pltpu.VMEM((4, 16, 1024), F32),
        pltpu.VMEM((4, 16, 1024), F32),
        pltpu.VMEM((64, 512), F32),
        pltpu.VMEM((64, 128), F32),
        pltpu.VMEM((nz, 16, 512), BF16),
        pltpu.VMEM((ny, 16, 512), BF16),
        pltpu.VMEM((ny, 16, 512), BF16),
        pltpu.VMEM((ny, 16, 256), BF16),
        pltpu.VMEM((4, 16, 512), BF16),
        pltpu.VMEM((4, 16, 128), BF16),
        pltpu.VMEM((no, rpo, 640), F32),
        pltpu.VMEM((no, rpo, 640), F32),
        pltpu.VMEM((2 * rpo, 384), BF16),
        pltpu.VMEM((2 * rpo, 384), BF16),
        pltpu.VMEM((2 * rpo, 384), BF16),
        pltpu.VMEM((no, 2 * rpo, 384), BF16),
        pltpu.VMEM((256, 256), F32),
        pltpu.VMEM((256, 256), F32),
        pltpu.VMEM((256, 256), F32),
        pltpu.VMEM((16, 256), BF16),
        pltpu.VMEM((no, 16, 256), BF16),
        pltpu.VMEM((16, 256), BF16),
        pltpu.VMEM((16, 256), BF16),
        pltpu.VMEM((32, 256), F32),
        pltpu.VMEM((32, 256), F32),
        pltpu.VMEM((nz, 16, 384), BF16),
        pltpu.VMEM((ny, 16, 384), BF16),
        pltpu.VMEM((ny, 16, 384), BF16),
        pltpu.VMEM((16, 1024), F32),
        pltpu.VMEM((16, 1024), BF16),
        pltpu.SemaphoreType.DMA((copies,)),
        pltpu.SemaphoreType.DMA((copies,)),
        pltpu.SemaphoreType.DMA((4,)),
    ]
    return pl.pallas_call(
        functools.partial(kernel, geo),
        out_shape=(
            jax.ShapeDtypeStruct(queries.shape, BF16),
            jax.ShapeDtypeStruct(mamba_x.shape, BF16),
        ),
        in_specs=[pl.BlockSpec(memory_space=pltpu.SMEM)]
        + [vmem] * 16
        + [pl.BlockSpec(memory_space=pl.ANY)] * 4,
        out_specs=(vmem, vmem),
        scratch_shapes=scratch,
        compiler_params=pltpu.CompilerParams(
            collective_id=0, has_side_effects=True, vmem_limit_bytes=48 * 1024 * 1024
        ),
    )(
        slot_source,
        slot_source.reshape(1, -1),
        kv_lengths.reshape(1, -1),
        page_table,
        queries,
        new_kv,
        mamba_x,
        mamba_z,
        conv_state,
        dt_bias.reshape(1, -1),
        a_rate,
        skip_gain.reshape(1, -1),
        conv_weight,
        conv_bias.reshape(1, -1),
        dt_gain.reshape(1, -1),
        b_gain.reshape(1, -1),
        c_gain.reshape(1, -1),
        kv_pool,
        ssm_state,
        x_proj_weight,
        dt_proj_weight,
    )


def solution(mesh):
    placed = (
        P(None, "rep", "tp"),
        P(None, "rep", "tp"),
        P("rep", "tp", None, None),
        P("rep", None),
        P(),
        P(),
        P(None, "rep", "tp"),
        P(None, "rep", "tp"),
        P("rep", None, "tp"),
        P("rep", None, "tp"),
        P(None, "tp"),
        P(None, "tp"),
        P("tp"),
        P(None, "tp"),
        P("tp"),
        P(None, "tp"),
        P("tp"),
        P(),
        P(),
        P(),
    )
    return jax.shard_map(
        functools.partial(shards, geometry(mesh)),
        mesh=mesh,
        in_specs=placed,
        out_specs=(P(None, "rep", "tp"), P(None, "rep", "tp")),
        check_vma=False,
    )
```

```python
import functools

import jax
import jax.numpy as jnp
from jax import lax
from jax.experimental import pallas as pl
from jax.experimental.pallas import tpu as pltpu
from jax.sharding import PartitionSpec as P

F32 = jnp.float32
BF16 = jnp.bfloat16
I32 = jnp.int32
EPS = 1e-06
MASKED = -1e30
SCALE = 128**-0.5


def geometry(mesh):
    rep, tp = mesh.shape["rep"], mesh.shape["tp"]
    ny = 4 if rep >= 16 else 2
    return (rep // ny, ny, tp // 4)


def nn(a, b):
    return lax.dot_general(a, b, (((1,), (0,)), ((), ())), preferred_element_type=F32)


def nt(a, b):
    return lax.dot_general(a, b, (((1,), (1,)), ((), ())), preferred_element_type=F32)


def hot(cond):
    return jnp.where(cond, 1.0, 0.0).astype(BF16)


def iota(shape, dim):
    return lax.broadcasted_iota(I32, shape, dim)


def silu(v):
    return v / (1.0 + jnp.exp(-v))


def softplus(v):
    return jnp.maximum(v, 0.0) + jnp.log1p(jnp.exp(-jnp.abs(v)))


def attend(q_rows, keys, values, extra_keys, extra_values, bias, extra_bias):
    scores = nt(q_rows, keys) * SCALE + bias
    extra = nt(q_rows, extra_keys) * SCALE + extra_bias
    peak = jnp.maximum(
        jnp.max(scores, axis=1, keepdims=True), jnp.max(extra, axis=1, keepdims=True)
    )
    weight = jnp.exp(scores - peak)
    extra_weight = jnp.exp(extra - peak)
    total = jnp.sum(weight, axis=1, keepdims=True) + jnp.sum(extra_weight, axis=1, keepdims=True)
    out = nn(weight.astype(BF16), values) + nn(extra_weight.astype(BF16), extra_values)
    lane = iota((q_rows.shape[0], 128), 1)
    return out, jnp.where(lane < 64, peak, total)


def combine(near, far):
    near_peak, near_sum = near[:, 128:129], near[:, 192:193]
    far_peak, far_sum = far[:, 128:129], far[:, 192:193]
    peak = jnp.maximum(near_peak, far_peak)
    near_scale = jnp.exp(near_peak - peak)
    far_scale = jnp.exp(far_peak - peak)
    numer = near[:, :128] * near_scale + far[:, :128] * far_scale
    return numer / (near_sum * near_scale + far_sum * far_scale)


def tail_norm(tail):
    lane = iota(tail.shape, 1)
    square = tail * tail
    mean_b = jnp.sum(jnp.where(lane < 16, square, 0.0), axis=1, keepdims=True) / 16.0
    mean_c = jnp.sum(
        jnp.where((lane >= 16) & (lane < 32), square, 0.0), axis=1, keepdims=True
    ) / 16.0
    scale = jnp.where(lane < 16, lax.rsqrt(mean_b + EPS), lax.rsqrt(mean_c + EPS))
    return jnp.where(lane < 32, tail * scale, 0.0)


def by_quarter(blocks):
    quarter = iota(blocks[0].shape, 0) >> 2
    return jnp.where(
        quarter == 0,
        blocks[0],
        jnp.where(quarter == 1, blocks[1], jnp.where(quarter == 2, blocks[2], blocks[3])),
    )


def kernel(
    geo,
    src_ref_h,
    q_ref_h,
    nk_ref_h,
    x_ref_h,
    src_s_h,
    conv_ref_h,
    cw_ref_h,
    cb_ref_h,
    xw_h,
    page_ref_h,
    len_ref_h,
    pool_h,
    dtg_ref_h,
    dw_h,
    dtb_ref_h,
    bg_ref_h,
    cg_ref_h,
    skip_ref_h,
    a_ref_h,
    ssm_h,
    z_ref_h,
    attn_ref,
    mix_ref,
    src_ref,
    q_ref,
    nk_ref,
    x_ref,
    src_s,
    conv_ref,
    cw_ref,
    cb_ref,
    xw,
    page_ref,
    len_ref,
    pool,
    dtg_ref,
    dw,
    dtb_ref,
    bg_ref,
    cg_ref,
    skip_ref,
    a_ref,
    ssm,
    z_ref,
    mid,
    act,
    dts,
    mixed,
    dtl,
    tails,
    gather_in,
    stage_y,
    land_y,
    land_o,
    q_other,
    nk_other,
    part,
    part_land,
    half_send,
    half_land,
    norm_send,
    norm_land,
    near,
    away,
    far,
    late_send,
    late_land,
    late_half,
    late_half_land,
    late_away,
    late_far,
    gather_out,
    stage_r,
    land_r,
    bias_ref,
    mask_ref,
    ssem,
    rsem,
    lsem,
):
    nz, ny, nx = geo
    no = 2 * nx
    rpo = 64 // no
    n = src_ref.shape[1]
    rep, tp = lax.axis_index("rep"), lax.axis_index("tp")
    zi, yi = rep // ny, rep % ny
    core, zh, xi = tp % 2, (tp // 2) % 2, tp // 4
    own = xi * 2 + core
    tp_other = tp + 1 - 2 * core
    tp_half = tp + 2 - 4 * zh

    def o_tp(d):
        o = (own + d) % no
        return (o // 2) * 4 + zh * 2 + o % 2

    def z_rep(d):
        return ((zi + d) % nz) * ny + yi

    def y_rep(e):
        return zi * ny + (yi + e) % ny

    partners = [(z_rep(d), tp) for d in range(1, nz)]
    partners += [(y_rep(e), tp) for e in range(1, ny)]
    partners += [(y_rep(e), tp_other) for e in range(1, ny)]
    partners += [(rep, o_tp(d)) for d in range(1, no)]
    partners += [(rep, tp_half)]
    barrier = pltpu.get_barrier_semaphore()
    for device in partners:
        pl.semaphore_signal(
            barrier, inc=1, device_id=device, device_id_type=pl.DeviceIdType.MESH
        )

    loads = {}
    for k, (name, a, b) in enumerate(
        (
            ("src_ref", src_ref_h, src_ref),
            ("q_ref", q_ref_h, q_ref),
            ("nk_ref", nk_ref_h, nk_ref),
            ("x_ref", x_ref_h, x_ref),
            ("src_s", src_s_h, src_s),
            ("conv_ref", conv_ref_h, conv_ref),
            ("cw_ref", cw_ref_h, cw_ref),
            ("cb_ref", cb_ref_h, cb_ref),
            ("xw", xw_h, xw),
            ("page_ref", page_ref_h, page_ref),
            ("len_ref", len_ref_h, len_ref),
            ("pool", pool_h, pool),
            ("dtg_ref", dtg_ref_h, dtg_ref),
            ("dw", dw_h, dw),
            ("dtb_ref", dtb_ref_h, dtb_ref),
            ("bg_ref", bg_ref_h, bg_ref),
            ("cg_ref", cg_ref_h, cg_ref),
            ("skip_ref", skip_ref_h, skip_ref),
            ("a_ref", a_ref_h, a_ref),
            ("ssm", ssm_h, ssm),
            ("z_ref", z_ref_h, z_ref),
        )
    ):
        loads[name] = pltpu.make_async_copy(a, b, lsem.at[k])
        loads[name].start()

    def need(*names):
        for name in names:
            loads[name].wait()

    used = []

    def push(src, dst, device):
        k = len(used)
        copy = pltpu.make_async_remote_copy(
            src_ref=src,
            dst_ref=dst,
            send_sem=ssem.at[k],
            recv_sem=rsem.at[k],
            device_id=device,
            device_id_type=pl.DeviceIdType.MESH,
        )
        copy.start()
        used.append(copy)
        return copy

    need("src_ref")
    src = src_ref[...]
    lane_n = iota((1, n), 1)
    foreign = src != lane_n
    foreign16 = jnp.broadcast_to(hot(foreign), (16, n))
    slot_pick = hot(iota((128, n), 1) == rep * 16 + (iota((128, n), 0) & 15))
    f128 = nt(foreign16, slot_pick)
    before = hot(
        (iota((128, 128), 0) < 16) & (iota((128, 128), 0) < (iota((128, 128), 1) & 15))
    )
    k128 = nn(f128.astype(BF16), before)
    row = iota((16, 128), 0)
    col = iota((16, 128), 1)
    rank = ((row >> 1) & 1).astype(F32)
    place = (f128 > 0.5) & (k128 == rank)
    pack = hot(place & ((row >> 2) == ((col >> 4) & 3)) & ((row & 1) == (col >> 6)))
    pick16 = hot(place & (col < 16))[:, :16]

    need("q_ref", "nk_ref", "x_ref")
    blocks = []
    nothing = jnp.zeros((16, 256), BF16)
    for s in (2, 3):
        x_s = x_ref[s]
        q_s = q_ref[s]
        nk_s = nk_ref[s]
        for b in range(4):
            side = (
                q_s[:, b * 256 : (b + 1) * 256]
                if b < 2
                else (jnp.concatenate([nk_s, nothing[:, :128]], axis=1) if b == 2 else nothing)
            )
            blocks.append(jnp.concatenate([x_s[:, b * 256 : (b + 1) * 256], side], axis=1))
    gather_in[0] = nn(pack, jnp.concatenate(blocks, axis=0)).astype(BF16)

    pl.semaphore_wait(barrier, len(partners))

    z_in = [push(gather_in.at[0], gather_in.at[d], (z_rep(d), tp)) for d in range(1, nz)]
    q_swap = push(q_ref, q_other, (rep, tp_other))
    nk_swap = push(nk_ref, nk_other, (rep, tp_other))

    need("conv_ref", "cw_ref", "cb_ref")
    window = [conv_ref[w].astype(F32) for w in range(3)] + [x_ref[s].astype(F32) for s in range(4)]
    conv_last = window[2].astype(BF16)
    cw = cw_ref[...]
    cb = cb_ref[...]
    activ = []
    for s in range(4):
        total = window[s] * cw[0:1]
        for w in range(1, 4):
            total = total + window[s + w] * cw[w : w + 1]
        activ.append(silu(total + cb))
        act[s] = activ[s]
    activ_b = jnp.concatenate([v.astype(BF16) for v in activ], axis=0)
    need("xw")

    def project(rows):
        tail = jnp.concatenate([xw[512:544, :], jnp.zeros((96, 1024), BF16)], axis=0)
        return nt(rows, xw[0:512, :]), nt(rows, tail)

    main, tail = project(activ_b)
    for o in range(no):
        part[o, :, 0:512] = main[o * rpo : (o + 1) * rpo]
        part[o, :, 512:640] = tail[o * rpo : (o + 1) * rpo]
    part_out = [
        push(part.at[(own + d) % no], part_land.at[d], (rep, o_tp(d))) for d in range(1, no)
    ]

    same = iota((n, n), 0)
    lane_nn = iota((n, n), 1)
    rank16 = nn(foreign16, hot(((same >> 4) == (lane_nn >> 4)) & (same < lane_nn)))
    rank_there = nn(rank16.astype(BF16), hot(same == src))
    home = jnp.where(foreign, (lane_n >> 4) * 2 + rank16[0:1].astype(I32), -1)
    donor = jnp.where(foreign, (src >> 4) * 2 + rank_there[0:1].astype(I32), -1)
    to_row = iota((ny * 16, n), 0)
    to_code = (zi * ny + ((yi + (to_row >> 4)) & (ny - 1))) * 2 + ((to_row >> 1) & 1)
    from_row = iota((nz * 16, n), 0)
    from_code = (((zi - (from_row >> 4)) & (nz - 1)) * ny + yi) * 2 + ((from_row >> 1) & 1)
    r_ = iota((ny * 16, nz * 16), 0)
    c_ = iota((ny * 16, nz * 16), 1)
    alike = ((r_ >> 2) & 3 == (c_ >> 2) & 3) & ((r_ & 1) == (c_ & 1))
    select_in = hot(alike & (nt(hot(donor == to_code), hot(home == from_code)) > 0.5))
    select_out = hot(alike & (nt(hot(home == to_code), hot(donor == from_code)) > 0.5))

    need("page_ref", "len_ref")
    own_lane = iota((16, n), 1) == rep * 16 + iota((16, n), 0)
    lengths = jnp.sum(jnp.where(own_lane, len_ref[...], 0), axis=1, keepdims=True)
    foreign_col = (
        jnp.sum(jnp.where(own_lane & foreign, 1.0, 0.0), axis=1, keepdims=True) > 0.5
    )
    table = page_ref[...]
    eye = iota((16, 16), 0) == iota((16, 16), 1)
    cache_lane = iota((16, 1024), 1)
    allowed = jnp.zeros((16, 1024), F32)
    for k in range(4):
        page = jnp.where(core == 0, table[2 * k : 2 * k + 1], table[2 * k + 1 : 2 * k + 2])
        page = jnp.sum(jnp.where(eye, page, 0), axis=1, keepdims=True)
        limit = lengths - (2 * k + core) * 16
        allowed = jnp.where(
            ((cache_lane >> 4) == page) & ((cache_lane & 15) < limit), 1.0, allowed
        )
    mask_ref[...] = allowed.astype(BF16)
    bias_ref[...] = jnp.where(allowed > 0.5, 0.0, MASKED)

    for copy in z_in:
        copy.wait_recv()
    chosen = nn(select_in, gather_in[...].reshape(nz * 16, 512)).astype(BF16)
    for e in range(ny):
        stage_y[e] = chosen[e * 16 : (e + 1) * 16]
    land_y[0] = chosen[0:16]
    y_in = [push(stage_y.at[e], land_y.at[e], (y_rep(e), tp)) for e in range(1, ny)]
    y_in += [
        push(stage_y.at[e, :, 256:512], land_o.at[e], (y_rep(e), tp_other)) for e in range(ny)
    ]

    for copy in part_out:
        copy.wait_recv()
    summed = part[own]
    for d in range(1, no):
        summed = summed + part_land[d]
    blank = jnp.zeros((rpo, 128), F32)

    def pack_half(v):
        return jnp.concatenate(
            [
                jnp.concatenate([v[:, 0:256], v[:, 512:640]], axis=1),
                jnp.concatenate([v[:, 256:512], blank], axis=1),
            ],
            axis=0,
        ).astype(BF16)

    def unpack_half(v):
        v = v.astype(F32)
        return jnp.concatenate([v[:rpo, 0:256], v[rpo:, 0:256], v[:rpo, 256:384]], axis=1)

    half_send[...] = pack_half(summed)
    half = push(half_send, half_land, (rep, tp_half))

    need("pool")
    q_swap.wait_recv()
    nk_swap.wait_recv()
    pages = pool[...].reshape(1024, 256)
    keys, values = pages[:, 0:128], pages[:, 128:256]
    pad64 = jnp.zeros((64, 128), BF16)
    new_keys = [nk_ref[s] for s in range(4)]
    new_values = [nk_other[s] for s in range(4)]
    extra_keys = jnp.concatenate(new_keys + [pad64], axis=0)
    extra_values = jnp.concatenate(new_values + [pad64], axis=0)
    row_q = iota((256, 128), 0)
    col_q = iota((256, 128), 1)
    extra_bias = jnp.where(
        ((row_q & 15) == (col_q & 15)) & ((col_q >> 4) <= (row_q >> 6)) & (core == 0), 0.0, MASKED
    )
    bias16 = bias_ref[...]
    bias = jnp.concatenate([bias16] * 16, axis=0)
    for source, target in ((q_other, away), (q_ref, near)):
        rows = jnp.concatenate(
            [source[s][:, h * 128 : (h + 1) * 128] for s in range(4) for h in range(4)], axis=0
        )
        out, stats = attend(rows, keys, values, extra_keys, extra_values, bias, extra_bias)
        target[:, 0:128] = out
        target[:, 128:256] = stats
        if target is away:
            partial = push(away, far, (rep, tp_other))

    for copy in y_in:
        copy.wait_recv()
    er = iota((128, ny * 16), 0)
    ec = iota((128, ny * 16), 1)
    wanted_step = jnp.where(er < 64, er & 1, 0)
    expand = hot(
        (((er >> 4) & 3) == ((ec >> 2) & 3))
        & (((er >> 1) & 1) == ((ec >> 1) & 1))
        & (wanted_step == (ec & 1))
    )
    arrived = nn(expand, land_y[...].reshape(ny * 16, 512))
    arrived_o = nn(expand[0:64], land_o[...].reshape(ny * 16, 256))
    x_now = jnp.concatenate([arrived[b * 16 : (b + 1) * 16, 0:256] for b in range(4)], axis=1)
    x_prev = jnp.concatenate(
        [arrived[64 + b * 16 : 64 + (b + 1) * 16, 0:256] for b in range(4)], axis=1
    )
    last_row = nn(pick16, conv_last)
    x_zero = nn(pick16, x_ref[0])
    x_one = nn(pick16, x_ref[1])
    odd = (iota((16, 1024), 0) & 1) == 1
    total = jnp.where(odd, x_zero, last_row) * cw[0:1]
    total = total + jnp.where(odd, x_one, x_zero) * cw[1:2]
    total = total + jnp.where(odd, x_prev, x_one) * cw[2:3]
    total = total + x_now * cw[3:4]
    late_act = silu(total + cb)
    main, tail = project(late_act.astype(BF16))
    late_own = jnp.concatenate(
        [by_quarter([main[:, b * 128 : (b + 1) * 128] for b in range(4)]), tail], axis=1
    )
    late_send[...] = late_own.astype(BF16)
    late_out = [push(late_send, late_land.at[d], (rep, o_tp(d))) for d in range(1, no)]

    need("dtg_ref")
    half.wait_recv()
    summed = summed + unpack_half(half_land[...])
    main = summed[:, 0:512]
    mean = jnp.sum(main * main, axis=1, keepdims=True) / 512.0
    low = main * lax.rsqrt(mean + EPS) * dtg_ref[...]
    normed = jnp.concatenate([low, tail_norm(summed[:, 512:640])], axis=1)
    packed = pack_half(normed)
    norm_send[...] = packed
    norm_out = [push(norm_send, norm_land.at[d], (rep, o_tp(d))) for d in range(1, no)]

    def take(o, v):
        v = unpack_half(v)
        start = pl.multiple_of(o * rpo, rpo)
        dtl[pl.ds(start, rpo), :] = v[:, 0:512]
        tails[pl.ds(start, rpo), :] = v[:, 512:640]

    take(own, packed)

    q_late = jnp.concatenate(
        [
            v[(h // 2) * 16 : (h // 2) * 16 + 8, off + (h % 2) * 128 : off + (h % 2) * 128 + 128]
            for v, off in ((arrived, 256), (arrived_o, 0))
            for h in range(4)
        ],
        axis=0,
    ).astype(BF16)
    pad48 = jnp.zeros((48, 128), BF16)
    late_keys = jnp.concatenate(
        new_keys + [arrived[32:48, 256:384].astype(BF16), pad48], axis=0
    )
    late_values = jnp.concatenate(
        new_values + [arrived_o[32:48, 0:128].astype(BF16), pad48], axis=0
    )
    fits = (place & (col < 32)) | (
        (col >= 64)
        & (col < 68)
        & (((col >> 1) & 1) == ((row >> 1) & 1))
        & ((col & 1) <= (row & 1))
    )
    late_extra = jnp.where(fits & (core == 0), 0.0, MASKED)[0:8]
    late_bias = jnp.where(nn(pick16, mask_ref[...]) > 0.5, 0.0, MASKED)[0:8]
    out, stats = attend(
        q_late,
        keys,
        values,
        late_keys,
        late_values,
        jnp.concatenate([late_bias] * 8, axis=0),
        jnp.concatenate([late_extra] * 8, axis=0),
    )
    late_near = jnp.concatenate([out[0:32], stats[0:32]], axis=1)
    late_away[...] = jnp.concatenate([out[32:64], stats[32:64]], axis=1)
    late_partial = push(late_away, late_far, (rep, tp_other))

    for copy in late_out:
        copy.wait_recv()
    late_sum = late_own
    for d in range(1, no):
        late_sum = late_sum + late_land[d].astype(F32)
    late_half[...] = late_sum.astype(BF16)
    late_swap = push(late_half, late_half_land, (rep, tp_half))

    for d, copy in enumerate(norm_out, 1):
        copy.wait_recv()
        take((own - d + no) % no, norm_land[d])
    need("dw", "dtb_ref", "bg_ref", "cg_ref", "skip_ref", "a_ref", "ssm")
    steps = softplus(nn(dtl[...].astype(BF16), dw[...]) + dtb_ref[...])
    for s in range(4):
        dts[s] = steps[s * 16 : (s + 1) * 16]
    b_gain = jnp.sum(jnp.where(eye, bg_ref[...], 0.0), axis=1, keepdims=True)
    c_gain = jnp.sum(jnp.where(eye, cg_ref[...], 0.0), axis=1, keepdims=True)
    skip = skip_ref[...]

    def columns(tail_row):
        b = jnp.sum(jnp.where(col == row, tail_row, 0.0), axis=1, keepdims=True) * b_gain
        c = jnp.sum(jnp.where(col == row + 16, tail_row, 0.0), axis=1, keepdims=True) * c_gain
        return b, c

    def advance(state, dt_row, act_row, tail_row):
        b, c = columns(tail_row)
        state = jnp.exp(-dt_row * a_ref[...]) * state + (dt_row * act_row) * b
        return state, jnp.sum(state * c, axis=0, keepdims=True) + skip * act_row

    def scan(first, held, keep):
        def body(i, carry):
            state = held[i]
            for s in (first, first + 1):
                state, out = advance(
                    state,
                    dts[s, pl.ds(i, 1), :],
                    act[s, pl.ds(i, 1), :],
                    tails[pl.ds(s * 16 + i, 1), :],
                )
                mixed[s, pl.ds(i, 1), :] = out
            if keep:
                mid[i] = state
            return carry

        lax.fori_loop(0, 16, body, 0)

    scan(0, ssm, True)

    late_swap.wait_recv()
    late_sum = late_sum + late_half_land[...].astype(F32)
    main = late_sum[:, 0:128]
    square = jnp.broadcast_to(jnp.sum(main * main, axis=1, keepdims=True), (16, 128))
    square = square + pltpu.roll(square, 8, 0)
    square = square + pltpu.roll(square, 4, 0)
    gain = dtg_ref[...]
    gains = by_quarter(
        [jnp.broadcast_to(gain[:, b * 128 : (b + 1) * 128], (16, 128)) for b in range(4)]
    )
    low = (main * lax.rsqrt(square / 512.0 + EPS) * gains).astype(BF16)
    wr = iota((64, 16), 0)
    wc = iota((64, 16), 1)
    spread = nn(hot(((wr >> 4) == (wc >> 2)) & ((wr & 3) == (wc & 3))), low)
    low = jnp.concatenate([spread[b * 16 : (b + 1) * 16] for b in range(4)], axis=1)
    late_dt = softplus(nn(low.astype(BF16), dw[...]) + dtb_ref[...])
    late_tail = tail_norm(late_sum[:, 128:256])

    need("src_s")
    base = rep * 16
    first = jnp.int32(-1)
    second = jnp.int32(0)
    for i in range(16):
        moves = src_s[base + i] != base + i
        second = jnp.where(moves & (first >= 0), i, second)
        first = jnp.where(moves & (first < 0), i, first)
    first = jnp.maximum(first, 0)
    rows = iota((16, 1024), 0) & 3
    late_mixed = jnp.zeros((16, 1024), F32)
    for r, slot in enumerate((first, second)):
        state = mid[slot]
        for s in range(2):
            m = r * 2 + s
            state, out = advance(
                state, late_dt[m : m + 1], late_act[m : m + 1], late_tail[m : m + 1]
            )
            late_mixed = jnp.where(rows == m, out, late_mixed)
    late_partial.wait_recv()
    heads = combine(late_near, late_far[...]).astype(BF16)
    hr = iota((16, 32), 0)
    hc = iota((16, 32), 1)
    heads = nn(hot(((hr >> 2) == (hc >> 3)) & ((hr & 3) == (hc & 7))), heads)
    quarter = by_quarter([late_mixed[:, b * 256 : (b + 1) * 256] for b in range(4)])
    gather_out[0] = jnp.concatenate([quarter, heads], axis=1).astype(BF16)
    z_out = [push(gather_out.at[0], gather_out.at[d], (z_rep(d), tp)) for d in range(1, nz)]

    scan(2, mid, False)
    need("z_ref")
    partial.wait_recv()
    kept = []
    for s in range(4):
        block = combine(near[s * 64 : (s + 1) * 64, :], far[s * 64 : (s + 1) * 64, :])
        block = jnp.concatenate([block[h * 16 : (h + 1) * 16] for h in range(4)], axis=1)
        if s < 2:
            attn_ref[s] = block.astype(BF16)
            mix_ref[s] = (mixed[s] * silu(z_ref[s].astype(F32))).astype(BF16)
        else:
            kept.append(block)

    for copy in z_out:
        copy.wait_recv()
    chosen = nn(select_out, gather_out[...].reshape(nz * 16, 384)).astype(BF16)
    for e in range(ny):
        stage_r[e] = chosen[e * 16 : (e + 1) * 16]
    land_r[0] = chosen[0:16]
    y_out = [push(stage_r.at[e], land_r.at[e], (y_rep(e), tp)) for e in range(1, ny)]
    own_code = rep * 2 + ((iota((ny * 16, n), 0) >> 1) & 1)
    fr = iota((128, ny * 16), 0)
    fc = iota((128, ny * 16), 1)
    put = hot(
        (((fr >> 4) & 3) == ((fc >> 2) & 3))
        & ((fr >> 6) == (fc & 1))
        & (nt(slot_pick, hot(home == own_code)) > 0.5)
    )
    for copy in y_out:
        copy.wait_recv()
    returned = nn(put, land_r[...].reshape(ny * 16, 384))
    for s in (2, 3):
        pieces = [returned[(s - 2) * 64 + b * 16 : (s - 2) * 64 + b * 16 + 16] for b in range(4)]
        back = jnp.concatenate([v[:, 0:256] for v in pieces], axis=1)
        whole = jnp.where(foreign_col, back, mixed[s])
        mix_ref[s] = (whole * silu(z_ref[s].astype(F32))).astype(BF16)
        back = jnp.concatenate([v[:, 256:384] for v in pieces], axis=1)
        attn_ref[s] = jnp.where(foreign_col, back, kept[s - 2]).astype(BF16)

    for copy in used:
        copy.wait_send()


def shards(
    geo,
    queries,
    new_kv,
    kv_pool,
    page_table,
    kv_lengths,
    slot_source,
    mamba_x,
    mamba_z,
    conv_state,
    ssm_state,
    x_proj_weight,
    dt_proj_weight,
    dt_bias,
    a_rate,
    skip_gain,
    conv_weight,
    conv_bias,
    dt_gain,
    b_gain,
    c_gain,
):
    nz, ny, nx = geo
    no = 2 * nx
    rpo = 64 // no
    copies = (
        (nz - 1) + 2 + (no - 1) + (ny - 1) + ny + 1 + 1 + (no - 1) + (no - 1) + 1 + 1
        + (nz - 1) + (ny - 1)
    )
    operands = (
        slot_source.reshape(1, -1),
        queries,
        new_kv,
        mamba_x,
        slot_source,
        conv_state.transpose(1, 0, 2),
        conv_weight,
        conv_bias.reshape(1, -1),
        x_proj_weight,
        page_table.T,
        kv_lengths.reshape(1, -1),
        kv_pool,
        dt_gain.reshape(1, -1),
        dt_proj_weight,
        dt_bias.reshape(1, -1),
        b_gain.reshape(1, -1),
        c_gain.reshape(1, -1),
        skip_gain.reshape(1, -1),
        a_rate,
        ssm_state,
        mamba_z,
    )
    vmem = pl.BlockSpec(memory_space=pltpu.VMEM)
    scratch = [
        pltpu.SMEM(v.shape, v.dtype) if k == 4 else pltpu.VMEM(v.shape, v.dtype)
        for k, v in enumerate(operands)
    ] + [
        pltpu.VMEM((16, 16, 1024), F32),
        pltpu.VMEM((4, 16, 1024), F32),
        pltpu.VMEM((4, 16, 1024), F32),
        pltpu.VMEM((4, 16, 1024), F32),
        pltpu.VMEM((64, 512), F32),
        pltpu.VMEM((64, 128), F32),
        pltpu.VMEM((nz, 16, 512), BF16),
        pltpu.VMEM((ny, 16, 512), BF16),
        pltpu.VMEM((ny, 16, 512), BF16),
        pltpu.VMEM((ny, 16, 256), BF16),
        pltpu.VMEM((4, 16, 512), BF16),
        pltpu.VMEM((4, 16, 128), BF16),
        pltpu.VMEM((no, rpo, 640), F32),
        pltpu.VMEM((no, rpo, 640), F32),
        pltpu.VMEM((2 * rpo, 384), BF16),
        pltpu.VMEM((2 * rpo, 384), BF16),
        pltpu.VMEM((2 * rpo, 384), BF16),
        pltpu.VMEM((no, 2 * rpo, 384), BF16),
        pltpu.VMEM((256, 256), F32),
        pltpu.VMEM((256, 256), F32),
        pltpu.VMEM((256, 256), F32),
        pltpu.VMEM((16, 256), BF16),
        pltpu.VMEM((no, 16, 256), BF16),
        pltpu.VMEM((16, 256), BF16),
        pltpu.VMEM((16, 256), BF16),
        pltpu.VMEM((32, 256), F32),
        pltpu.VMEM((32, 256), F32),
        pltpu.VMEM((nz, 16, 384), BF16),
        pltpu.VMEM((ny, 16, 384), BF16),
        pltpu.VMEM((ny, 16, 384), BF16),
        pltpu.VMEM((16, 1024), F32),
        pltpu.VMEM((16, 1024), BF16),
        pltpu.SemaphoreType.DMA((copies,)),
        pltpu.SemaphoreType.DMA((copies,)),
        pltpu.SemaphoreType.DMA((len(operands),)),
    ]
    return pl.pallas_call(
        functools.partial(kernel, geo),
        out_shape=(
            jax.ShapeDtypeStruct(queries.shape, BF16),
            jax.ShapeDtypeStruct(mamba_x.shape, BF16),
        ),
        in_specs=[pl.BlockSpec(memory_space=pl.ANY)] * len(operands),
        out_specs=(vmem, vmem),
        scratch_shapes=scratch,
        compiler_params=pltpu.CompilerParams(
            collective_id=0, has_side_effects=True, vmem_limit_bytes=60 * 1024 * 1024
        ),
    )(*operands)


def solution(mesh):
    placed = (
        P(None, "rep", "tp"),
        P(None, "rep", "tp"),
        P("rep", "tp", None, None),
        P("rep", None),
        P(),
        P(),
        P(None, "rep", "tp"),
        P(None, "rep", "tp"),
        P("rep", None, "tp"),
        P("rep", None, "tp"),
        P(None, "tp"),
        P(None, "tp"),
        P("tp"),
        P(None, "tp"),
        P("tp"),
        P(None, "tp"),
        P("tp"),
        P(),
        P(),
        P(),
    )
    return jax.shard_map(
        functools.partial(shards, geometry(mesh)),
        mesh=mesh,
        in_specs=placed,
        out_specs=(P(None, "rep", "tp"), P(None, "rep", "tp")),
        check_vma=False,
    )
```

```python
import functools

import jax
import jax.numpy as jnp
from jax import lax
from jax.experimental import pallas as pl
from jax.experimental.pallas import tpu as pltpu
from jax.sharding import PartitionSpec as P

F32 = jnp.float32
BF16 = jnp.bfloat16
I32 = jnp.int32
EPS = 1e-06
MASKED = -1e30
SCALE = 128**-0.5


def geometry(mesh):
    rep, tp = mesh.shape["rep"], mesh.shape["tp"]
    ny = 4 if rep >= 16 else 2
    return (rep // ny, ny, tp // 4)


def nn(a, b):
    return lax.dot_general(a, b, (((1,), (0,)), ((), ())), preferred_element_type=F32)


def nt(a, b):
    return lax.dot_general(a, b, (((1,), (1,)), ((), ())), preferred_element_type=F32)


def hot(cond):
    return jnp.where(cond, 1.0, 0.0).astype(BF16)


def iota(shape, dim):
    return lax.broadcasted_iota(I32, shape, dim)


def silu(v):
    return v / (1.0 + jnp.exp(-v))


def softplus(v):
    return jnp.maximum(v, 0.0) + jnp.log1p(jnp.exp(-jnp.abs(v)))


def attend(q_rows, keys, values, extra_keys, extra_values, bias, extra_bias):
    scores = nt(q_rows, keys) * SCALE + bias
    extra = nt(q_rows, extra_keys) * SCALE + extra_bias
    peak = jnp.maximum(
        jnp.max(scores, axis=1, keepdims=True), jnp.max(extra, axis=1, keepdims=True)
    )
    weight = jnp.exp(scores - peak)
    extra_weight = jnp.exp(extra - peak)
    total = jnp.sum(weight, axis=1, keepdims=True) + jnp.sum(extra_weight, axis=1, keepdims=True)
    out = nn(weight.astype(BF16), values) + nn(extra_weight.astype(BF16), extra_values)
    lane = iota((q_rows.shape[0], 128), 1)
    return out, jnp.where(lane < 64, peak, total)


def combine(near, far):
    near_peak, near_sum = near[:, 128:129], near[:, 192:193]
    far_peak, far_sum = far[:, 128:129], far[:, 192:193]
    peak = jnp.maximum(near_peak, far_peak)
    near_scale = jnp.exp(near_peak - peak)
    far_scale = jnp.exp(far_peak - peak)
    numer = near[:, :128] * near_scale + far[:, :128] * far_scale
    return numer / (near_sum * near_scale + far_sum * far_scale)


def tail_norm(tail):
    lane = iota(tail.shape, 1)
    square = tail * tail
    mean_b = jnp.sum(jnp.where(lane < 16, square, 0.0), axis=1, keepdims=True) / 16.0
    mean_c = jnp.sum(
        jnp.where((lane >= 16) & (lane < 32), square, 0.0), axis=1, keepdims=True
    ) / 16.0
    scale = jnp.where(lane < 16, lax.rsqrt(mean_b + EPS), lax.rsqrt(mean_c + EPS))
    return jnp.where(lane < 32, tail * scale, 0.0)


def by_quarter(blocks):
    quarter = iota(blocks[0].shape, 0) >> 2
    return jnp.where(
        quarter == 0,
        blocks[0],
        jnp.where(quarter == 1, blocks[1], jnp.where(quarter == 2, blocks[2], blocks[3])),
    )


def kernel(
    geo,
    src_ref_h,
    q_ref_h,
    nk_ref_h,
    x_ref_h,
    src_s_h,
    conv_ref_h,
    cw_ref_h,
    cb_ref_h,
    xw_h,
    page_ref_h,
    len_ref_h,
    pool_h,
    dtg_ref_h,
    dw_h,
    dtb_ref_h,
    bg_ref_h,
    cg_ref_h,
    skip_ref_h,
    a_ref_h,
    ssm_h,
    z_ref_h,
    attn_ref,
    mix_ref,
    src_ref,
    q_ref,
    nk_ref,
    x_ref,
    src_s,
    conv_ref,
    cw_ref,
    cb_ref,
    xw,
    page_ref,
    len_ref,
    pool,
    dtg_ref,
    dw,
    dtb_ref,
    bg_ref,
    cg_ref,
    skip_ref,
    a_ref,
    ssm,
    z_ref,
    mid,
    act,
    dts,
    mixed,
    dtl,
    tails,
    gather_x,
    stage_x,
    land_x,
    gather_q,
    stage_q,
    land_q,
    land_o,
    q_other,
    nk_other,
    part,
    part_land,
    half_send,
    half_land,
    norm_send,
    norm_land,
    near,
    away,
    far,
    late_send,
    late_land,
    late_half,
    late_half_land,
    late_away,
    late_far,
    gather_m,
    stage_m,
    land_m,
    gather_a,
    stage_a,
    land_a,
    bias_ref,
    mask_ref,
    ssem,
    rsem,
    lsem,
    ready,
):
    nz, ny, nx = geo
    no = 2 * nx
    rpo = 64 // no
    n = src_ref.shape[1]
    rep, tp = lax.axis_index("rep"), lax.axis_index("tp")
    zi, yi = rep // ny, rep % ny
    core, zh, xi = tp % 2, (tp // 2) % 2, tp // 4
    own = xi * 2 + core
    tp_other = tp + 1 - 2 * core
    tp_half = tp + 2 - 4 * zh

    def o_tp(d):
        o = (own + d) % no
        return (o // 2) * 4 + zh * 2 + o % 2

    def z_rep(d):
        return ((zi + d) % nz) * ny + yi

    def y_rep(e):
        return zi * ny + (yi + e) % ny

    partners = [(z_rep(d), tp) for d in range(1, nz)]
    partners += [(y_rep(e), tp) for e in range(1, ny)]
    partners += [(y_rep(e), tp_other) for e in range(1, ny)]
    partners += [(rep, o_tp(d)) for d in range(1, no)]
    mirror = ((nz - 1 - zi) * ny + yi, tp_half)
    partners += [mirror]
    barrier = pltpu.get_barrier_semaphore()
    for device in partners:
        pl.semaphore_signal(
            barrier, inc=1, device_id=device, device_id_type=pl.DeviceIdType.MESH
        )

    loads = {}
    for k, (name, a, b) in enumerate(
        (
            ("src_ref", src_ref_h, src_ref),
            ("q_ref", q_ref_h, q_ref),
            ("nk_ref", nk_ref_h, nk_ref),
            ("x_ref", x_ref_h, x_ref),
            ("src_s", src_s_h, src_s),
            ("conv_ref", conv_ref_h, conv_ref),
            ("cw_ref", cw_ref_h, cw_ref),
            ("cb_ref", cb_ref_h, cb_ref),
            ("xw", xw_h, xw),
            ("page_ref", page_ref_h, page_ref),
            ("len_ref", len_ref_h, len_ref),
            ("pool", pool_h, pool),
            ("dtg_ref", dtg_ref_h, dtg_ref),
            ("dw", dw_h, dw),
            ("dtb_ref", dtb_ref_h, dtb_ref),
            ("bg_ref", bg_ref_h, bg_ref),
            ("cg_ref", cg_ref_h, cg_ref),
            ("skip_ref", skip_ref_h, skip_ref),
            ("a_ref", a_ref_h, a_ref),
            ("ssm", ssm_h, ssm),
            ("z_ref", z_ref_h, z_ref),
        )
    ):
        loads[name] = pltpu.make_async_copy(a, b, lsem.at[k])
        loads[name].start()

    def need(*names):
        for name in names:
            loads[name].wait()

    used = []

    def push(src, dst, device):
        k = len(used)
        copy = pltpu.make_async_remote_copy(
            src_ref=src,
            dst_ref=dst,
            send_sem=ssem.at[k],
            recv_sem=rsem.at[k],
            device_id=device,
            device_id_type=pl.DeviceIdType.MESH,
        )
        copy.start()
        used.append(copy)
        return copy

    need("src_ref")
    src = src_ref[...]
    lane_n = iota((1, n), 1)
    foreign = src != lane_n
    foreign16 = jnp.broadcast_to(hot(foreign), (16, n))
    slot_pick = hot(iota((128, n), 1) == rep * 16 + (iota((128, n), 0) & 15))
    f128 = nt(foreign16, slot_pick)
    before = hot(
        (iota((128, 128), 0) < 16) & (iota((128, 128), 0) < (iota((128, 128), 1) & 15))
    )
    k128 = nn(f128.astype(BF16), before)
    row = iota((16, 128), 0)
    col = iota((16, 128), 1)
    rank = ((row >> 1) & 1).astype(F32)
    place = (f128 > 0.5) & (k128 == rank)
    pack = hot(place & ((row >> 2) == ((col >> 4) & 3)) & ((row & 1) == (col >> 6)))
    pick16 = hot(place & (col < 16))[:, :16]

    need("q_ref", "nk_ref", "x_ref")
    blocks = []
    nothing = jnp.zeros((16, 256), BF16)
    for s in (2, 3):
        x_s = x_ref[s]
        q_s = q_ref[s]
        nk_s = nk_ref[s]
        for b in range(4):
            side = (
                q_s[:, b * 256 : (b + 1) * 256]
                if b < 2
                else (jnp.concatenate([nk_s, nothing[:, :128]], axis=1) if b == 2 else nothing)
            )
            blocks.append(jnp.concatenate([x_s[:, b * 256 : (b + 1) * 256], side], axis=1))
    item = nn(pack, jnp.concatenate(blocks, axis=0)).astype(BF16)
    gather_x[0] = item[:, 0:256]
    gather_q[0] = item[:, 256:512]

    pl.semaphore_wait(barrier, len(partners))
    pl.semaphore_signal(ready, inc=1, device_id=mirror, device_id_type=pl.DeviceIdType.MESH)

    z_x = [push(gather_x.at[0], gather_x.at[d], (z_rep(d), tp)) for d in range(1, nz)]
    z_q = [push(gather_q.at[0], gather_q.at[d], (z_rep(d), tp)) for d in range(1, nz)]
    q_swap = push(q_ref, q_other, (rep, tp_other))
    nk_swap = push(nk_ref, nk_other, (rep, tp_other))

    need("conv_ref", "cw_ref", "cb_ref")
    window = [conv_ref[w].astype(F32) for w in range(3)] + [x_ref[s].astype(F32) for s in range(4)]
    conv_last = window[2].astype(BF16)
    cw = cw_ref[...]
    cb = cb_ref[...]
    activ = []
    for s in range(4):
        total = window[s] * cw[0:1]
        for w in range(1, 4):
            total = total + window[s + w] * cw[w : w + 1]
        activ.append(silu(total + cb))
        act[s] = activ[s]
    activ_b = jnp.concatenate([v.astype(BF16) for v in activ], axis=0)
    need("xw")

    def project(rows):
        tail = jnp.concatenate([xw[512:544, :], jnp.zeros((96, 1024), BF16)], axis=0)
        return nt(rows, xw[0:512, :]), nt(rows, tail)

    main, tail = project(activ_b)
    for o in range(no):
        part[o, :, 0:512] = main[o * rpo : (o + 1) * rpo]
        part[o, :, 512:640] = tail[o * rpo : (o + 1) * rpo]
    part_out = [
        push(part.at[(own + d) % no], part_land.at[d], (rep, o_tp(d))) for d in range(1, no)
    ]

    same = iota((n, n), 0)
    lane_nn = iota((n, n), 1)
    rank16 = nn(foreign16, hot(((same >> 4) == (lane_nn >> 4)) & (same < lane_nn)))
    rank_there = nn(rank16.astype(BF16), hot(same == src))
    home = jnp.where(foreign, (lane_n >> 4) * 2 + rank16[0:1].astype(I32), -1)
    donor = jnp.where(foreign, (src >> 4) * 2 + rank_there[0:1].astype(I32), -1)
    to_row = iota((ny * 16, n), 0)
    to_code = (zi * ny + ((yi + (to_row >> 4)) & (ny - 1))) * 2 + ((to_row >> 1) & 1)
    from_row = iota((nz * 16, n), 0)
    from_code = (((zi - (from_row >> 4)) & (nz - 1)) * ny + yi) * 2 + ((from_row >> 1) & 1)
    r_ = iota((ny * 16, nz * 16), 0)
    c_ = iota((ny * 16, nz * 16), 1)
    alike = ((r_ >> 2) & 3 == (c_ >> 2) & 3) & ((r_ & 1) == (c_ & 1))
    select_in = hot(alike & (nt(hot(donor == to_code), hot(home == from_code)) > 0.5))
    select_out = hot(alike & (nt(hot(home == to_code), hot(donor == from_code)) > 0.5))

    def select(copies, chooser, gathered, staged, landing):
        for copy in copies:
            copy.wait_recv()
        width = gathered.shape[2]
        chosen = nn(chooser, gathered[...].reshape(nz * 16, width)).astype(BF16)
        for e in range(ny):
            staged[e] = chosen[e * 16 : (e + 1) * 16]
        landing[0] = chosen[0:16]
        return [push(staged.at[e], landing.at[e], (y_rep(e), tp)) for e in range(1, ny)]

    y_x = select(z_x, select_in, gather_x, stage_x, land_x)

    for copy in part_out:
        copy.wait_recv()
    summed = part[own]
    for d in range(1, no):
        summed = summed + part_land[d]
    blank = jnp.zeros((rpo, 128), F32)

    def pack_half(v):
        return jnp.concatenate(
            [
                jnp.concatenate([v[:, 0:256], v[:, 512:640]], axis=1),
                jnp.concatenate([v[:, 256:512], blank], axis=1),
            ],
            axis=0,
        ).astype(BF16)

    def unpack_half(v):
        v = v.astype(F32)
        return jnp.concatenate([v[:rpo, 0:256], v[rpo:, 0:256], v[:rpo, 256:384]], axis=1)

    half_send[...] = pack_half(summed)
    pl.semaphore_wait(ready, 1)
    half = push(half_send, half_land, (rep, tp_half))

    y_q = select(z_q, select_in, gather_q, stage_q, land_q)
    y_q += [push(stage_q.at[e], land_o.at[e], (y_rep(e), tp_other)) for e in range(ny)]

    need("page_ref", "len_ref")
    own_lane = iota((16, n), 1) == rep * 16 + iota((16, n), 0)
    lengths = jnp.sum(jnp.where(own_lane, len_ref[...], 0), axis=1, keepdims=True)
    foreign_col = (
        jnp.sum(jnp.where(own_lane & foreign, 1.0, 0.0), axis=1, keepdims=True) > 0.5
    )
    table = page_ref[...]
    eye = iota((16, 16), 0) == iota((16, 16), 1)
    cache_lane = iota((16, 1024), 1)
    allowed = jnp.zeros((16, 1024), F32)
    for k in range(4):
        page = jnp.where(core == 0, table[2 * k : 2 * k + 1], table[2 * k + 1 : 2 * k + 2])
        page = jnp.sum(jnp.where(eye, page, 0), axis=1, keepdims=True)
        limit = lengths - (2 * k + core) * 16
        allowed = jnp.where(
            ((cache_lane >> 4) == page) & ((cache_lane & 15) < limit), 1.0, allowed
        )
    mask_ref[...] = allowed.astype(BF16)
    bias_ref[...] = jnp.where(allowed > 0.5, 0.0, MASKED)

    for copy in y_x:
        copy.wait_recv()
    er = iota((128, ny * 16), 0)
    ec = iota((128, ny * 16), 1)
    wanted_step = jnp.where(er < 64, er & 1, 0)
    expand = hot(
        (((er >> 4) & 3) == ((ec >> 2) & 3))
        & (((er >> 1) & 1) == ((ec >> 1) & 1))
        & (wanted_step == (ec & 1))
    )
    arrived = nn(expand, land_x[...].reshape(ny * 16, 256))
    x_now = jnp.concatenate([arrived[b * 16 : (b + 1) * 16] for b in range(4)], axis=1)
    x_prev = jnp.concatenate(
        [arrived[64 + b * 16 : 64 + (b + 1) * 16] for b in range(4)], axis=1
    )
    last_row = nn(pick16, conv_last)
    x_zero = nn(pick16, x_ref[0])
    x_one = nn(pick16, x_ref[1])
    odd = (iota((16, 1024), 0) & 1) == 1
    total = jnp.where(odd, x_zero, last_row) * cw[0:1]
    total = total + jnp.where(odd, x_one, x_zero) * cw[1:2]
    total = total + jnp.where(odd, x_prev, x_one) * cw[2:3]
    total = total + x_now * cw[3:4]
    late_act = silu(total + cb)
    main, tail = project(late_act.astype(BF16))
    late_own = jnp.concatenate(
        [by_quarter([main[:, b * 128 : (b + 1) * 128] for b in range(4)]), tail], axis=1
    )
    late_send[...] = late_own.astype(BF16)
    late_out = [push(late_send, late_land.at[d], (rep, o_tp(d))) for d in range(1, no)]

    need("pool")
    q_swap.wait_recv()
    nk_swap.wait_recv()
    pages = pool[...].reshape(1024, 256)
    keys, values = pages[:, 0:128], pages[:, 128:256]
    pad64 = jnp.zeros((64, 128), BF16)
    new_keys = [nk_ref[s] for s in range(4)]
    new_values = [nk_other[s] for s in range(4)]
    extra_keys = jnp.concatenate(new_keys + [pad64], axis=0)
    extra_values = jnp.concatenate(new_values + [pad64], axis=0)
    row_q = iota((256, 128), 0)
    col_q = iota((256, 128), 1)
    extra_bias = jnp.where(
        ((row_q & 15) == (col_q & 15)) & ((col_q >> 4) <= (row_q >> 6)) & (core == 0), 0.0, MASKED
    )
    bias16 = bias_ref[...]
    bias = jnp.concatenate([bias16] * 16, axis=0)
    for source, target in ((q_other, away), (q_ref, near)):
        rows = jnp.concatenate(
            [source[s][:, h * 128 : (h + 1) * 128] for s in range(4) for h in range(4)], axis=0
        )
        out, stats = attend(rows, keys, values, extra_keys, extra_values, bias, extra_bias)
        target[:, 0:128] = out
        target[:, 128:256] = stats
        if target is away:
            partial = push(away, far, (rep, tp_other))

    need("dtg_ref")
    half.wait_recv()
    summed = summed + unpack_half(half_land[...])
    main = summed[:, 0:512]
    mean = jnp.sum(main * main, axis=1, keepdims=True) / 512.0
    low = main * lax.rsqrt(mean + EPS) * dtg_ref[...]
    normed = jnp.concatenate([low, tail_norm(summed[:, 512:640])], axis=1)
    packed = pack_half(normed)
    norm_send[...] = packed
    norm_out = [push(norm_send, norm_land.at[d], (rep, o_tp(d))) for d in range(1, no)]

    def take(o, v):
        v = unpack_half(v)
        start = pl.multiple_of(o * rpo, rpo)
        dtl[pl.ds(start, rpo), :] = v[:, 0:512]
        tails[pl.ds(start, rpo), :] = v[:, 512:640]

    take(own, packed)

    for copy in late_out:
        copy.wait_recv()
    late_sum = late_own
    for d in range(1, no):
        late_sum = late_sum + late_land[d].astype(F32)
    late_half[...] = late_sum.astype(BF16)
    late_swap = push(late_half, late_half_land, (rep, tp_half))

    for copy in y_q:
        copy.wait_recv()
    arrived_q = nn(expand[0:64], land_q[...].reshape(ny * 16, 256))
    arrived_o = nn(expand[0:64], land_o[...].reshape(ny * 16, 256))
    q_late = jnp.concatenate(
        [
            v[(h // 2) * 16 : (h // 2) * 16 + 8, (h % 2) * 128 : (h % 2) * 128 + 128]
            for v in (arrived_q, arrived_o)
            for h in range(4)
        ],
        axis=0,
    ).astype(BF16)
    pad48 = jnp.zeros((48, 128), BF16)
    late_keys = jnp.concatenate(
        new_keys + [arrived_q[32:48, 0:128].astype(BF16), pad48], axis=0
    )
    late_values = jnp.concatenate(
        new_values + [arrived_o[32:48, 0:128].astype(BF16), pad48], axis=0
    )
    fits = (place & (col < 32)) | (
        (col >= 64)
        & (col < 68)
        & (((col >> 1) & 1) == ((row >> 1) & 1))
        & ((col & 1) <= (row & 1))
    )
    late_extra = jnp.where(fits & (core == 0), 0.0, MASKED)[0:8]
    late_bias = jnp.where(nn(pick16, mask_ref[...]) > 0.5, 0.0, MASKED)[0:8]
    out, stats = attend(
        q_late,
        keys,
        values,
        late_keys,
        late_values,
        jnp.concatenate([late_bias] * 8, axis=0),
        jnp.concatenate([late_extra] * 8, axis=0),
    )
    late_near = jnp.concatenate([out[0:32], stats[0:32]], axis=1)
    late_away[...] = jnp.concatenate([out[32:64], stats[32:64]], axis=1)
    late_partial = push(late_away, late_far, (rep, tp_other))

    for d, copy in enumerate(norm_out, 1):
        copy.wait_recv()
        take((own - d + no) % no, norm_land[d])
    need("dw", "dtb_ref", "bg_ref", "cg_ref", "skip_ref", "a_ref", "ssm")
    steps = softplus(nn(dtl[...].astype(BF16), dw[...]) + dtb_ref[...])
    for s in range(4):
        dts[s] = steps[s * 16 : (s + 1) * 16]
    b_gain = jnp.sum(jnp.where(eye, bg_ref[...], 0.0), axis=1, keepdims=True)
    c_gain = jnp.sum(jnp.where(eye, cg_ref[...], 0.0), axis=1, keepdims=True)
    skip = skip_ref[...]

    def columns(tail_row):
        b = jnp.sum(jnp.where(col == row, tail_row, 0.0), axis=1, keepdims=True) * b_gain
        c = jnp.sum(jnp.where(col == row + 16, tail_row, 0.0), axis=1, keepdims=True) * c_gain
        return b, c

    def advance(state, dt_row, act_row, tail_row):
        b, c = columns(tail_row)
        state = jnp.exp(-dt_row * a_ref[...]) * state + (dt_row * act_row) * b
        return state, jnp.sum(state * c, axis=0, keepdims=True) + skip * act_row

    def scan(first, held, keep):
        def body(i, carry):
            state = held[i]
            for s in (first, first + 1):
                state, out = advance(
                    state,
                    dts[s, pl.ds(i, 1), :],
                    act[s, pl.ds(i, 1), :],
                    tails[pl.ds(s * 16 + i, 1), :],
                )
                mixed[s, pl.ds(i, 1), :] = out
            if keep:
                mid[i] = state
            return carry

        lax.fori_loop(0, 16, body, 0)

    scan(0, ssm, True)

    late_partial.wait_recv()
    heads = combine(late_near, late_far[...]).astype(BF16)
    hr = iota((16, 32), 0)
    hc = iota((16, 32), 1)
    heads = nn(hot(((hr >> 2) == (hc >> 3)) & ((hr & 3) == (hc & 7))), heads)
    gather_a[0] = heads.astype(BF16)
    z_a = [push(gather_a.at[0], gather_a.at[d], (z_rep(d), tp)) for d in range(1, nz)]

    late_swap.wait_recv()
    late_sum = late_sum + late_half_land[...].astype(F32)
    main = late_sum[:, 0:128]
    square = jnp.broadcast_to(jnp.sum(main * main, axis=1, keepdims=True), (16, 128))
    square = square + pltpu.roll(square, 8, 0)
    square = square + pltpu.roll(square, 4, 0)
    gain = dtg_ref[...]
    gains = by_quarter(
        [jnp.broadcast_to(gain[:, b * 128 : (b + 1) * 128], (16, 128)) for b in range(4)]
    )
    low = (main * lax.rsqrt(square / 512.0 + EPS) * gains).astype(BF16)
    wr = iota((64, 16), 0)
    wc = iota((64, 16), 1)
    spread = nn(hot(((wr >> 4) == (wc >> 2)) & ((wr & 3) == (wc & 3))), low)
    low = jnp.concatenate([spread[b * 16 : (b + 1) * 16] for b in range(4)], axis=1)
    late_dt = softplus(nn(low.astype(BF16), dw[...]) + dtb_ref[...])
    late_tail = tail_norm(late_sum[:, 128:256])

    need("src_s")
    base = rep * 16
    first = jnp.int32(-1)
    second = jnp.int32(0)
    for i in range(16):
        moves = src_s[base + i] != base + i
        second = jnp.where(moves & (first >= 0), i, second)
        first = jnp.where(moves & (first < 0), i, first)
    first = jnp.maximum(first, 0)
    rows = iota((16, 1024), 0) & 3
    late_mixed = jnp.zeros((16, 1024), F32)
    for r, slot in enumerate((first, second)):
        state = mid[slot]
        for s in range(2):
            m = r * 2 + s
            state, out = advance(
                state, late_dt[m : m + 1], late_act[m : m + 1], late_tail[m : m + 1]
            )
            late_mixed = jnp.where(rows == m, out, late_mixed)
    gather_m[0] = by_quarter(
        [late_mixed[:, b * 256 : (b + 1) * 256] for b in range(4)]
    ).astype(BF16)
    z_m = [push(gather_m.at[0], gather_m.at[d], (z_rep(d), tp)) for d in range(1, nz)]

    scan(2, mid, False)
    need("z_ref")
    partial.wait_recv()
    kept = []
    for s in range(4):
        block = combine(near[s * 64 : (s + 1) * 64, :], far[s * 64 : (s + 1) * 64, :])
        block = jnp.concatenate([block[h * 16 : (h + 1) * 16] for h in range(4)], axis=1)
        if s < 2:
            attn_ref[s] = block.astype(BF16)
            mix_ref[s] = (mixed[s] * silu(z_ref[s].astype(F32))).astype(BF16)
        else:
            kept.append(block)

    y_a = select(z_a, select_out, gather_a, stage_a, land_a)
    own_code = rep * 2 + ((iota((ny * 16, n), 0) >> 1) & 1)
    fr = iota((128, ny * 16), 0)
    fc = iota((128, ny * 16), 1)
    put = hot(
        (((fr >> 4) & 3) == ((fc >> 2) & 3))
        & ((fr >> 6) == (fc & 1))
        & (nt(slot_pick, hot(home == own_code)) > 0.5)
    )
    y_m = select(z_m, select_out, gather_m, stage_m, land_m)
    for copy in y_a + y_m:
        copy.wait_recv()
    returned = nn(put, land_m[...].reshape(ny * 16, 256))
    attended = nn(put, land_a[...].reshape(ny * 16, 128))
    for s in (2, 3):
        spots = [(s - 2) * 64 + b * 16 for b in range(4)]
        back = jnp.concatenate([returned[p : p + 16] for p in spots], axis=1)
        whole = jnp.where(foreign_col, back, mixed[s])
        mix_ref[s] = (whole * silu(z_ref[s].astype(F32))).astype(BF16)
        back = jnp.concatenate([attended[p : p + 16] for p in spots], axis=1)
        attn_ref[s] = jnp.where(foreign_col, back, kept[s - 2]).astype(BF16)

    for copy in used:
        copy.wait_send()


def shards(
    geo,
    queries,
    new_kv,
    kv_pool,
    page_table,
    kv_lengths,
    slot_source,
    mamba_x,
    mamba_z,
    conv_state,
    ssm_state,
    x_proj_weight,
    dt_proj_weight,
    dt_bias,
    a_rate,
    skip_gain,
    conv_weight,
    conv_bias,
    dt_gain,
    b_gain,
    c_gain,
):
    nz, ny, nx = geo
    no = 2 * nx
    rpo = 64 // no
    copies = 4 * (nz - 1) + 4 * (ny - 1) + ny + 3 * (no - 1) + 6
    operands = (
        slot_source.reshape(1, -1),
        queries,
        new_kv,
        mamba_x,
        slot_source,
        conv_state.transpose(1, 0, 2),
        conv_weight,
        conv_bias.reshape(1, -1),
        x_proj_weight,
        page_table.T,
        kv_lengths.reshape(1, -1),
        kv_pool,
        dt_gain.reshape(1, -1),
        dt_proj_weight,
        dt_bias.reshape(1, -1),
        b_gain.reshape(1, -1),
        c_gain.reshape(1, -1),
        skip_gain.reshape(1, -1),
        a_rate,
        ssm_state,
        mamba_z,
    )
    vmem = pl.BlockSpec(memory_space=pltpu.VMEM)
    scratch = [
        pltpu.SMEM(v.shape, v.dtype) if k == 4 else pltpu.VMEM(v.shape, v.dtype)
        for k, v in enumerate(operands)
    ] + [
        pltpu.VMEM((16, 16, 1024), F32),
        pltpu.VMEM((4, 16, 1024), F32),
        pltpu.VMEM((4, 16, 1024), F32),
        pltpu.VMEM((4, 16, 1024), F32),
        pltpu.VMEM((64, 512), F32),
        pltpu.VMEM((64, 128), F32),
        pltpu.VMEM((nz, 16, 256), BF16),
        pltpu.VMEM((ny, 16, 256), BF16),
        pltpu.VMEM((ny, 16, 256), BF16),
        pltpu.VMEM((nz, 16, 256), BF16),
        pltpu.VMEM((ny, 16, 256), BF16),
        pltpu.VMEM((ny, 16, 256), BF16),
        pltpu.VMEM((ny, 16, 256), BF16),
        pltpu.VMEM((4, 16, 512), BF16),
        pltpu.VMEM((4, 16, 128), BF16),
        pltpu.VMEM((no, rpo, 640), F32),
        pltpu.VMEM((no, rpo, 640), F32),
        pltpu.VMEM((2 * rpo, 384), BF16),
        pltpu.VMEM((2 * rpo, 384), BF16),
        pltpu.VMEM((2 * rpo, 384), BF16),
        pltpu.VMEM((no, 2 * rpo, 384), BF16),
        pltpu.VMEM((256, 256), F32),
        pltpu.VMEM((256, 256), F32),
        pltpu.VMEM((256, 256), F32),
        pltpu.VMEM((16, 256), BF16),
        pltpu.VMEM((no, 16, 256), BF16),
        pltpu.VMEM((16, 256), BF16),
        pltpu.VMEM((16, 256), BF16),
        pltpu.VMEM((32, 256), F32),
        pltpu.VMEM((32, 256), F32),
        pltpu.VMEM((nz, 16, 256), BF16),
        pltpu.VMEM((ny, 16, 256), BF16),
        pltpu.VMEM((ny, 16, 256), BF16),
        pltpu.VMEM((nz, 16, 128), BF16),
        pltpu.VMEM((ny, 16, 128), BF16),
        pltpu.VMEM((ny, 16, 128), BF16),
        pltpu.VMEM((16, 1024), F32),
        pltpu.VMEM((16, 1024), BF16),
        pltpu.SemaphoreType.DMA((copies,)),
        pltpu.SemaphoreType.DMA((copies,)),
        pltpu.SemaphoreType.DMA((len(operands),)),
        pltpu.SemaphoreType.REGULAR,
    ]
    return pl.pallas_call(
        functools.partial(kernel, geo),
        out_shape=(
            pltpu.VMEM(queries.shape, BF16),
            pltpu.VMEM(mamba_x.shape, BF16),
        ),
        in_specs=[pl.BlockSpec(memory_space=pl.ANY)] * len(operands),
        out_specs=(vmem, vmem),
        scratch_shapes=scratch,
        compiler_params=pltpu.CompilerParams(
            collective_id=0, has_side_effects=True, vmem_limit_bytes=60 * 1024 * 1024
        ),
    )(*operands)


def solution(mesh):
    placed = (
        P(None, "rep", "tp"),
        P(None, "rep", "tp"),
        P("rep", "tp", None, None),
        P("rep", None),
        P(),
        P(),
        P(None, "rep", "tp"),
        P(None, "rep", "tp"),
        P("rep", None, "tp"),
        P("rep", None, "tp"),
        P(None, "tp"),
        P(None, "tp"),
        P("tp"),
        P(None, "tp"),
        P("tp"),
        P(None, "tp"),
        P("tp"),
        P(),
        P(),
        P(),
    )
    return jax.shard_map(
        functools.partial(shards, geometry(mesh)),
        mesh=mesh,
        in_specs=placed,
        out_specs=(P(None, "rep", "tp"), P(None, "rep", "tp")),
        check_vma=False,
    )
```

```python
import functools

import jax
import jax.numpy as jnp
from jax import lax
from jax.experimental import pallas as pl
from jax.experimental.pallas import tpu as pltpu
from jax.sharding import PartitionSpec as P

F32 = jnp.float32
BF16 = jnp.bfloat16
I32 = jnp.int32
EPS = 1e-06
MASKED = -1e30
SCALE = 128**-0.5


def geometry(mesh):
    rep, tp = mesh.shape["rep"], mesh.shape["tp"]
    ny = 4 if rep >= 16 else 2
    return (rep // ny, ny, tp // 4)


def nn(a, b):
    return lax.dot_general(a, b, (((1,), (0,)), ((), ())), preferred_element_type=F32)


def nt(a, b):
    return lax.dot_general(a, b, (((1,), (1,)), ((), ())), preferred_element_type=F32)


def hot(cond):
    return jnp.where(cond, 1.0, 0.0).astype(BF16)


def iota(shape, dim):
    return lax.broadcasted_iota(I32, shape, dim)


def silu(v):
    return v / (1.0 + jnp.exp(-v))


def softplus(v):
    return jnp.maximum(v, 0.0) + jnp.log1p(jnp.exp(-jnp.abs(v)))


def attend(q_rows, keys, values, extra_keys, extra_values, bias, extra_bias):
    scores = nt(q_rows, keys) * SCALE + bias
    extra = nt(q_rows, extra_keys) * SCALE + extra_bias
    peak = jnp.maximum(
        jnp.max(scores, axis=1, keepdims=True), jnp.max(extra, axis=1, keepdims=True)
    )
    weight = jnp.exp(scores - peak)
    extra_weight = jnp.exp(extra - peak)
    total = jnp.sum(weight, axis=1, keepdims=True) + jnp.sum(extra_weight, axis=1, keepdims=True)
    out = nn(weight.astype(BF16), values) + nn(extra_weight.astype(BF16), extra_values)
    lane = iota((q_rows.shape[0], 128), 1)
    return out, jnp.where(lane < 64, peak, total)


def combine(near, far):
    near_peak, near_sum = near[:, 128:129], near[:, 192:193]
    far_peak, far_sum = far[:, 128:129], far[:, 192:193]
    peak = jnp.maximum(near_peak, far_peak)
    near_scale = jnp.exp(near_peak - peak)
    far_scale = jnp.exp(far_peak - peak)
    numer = near[:, :128] * near_scale + far[:, :128] * far_scale
    return numer / (near_sum * near_scale + far_sum * far_scale)


def tail_norm(tail):
    lane = iota(tail.shape, 1)
    square = tail * tail
    mean_b = jnp.sum(jnp.where(lane < 16, square, 0.0), axis=1, keepdims=True) / 16.0
    mean_c = jnp.sum(
        jnp.where((lane >= 16) & (lane < 32), square, 0.0), axis=1, keepdims=True
    ) / 16.0
    scale = jnp.where(lane < 16, lax.rsqrt(mean_b + EPS), lax.rsqrt(mean_c + EPS))
    return jnp.where(lane < 32, tail * scale, 0.0)


def by_quarter(blocks):
    quarter = iota(blocks[0].shape, 0) >> 2
    return jnp.where(
        quarter == 0,
        blocks[0],
        jnp.where(quarter == 1, blocks[1], jnp.where(quarter == 2, blocks[2], blocks[3])),
    )


def kernel(
    geo,
    src_ref_h,
    q_ref_h,
    nk_ref_h,
    x_ref_h,
    src_s_h,
    conv_ref_h,
    cw_ref_h,
    cb_ref_h,
    xw_h,
    page_ref_h,
    len_ref_h,
    pool_h,
    dtg_ref_h,
    dw_h,
    dtb_ref_h,
    bg_ref_h,
    cg_ref_h,
    skip_ref_h,
    a_ref_h,
    ssm_h,
    z_ref_h,
    attn_ref,
    mix_ref,
    src_ref,
    q_ref,
    nk_ref,
    x_ref,
    src_s,
    conv_ref,
    cw_ref,
    cb_ref,
    xw,
    page_ref,
    len_ref,
    pool,
    dtg_ref,
    dw,
    dtb_ref,
    bg_ref,
    cg_ref,
    skip_ref,
    a_ref,
    ssm,
    z_ref,
    mid,
    act,
    dts,
    mixed,
    dtl,
    tails,
    item_x,
    gather_x,
    stage_x,
    land_x,
    gather_q,
    stage_q,
    land_q,
    land_o,
    q_other,
    nk_other,
    part,
    part_land,
    half_send,
    half_land,
    norm_send,
    norm_land,
    near,
    away,
    far,
    late_send,
    late_land,
    late_half,
    late_half_land,
    late_acc,
    late_total,
    late_away,
    late_far,
    item_m,
    gather_m,
    stage_m,
    land_m,
    gather_a,
    stage_a,
    land_a,
    bias_ref,
    mask_ref,
    ssem,
    rsem,
    lsem,
    ready,
    zs,
    zr,
    ys,
    yr,
    ls,
    lr,
    hs,
    hr,
):
    nz, ny, nx = geo
    no = 2 * nx
    rpo = 64 // no
    n = src_ref.shape[1]
    rep, tp = lax.axis_index("rep"), lax.axis_index("tp")
    zi, yi = rep // ny, rep % ny
    core, zh, xi = tp % 2, (tp // 2) % 2, tp // 4
    own = xi * 2 + core
    tp_other = tp + 1 - 2 * core
    tp_half = tp + 2 - 4 * zh
    tp_odd = tp + 1 - core

    def o_tp(d):
        o = (own + d) % no
        return (o // 2) * 4 + zh * 2 + o % 2

    def z_rep(d):
        return ((zi + d) % nz) * ny + yi

    def y_rep(e):
        return zi * ny + (yi + e) % ny

    partners = [(z_rep(d), tp) for d in range(1, nz)]
    partners += [(z_rep(d), tp_other) for d in range(1, nz)]
    partners += [(y_rep(e), tp) for e in range(1, ny)]
    partners += [(y_rep(e), tp_other) for e in range(1, ny)]
    partners += [(rep, o_tp(d)) for d in range(1, no)]
    mirror = ((nz - 1 - zi) * ny + yi, tp_half)
    partners += [mirror]
    barrier = pltpu.get_barrier_semaphore()
    for device in partners:
        pl.semaphore_signal(
            barrier, inc=1, device_id=device, device_id_type=pl.DeviceIdType.MESH
        )

    loads = {}
    for k, (name, a, b) in enumerate(
        (
            ("src_ref", src_ref_h, src_ref),
            ("q_ref", q_ref_h, q_ref),
            ("nk_ref", nk_ref_h, nk_ref),
            ("x_ref", x_ref_h, x_ref),
            ("src_s", src_s_h, src_s),
            ("conv_ref", conv_ref_h, conv_ref),
            ("cw_ref", cw_ref_h, cw_ref),
            ("cb_ref", cb_ref_h, cb_ref),
            ("xw", xw_h, xw),
            ("page_ref", page_ref_h, page_ref),
            ("len_ref", len_ref_h, len_ref),
            ("pool", pool_h, pool),
            ("dtg_ref", dtg_ref_h, dtg_ref),
            ("dw", dw_h, dw),
            ("dtb_ref", dtb_ref_h, dtb_ref),
            ("bg_ref", bg_ref_h, bg_ref),
            ("cg_ref", cg_ref_h, cg_ref),
            ("skip_ref", skip_ref_h, skip_ref),
            ("a_ref", a_ref_h, a_ref),
            ("ssm", ssm_h, ssm),
            ("z_ref", z_ref_h, z_ref),
        )
    ):
        loads[name] = pltpu.make_async_copy(a, b, lsem.at[k])
        loads[name].start()

    def need(*names):
        for name in names:
            loads[name].wait()

    used = []

    def push(src, dst, device):
        k = len(used)
        copy = pltpu.make_async_remote_copy(
            src_ref=src,
            dst_ref=dst,
            send_sem=ssem.at[k],
            recv_sem=rsem.at[k],
            device_id=device,
            device_id_type=pl.DeviceIdType.MESH,
        )
        copy.start()
        used.append(copy)
        return copy

    def link(src, dst, send_sem, recv_sem, device):
        return pltpu.make_async_remote_copy(
            src_ref=src,
            dst_ref=dst,
            send_sem=send_sem,
            recv_sem=recv_sem,
            device_id=device,
            device_id_type=pl.DeviceIdType.MESH,
        )

    even, odd_core = pl.when(core == 0), pl.when(core == 1)

    def z_copy(k, item, gather, c, d):
        return link(item, gather.at[c, d], zs.at[k, d], zr.at[k, c, d], (z_rep(d), tp_odd))

    def y_copy(k, stage, land, c, e):
        return link(
            stage.at[c, e], land.at[e], ys.at[k, c, e], yr.at[k, e], (y_rep(e), tp_odd - 1 + c)
        )

    def late_copy(c, d):
        device = (rep, ((xi + d) % nx) * 4 + zh * 2 + 1)
        return link(late_send, late_land.at[c, d], ls.at[d], lr.at[c, d], device)

    def set_out(k, item, gather):
        for d in range(1, nz):
            z_copy(k, item, gather, core, d).start()

        @even
        def _():
            z_copy(k, item, gather, 0, 0).start()

        @odd_core
        def _():
            gather[1, 0] = item[...]

    def turn(k, item, gather, stage, land, chooser):
        @odd_core
        def _():
            for c in range(2):
                for d in range(nz):
                    if (c, d) != (1, 0):
                        z_copy(k, item, gather, c, d).wait_recv()
                chosen = nn(chooser, gather[c].reshape(nz * 16, 256)).astype(BF16)
                for e in range(ny):
                    stage[c, e] = chosen[e * 16 : (e + 1) * 16]
                    if (c, e) != (1, 0):
                        y_copy(k, stage, land, c, e).start()
                    else:
                        land[0] = chosen[0:16]

    def arrive(k, stage, land):
        for e in range(1, ny):
            y_copy(k, stage, land, 0, e).wait_recv()

        @even
        def _():
            y_copy(k, stage, land, 0, 0).wait_recv()

    def drain(k, item, gather, stage, land):
        for d in range(1, nz):
            z_copy(k, item, gather, core, d).wait_send()

        @even
        def _():
            z_copy(k, item, gather, 0, 0).wait_send()

        @odd_core
        def _():
            for c in range(2):
                for e in range(ny):
                    if (c, e) != (1, 0):
                        y_copy(k, stage, land, c, e).wait_send()

    need("src_ref")
    src = src_ref[...]
    lane_n = iota((1, n), 1)
    foreign = src != lane_n
    foreign16 = jnp.broadcast_to(hot(foreign), (16, n))
    slot_pick = hot(iota((128, n), 1) == rep * 16 + (iota((128, n), 0) & 15))
    f128 = nt(foreign16, slot_pick)
    before = hot(
        (iota((128, 128), 0) < 16) & (iota((128, 128), 0) < (iota((128, 128), 1) & 15))
    )
    k128 = nn(f128.astype(BF16), before)
    row = iota((16, 128), 0)
    col = iota((16, 128), 1)
    rank = ((row >> 1) & 1).astype(F32)
    place = (f128 > 0.5) & (k128 == rank)
    pack = hot(place & ((row >> 2) == ((col >> 4) & 3)) & ((row & 1) == (col >> 6)))
    pick16 = hot(place & (col < 16))[:, :16]

    need("q_ref", "nk_ref", "x_ref")
    blocks = []
    nothing = jnp.zeros((16, 256), BF16)
    for s in (2, 3):
        x_s = x_ref[s]
        q_s = q_ref[s]
        nk_s = nk_ref[s]
        for b in range(4):
            side = (
                q_s[:, b * 256 : (b + 1) * 256]
                if b < 2
                else (jnp.concatenate([nk_s, nothing[:, :128]], axis=1) if b == 2 else nothing)
            )
            blocks.append(jnp.concatenate([x_s[:, b * 256 : (b + 1) * 256], side], axis=1))
    item = nn(pack, jnp.concatenate(blocks, axis=0)).astype(BF16)
    item_x[...] = item[:, 0:256]
    gather_q[0] = item[:, 256:512]

    pl.semaphore_wait(barrier, len(partners))
    pl.semaphore_signal(ready, inc=1, device_id=mirror, device_id_type=pl.DeviceIdType.MESH)

    set_out(0, item_x, gather_x)
    z_q = [push(gather_q.at[0], gather_q.at[d], (z_rep(d), tp)) for d in range(1, nz)]
    q_swap = push(q_ref, q_other, (rep, tp_other))
    nk_swap = push(nk_ref, nk_other, (rep, tp_other))

    need("conv_ref", "cw_ref", "cb_ref")
    window = [conv_ref[w].astype(F32) for w in range(3)] + [x_ref[s].astype(F32) for s in range(4)]
    conv_last = window[2].astype(BF16)
    cw = cw_ref[...]
    cb = cb_ref[...]
    activ = []
    for s in range(4):
        total = window[s] * cw[0:1]
        for w in range(1, 4):
            total = total + window[s + w] * cw[w : w + 1]
        activ.append(silu(total + cb))
        act[s] = activ[s]
    activ_b = jnp.concatenate([v.astype(BF16) for v in activ], axis=0)
    need("xw")

    def project(rows):
        tail = jnp.concatenate([xw[512:544, :], jnp.zeros((96, 1024), BF16)], axis=0)
        return nt(rows, xw[0:512, :]), nt(rows, tail)

    main, tail = project(activ_b)
    for o in range(no):
        part[o, :, 0:512] = main[o * rpo : (o + 1) * rpo]
        part[o, :, 512:640] = tail[o * rpo : (o + 1) * rpo]
    part_out = [
        push(part.at[(own + d) % no], part_land.at[d], (rep, o_tp(d))) for d in range(1, no)
    ]

    same = iota((n, n), 0)
    lane_nn = iota((n, n), 1)
    rank16 = nn(foreign16, hot(((same >> 4) == (lane_nn >> 4)) & (same < lane_nn)))
    rank_there = nn(rank16.astype(BF16), hot(same == src))
    home = jnp.where(foreign, (lane_n >> 4) * 2 + rank16[0:1].astype(I32), -1)
    donor = jnp.where(foreign, (src >> 4) * 2 + rank_there[0:1].astype(I32), -1)
    to_row = iota((ny * 16, n), 0)
    to_code = (zi * ny + ((yi + (to_row >> 4)) & (ny - 1))) * 2 + ((to_row >> 1) & 1)
    from_row = iota((nz * 16, n), 0)
    from_code = (((zi - (from_row >> 4)) & (nz - 1)) * ny + yi) * 2 + ((from_row >> 1) & 1)
    r_ = iota((ny * 16, nz * 16), 0)
    c_ = iota((ny * 16, nz * 16), 1)
    alike = ((r_ >> 2) & 3 == (c_ >> 2) & 3) & ((r_ & 1) == (c_ & 1))
    select_in = hot(alike & (nt(hot(donor == to_code), hot(home == from_code)) > 0.5))
    select_out = hot(alike & (nt(hot(home == to_code), hot(donor == from_code)) > 0.5))

    def select(copies, chooser, gathered, staged, landing):
        for copy in copies:
            copy.wait_recv()
        width = gathered.shape[2]
        chosen = nn(chooser, gathered[...].reshape(nz * 16, width)).astype(BF16)
        for e in range(ny):
            staged[e] = chosen[e * 16 : (e + 1) * 16]
        landing[0] = chosen[0:16]
        return [push(staged.at[e], landing.at[e], (y_rep(e), tp)) for e in range(1, ny)]

    turn(0, item_x, gather_x, stage_x, land_x, select_in)

    for copy in part_out:
        copy.wait_recv()
    summed = part[own]
    for d in range(1, no):
        summed = summed + part_land[d]
    blank = jnp.zeros((rpo, 128), F32)

    def pack_half(v):
        return jnp.concatenate(
            [
                jnp.concatenate([v[:, 0:256], v[:, 512:640]], axis=1),
                jnp.concatenate([v[:, 256:512], blank], axis=1),
            ],
            axis=0,
        ).astype(BF16)

    def unpack_half(v):
        v = v.astype(F32)
        return jnp.concatenate([v[:rpo, 0:256], v[rpo:, 0:256], v[:rpo, 256:384]], axis=1)

    half_send[...] = pack_half(summed)
    pl.semaphore_wait(ready, 1)
    half = push(half_send, half_land, (rep, tp_half))

    y_q = select(z_q, select_in, gather_q, stage_q, land_q)
    y_q += [push(stage_q.at[e], land_o.at[e], (y_rep(e), tp_other)) for e in range(ny)]

    need("page_ref", "len_ref")
    own_lane = iota((16, n), 1) == rep * 16 + iota((16, n), 0)
    lengths = jnp.sum(jnp.where(own_lane, len_ref[...], 0), axis=1, keepdims=True)
    foreign_col = (
        jnp.sum(jnp.where(own_lane & foreign, 1.0, 0.0), axis=1, keepdims=True) > 0.5
    )
    table = page_ref[...]
    eye = iota((16, 16), 0) == iota((16, 16), 1)
    cache_lane = iota((16, 1024), 1)
    allowed = jnp.zeros((16, 1024), F32)
    for k in range(4):
        page = jnp.where(core == 0, table[2 * k : 2 * k + 1], table[2 * k + 1 : 2 * k + 2])
        page = jnp.sum(jnp.where(eye, page, 0), axis=1, keepdims=True)
        limit = lengths - (2 * k + core) * 16
        allowed = jnp.where(
            ((cache_lane >> 4) == page) & ((cache_lane & 15) < limit), 1.0, allowed
        )
    mask_ref[...] = allowed.astype(BF16)
    bias_ref[...] = jnp.where(allowed > 0.5, 0.0, MASKED)

    arrive(0, stage_x, land_x)
    er = iota((128, ny * 16), 0)
    ec = iota((128, ny * 16), 1)
    wanted_step = jnp.where(er < 64, er & 1, 0)
    expand = hot(
        (((er >> 4) & 3) == ((ec >> 2) & 3))
        & (((er >> 1) & 1) == ((ec >> 1) & 1))
        & (wanted_step == (ec & 1))
    )
    arrived = nn(expand, land_x[...].reshape(ny * 16, 256))
    x_now = jnp.concatenate([arrived[b * 16 : (b + 1) * 16] for b in range(4)], axis=1)
    x_prev = jnp.concatenate(
        [arrived[64 + b * 16 : 64 + (b + 1) * 16] for b in range(4)], axis=1
    )
    last_row = nn(pick16, conv_last)
    x_zero = nn(pick16, x_ref[0])
    x_one = nn(pick16, x_ref[1])
    odd = (iota((16, 1024), 0) & 1) == 1
    total = jnp.where(odd, x_zero, last_row) * cw[0:1]
    total = total + jnp.where(odd, x_one, x_zero) * cw[1:2]
    total = total + jnp.where(odd, x_prev, x_one) * cw[2:3]
    total = total + x_now * cw[3:4]
    late_act = silu(total + cb)
    main, tail = project(late_act.astype(BF16))
    late_own = jnp.concatenate(
        [by_quarter([main[:, b * 128 : (b + 1) * 128] for b in range(4)]), tail], axis=1
    )
    late_send[...] = late_own.astype(BF16)
    for d in range(1, nx):
        late_copy(core, d).start()

    @even
    def _():
        late_copy(0, 0).start()


    need("pool")
    q_swap.wait_recv()
    nk_swap.wait_recv()
    pages = pool[...].reshape(1024, 256)
    keys, values = pages[:, 0:128], pages[:, 128:256]
    pad64 = jnp.zeros((64, 128), BF16)
    new_keys = [nk_ref[s] for s in range(4)]
    new_values = [nk_other[s] for s in range(4)]
    extra_keys = jnp.concatenate(new_keys + [pad64], axis=0)
    extra_values = jnp.concatenate(new_values + [pad64], axis=0)
    row_q = iota((256, 128), 0)
    col_q = iota((256, 128), 1)
    extra_bias = jnp.where(
        ((row_q & 15) == (col_q & 15)) & ((col_q >> 4) <= (row_q >> 6)) & (core == 0), 0.0, MASKED
    )
    bias16 = bias_ref[...]
    bias = jnp.concatenate([bias16] * 16, axis=0)
    for source, target in ((q_other, away), (q_ref, near)):
        rows = jnp.concatenate(
            [source[s][:, h * 128 : (h + 1) * 128] for s in range(4) for h in range(4)], axis=0
        )
        out, stats = attend(rows, keys, values, extra_keys, extra_values, bias, extra_bias)
        target[:, 0:128] = out
        target[:, 128:256] = stats
        if target is away:
            partial = push(away, far, (rep, tp_other))

    need("dtg_ref")
    half.wait_recv()
    summed = summed + unpack_half(half_land[...])
    main = summed[:, 0:512]
    mean = jnp.sum(main * main, axis=1, keepdims=True) / 512.0
    low = main * lax.rsqrt(mean + EPS) * dtg_ref[...]
    normed = jnp.concatenate([low, tail_norm(summed[:, 512:640])], axis=1)
    packed = pack_half(normed)
    norm_send[...] = packed
    norm_out = [push(norm_send, norm_land.at[d], (rep, o_tp(d))) for d in range(1, no)]

    def take(o, v):
        v = unpack_half(v)
        start = pl.multiple_of(o * rpo, rpo)
        dtl[pl.ds(start, rpo), :] = v[:, 0:512]
        tails[pl.ds(start, rpo), :] = v[:, 512:640]

    take(own, packed)

    late_swap = link(late_half, late_half_land, hs.at[0], hr.at[0], (rep, tp_half))
    late_over = link(late_total, late_total, hs.at[1], hr.at[1], (rep, tp_odd - 1))

    @odd_core
    def _():
        late_sum = late_own
        for c in range(2):
            for d in range(nx):
                if (c, d) != (1, 0):
                    late_copy(c, d).wait_recv()
                    late_sum = late_sum + late_land[c, d].astype(F32)
        late_acc[...] = late_sum
        late_half[...] = late_sum.astype(BF16)
        late_swap.start()

    for copy in y_q:
        copy.wait_recv()
    arrived_q = nn(expand[0:64], land_q[...].reshape(ny * 16, 256))
    arrived_o = nn(expand[0:64], land_o[...].reshape(ny * 16, 256))
    q_late = jnp.concatenate(
        [
            v[(h // 2) * 16 : (h // 2) * 16 + 8, (h % 2) * 128 : (h % 2) * 128 + 128]
            for v in (arrived_q, arrived_o)
            for h in range(4)
        ],
        axis=0,
    ).astype(BF16)
    pad48 = jnp.zeros((48, 128), BF16)
    late_keys = jnp.concatenate(
        new_keys + [arrived_q[32:48, 0:128].astype(BF16), pad48], axis=0
    )
    late_values = jnp.concatenate(
        new_values + [arrived_o[32:48, 0:128].astype(BF16), pad48], axis=0
    )
    fits = (place & (col < 32)) | (
        (col >= 64)
        & (col < 68)
        & (((col >> 1) & 1) == ((row >> 1) & 1))
        & ((col & 1) <= (row & 1))
    )
    late_extra = jnp.where(fits & (core == 0), 0.0, MASKED)[0:8]
    late_bias = jnp.where(nn(pick16, mask_ref[...]) > 0.5, 0.0, MASKED)[0:8]
    out, stats = attend(
        q_late,
        keys,
        values,
        late_keys,
        late_values,
        jnp.concatenate([late_bias] * 8, axis=0),
        jnp.concatenate([late_extra] * 8, axis=0),
    )
    late_near = jnp.concatenate([out[0:32], stats[0:32]], axis=1)
    late_away[...] = jnp.concatenate([out[32:64], stats[32:64]], axis=1)
    late_partial = push(late_away, late_far, (rep, tp_other))

    for d, copy in enumerate(norm_out, 1):
        copy.wait_recv()
        take((own - d + no) % no, norm_land[d])
    need("dw", "dtb_ref", "bg_ref", "cg_ref", "skip_ref", "a_ref", "ssm")
    steps = softplus(nn(dtl[...].astype(BF16), dw[...]) + dtb_ref[...])
    for s in range(4):
        dts[s] = steps[s * 16 : (s + 1) * 16]
    b_gain = jnp.sum(jnp.where(eye, bg_ref[...], 0.0), axis=1, keepdims=True)
    c_gain = jnp.sum(jnp.where(eye, cg_ref[...], 0.0), axis=1, keepdims=True)
    skip = skip_ref[...]

    def columns(tail_row):
        b = jnp.sum(jnp.where(col == row, tail_row, 0.0), axis=1, keepdims=True) * b_gain
        c = jnp.sum(jnp.where(col == row + 16, tail_row, 0.0), axis=1, keepdims=True) * c_gain
        return b, c

    def advance(state, dt_row, act_row, tail_row):
        b, c = columns(tail_row)
        state = jnp.exp(-dt_row * a_ref[...]) * state + (dt_row * act_row) * b
        return state, jnp.sum(state * c, axis=0, keepdims=True) + skip * act_row

    def scan(first, held, keep):
        def body(i, carry):
            state = held[i]
            for s in (first, first + 1):
                state, out = advance(
                    state,
                    dts[s, pl.ds(i, 1), :],
                    act[s, pl.ds(i, 1), :],
                    tails[pl.ds(s * 16 + i, 1), :],
                )
                mixed[s, pl.ds(i, 1), :] = out
            if keep:
                mid[i] = state
            return carry

        lax.fori_loop(0, 16, body, 0)

    scan(0, ssm, True)

    late_partial.wait_recv()
    heads = combine(late_near, late_far[...]).astype(BF16)
    hr = iota((16, 32), 0)
    hc = iota((16, 32), 1)
    heads = nn(hot(((hr >> 2) == (hc >> 3)) & ((hr & 3) == (hc & 7))), heads)
    gather_a[0] = heads.astype(BF16)
    z_a = [push(gather_a.at[0], gather_a.at[d], (z_rep(d), tp)) for d in range(1, nz)]

    @odd_core
    def _():
        late_swap.wait_recv()
        late_total[...] = late_acc[...] + late_half_land[...].astype(F32)
        late_over.start()

    @even
    def _():
        late_over.wait_recv()

    late_sum = late_total[...]
    main = late_sum[:, 0:128]
    square = jnp.broadcast_to(jnp.sum(main * main, axis=1, keepdims=True), (16, 128))
    square = square + pltpu.roll(square, 8, 0)
    square = square + pltpu.roll(square, 4, 0)
    gain = dtg_ref[...]
    gains = by_quarter(
        [jnp.broadcast_to(gain[:, b * 128 : (b + 1) * 128], (16, 128)) for b in range(4)]
    )
    low = (main * lax.rsqrt(square / 512.0 + EPS) * gains).astype(BF16)
    wr = iota((64, 16), 0)
    wc = iota((64, 16), 1)
    spread = nn(hot(((wr >> 4) == (wc >> 2)) & ((wr & 3) == (wc & 3))), low)
    low = jnp.concatenate([spread[b * 16 : (b + 1) * 16] for b in range(4)], axis=1)
    late_dt = softplus(nn(low.astype(BF16), dw[...]) + dtb_ref[...])
    late_tail = tail_norm(late_sum[:, 128:256])

    need("src_s")
    base = rep * 16
    first = jnp.int32(-1)
    second = jnp.int32(0)
    for i in range(16):
        moves = src_s[base + i] != base + i
        second = jnp.where(moves & (first >= 0), i, second)
        first = jnp.where(moves & (first < 0), i, first)
    first = jnp.maximum(first, 0)
    rows = iota((16, 1024), 0) & 3
    late_mixed = jnp.zeros((16, 1024), F32)
    for r, slot in enumerate((first, second)):
        state = mid[slot]
        for s in range(2):
            m = r * 2 + s
            state, out = advance(
                state, late_dt[m : m + 1], late_act[m : m + 1], late_tail[m : m + 1]
            )
            late_mixed = jnp.where(rows == m, out, late_mixed)
    item_m[...] = by_quarter(
        [late_mixed[:, b * 256 : (b + 1) * 256] for b in range(4)]
    ).astype(BF16)
    set_out(1, item_m, gather_m)

    scan(2, mid, False)
    need("z_ref")
    partial.wait_recv()
    kept = []
    for s in range(4):
        block = combine(near[s * 64 : (s + 1) * 64, :], far[s * 64 : (s + 1) * 64, :])
        block = jnp.concatenate([block[h * 16 : (h + 1) * 16] for h in range(4)], axis=1)
        if s < 2:
            attn_ref[s] = block.astype(BF16)
            mix_ref[s] = (mixed[s] * silu(z_ref[s].astype(F32))).astype(BF16)
        else:
            kept.append(block)

    y_a = select(z_a, select_out, gather_a, stage_a, land_a)
    own_code = rep * 2 + ((iota((ny * 16, n), 0) >> 1) & 1)
    fr = iota((128, ny * 16), 0)
    fc = iota((128, ny * 16), 1)
    put = hot(
        (((fr >> 4) & 3) == ((fc >> 2) & 3))
        & ((fr >> 6) == (fc & 1))
        & (nt(slot_pick, hot(home == own_code)) > 0.5)
    )
    turn(1, item_m, gather_m, stage_m, land_m, select_out)
    for copy in y_a:
        copy.wait_recv()
    arrive(1, stage_m, land_m)
    returned = nn(put, land_m[...].reshape(ny * 16, 256))
    attended = nn(put, land_a[...].reshape(ny * 16, 128))
    for s in (2, 3):
        spots = [(s - 2) * 64 + b * 16 for b in range(4)]
        back = jnp.concatenate([returned[p : p + 16] for p in spots], axis=1)
        whole = jnp.where(foreign_col, back, mixed[s])
        mix_ref[s] = (whole * silu(z_ref[s].astype(F32))).astype(BF16)
        back = jnp.concatenate([attended[p : p + 16] for p in spots], axis=1)
        attn_ref[s] = jnp.where(foreign_col, back, kept[s - 2]).astype(BF16)

    for copy in used:
        copy.wait_send()
    drain(0, item_x, gather_x, stage_x, land_x)
    drain(1, item_m, gather_m, stage_m, land_m)
    for d in range(1, nx):
        late_copy(core, d).wait_send()

    @even
    def _():
        late_copy(0, 0).wait_send()

    @odd_core
    def _():
        late_swap.wait_send()
        late_over.wait_send()


def shards(
    geo,
    queries,
    new_kv,
    kv_pool,
    page_table,
    kv_lengths,
    slot_source,
    mamba_x,
    mamba_z,
    conv_state,
    ssm_state,
    x_proj_weight,
    dt_proj_weight,
    dt_bias,
    a_rate,
    skip_gain,
    conv_weight,
    conv_bias,
    dt_gain,
    b_gain,
    c_gain,
):
    nz, ny, nx = geo
    no = 2 * nx
    rpo = 64 // no
    copies = 2 * (nz - 1) + 2 * (ny - 1) + ny + 2 * (no - 1) + 5
    operands = (
        slot_source.reshape(1, -1),
        queries,
        new_kv,
        mamba_x,
        slot_source,
        conv_state.transpose(1, 0, 2),
        conv_weight,
        conv_bias.reshape(1, -1),
        x_proj_weight,
        page_table.T,
        kv_lengths.reshape(1, -1),
        kv_pool,
        dt_gain.reshape(1, -1),
        dt_proj_weight,
        dt_bias.reshape(1, -1),
        b_gain.reshape(1, -1),
        c_gain.reshape(1, -1),
        skip_gain.reshape(1, -1),
        a_rate,
        ssm_state,
        mamba_z,
    )
    vmem = pl.BlockSpec(memory_space=pltpu.VMEM)
    scratch = [
        pltpu.SMEM(v.shape, v.dtype) if k == 4 else pltpu.VMEM(v.shape, v.dtype)
        for k, v in enumerate(operands)
    ] + [
        pltpu.VMEM((16, 16, 1024), F32),
        pltpu.VMEM((4, 16, 1024), F32),
        pltpu.VMEM((4, 16, 1024), F32),
        pltpu.VMEM((4, 16, 1024), F32),
        pltpu.VMEM((64, 512), F32),
        pltpu.VMEM((64, 128), F32),
        pltpu.VMEM((16, 256), BF16),
        pltpu.VMEM((2, nz, 16, 256), BF16),
        pltpu.VMEM((2, ny, 16, 256), BF16),
        pltpu.VMEM((ny, 16, 256), BF16),
        pltpu.VMEM((nz, 16, 256), BF16),
        pltpu.VMEM((ny, 16, 256), BF16),
        pltpu.VMEM((ny, 16, 256), BF16),
        pltpu.VMEM((ny, 16, 256), BF16),
        pltpu.VMEM((4, 16, 512), BF16),
        pltpu.VMEM((4, 16, 128), BF16),
        pltpu.VMEM((no, rpo, 640), F32),
        pltpu.VMEM((no, rpo, 640), F32),
        pltpu.VMEM((2 * rpo, 384), BF16),
        pltpu.VMEM((2 * rpo, 384), BF16),
        pltpu.VMEM((2 * rpo, 384), BF16),
        pltpu.VMEM((no, 2 * rpo, 384), BF16),
        pltpu.VMEM((256, 256), F32),
        pltpu.VMEM((256, 256), F32),
        pltpu.VMEM((256, 256), F32),
        pltpu.VMEM((16, 256), BF16),
        pltpu.VMEM((2, nx, 16, 256), BF16),
        pltpu.VMEM((16, 256), BF16),
        pltpu.VMEM((16, 256), BF16),
        pltpu.VMEM((16, 256), F32),
        pltpu.VMEM((16, 256), F32),
        pltpu.VMEM((32, 256), F32),
        pltpu.VMEM((32, 256), F32),
        pltpu.VMEM((16, 256), BF16),
        pltpu.VMEM((2, nz, 16, 256), BF16),
        pltpu.VMEM((2, ny, 16, 256), BF16),
        pltpu.VMEM((ny, 16, 256), BF16),
        pltpu.VMEM((nz, 16, 128), BF16),
        pltpu.VMEM((ny, 16, 128), BF16),
        pltpu.VMEM((ny, 16, 128), BF16),
        pltpu.VMEM((16, 1024), F32),
        pltpu.VMEM((16, 1024), BF16),
        pltpu.SemaphoreType.DMA((copies,)),
        pltpu.SemaphoreType.DMA((copies,)),
        pltpu.SemaphoreType.DMA((len(operands),)),
        pltpu.SemaphoreType.REGULAR,
        pltpu.SemaphoreType.DMA((2, nz)),
        pltpu.SemaphoreType.DMA((2, 2, nz)),
        pltpu.SemaphoreType.DMA((2, 2, ny)),
        pltpu.SemaphoreType.DMA((2, ny)),
        pltpu.SemaphoreType.DMA((nx,)),
        pltpu.SemaphoreType.DMA((2, nx)),
        pltpu.SemaphoreType.DMA((2,)),
        pltpu.SemaphoreType.DMA((2,)),
    ]
    return pl.pallas_call(
        functools.partial(kernel, geo),
        out_shape=(
            pltpu.VMEM(queries.shape, BF16),
            pltpu.VMEM(mamba_x.shape, BF16),
        ),
        in_specs=[pl.BlockSpec(memory_space=pl.ANY)] * len(operands),
        out_specs=(vmem, vmem),
        scratch_shapes=scratch,
        compiler_params=pltpu.CompilerParams(
            collective_id=0, has_side_effects=True, vmem_limit_bytes=60 * 1024 * 1024
        ),
    )(*operands)


def solution(mesh):
    placed = (
        P(None, "rep", "tp"),
        P(None, "rep", "tp"),
        P("rep", "tp", None, None),
        P("rep", None),
        P(),
        P(),
        P(None, "rep", "tp"),
        P(None, "rep", "tp"),
        P("rep", None, "tp"),
        P("rep", None, "tp"),
        P(None, "tp"),
        P(None, "tp"),
        P("tp"),
        P(None, "tp"),
        P("tp"),
        P(None, "tp"),
        P("tp"),
        P(),
        P(),
        P(),
    )
    return jax.shard_map(
        functools.partial(shards, geometry(mesh)),
        mesh=mesh,
        in_specs=placed,
        out_specs=(P(None, "rep", "tp"), P(None, "rep", "tp")),
        check_vma=False,
    )
```

```python
import functools

import jax
import jax.numpy as jnp
from jax import lax
from jax.experimental import pallas as pl
from jax.experimental.pallas import tpu as pltpu
from jax.sharding import PartitionSpec as P

F32 = jnp.float32
BF16 = jnp.bfloat16
I32 = jnp.int32
EPS = 1e-06
MASKED = -1e30
SCALE = 128**-0.5


def geometry(mesh):
    rep, tp = mesh.shape["rep"], mesh.shape["tp"]
    ny = 4 if rep >= 16 else 2
    return (rep // ny, ny, tp // 4)


def nn(a, b):
    return lax.dot_general(a, b, (((1,), (0,)), ((), ())), preferred_element_type=F32)


def nt(a, b):
    return lax.dot_general(a, b, (((1,), (1,)), ((), ())), preferred_element_type=F32)


def hot(cond):
    return jnp.where(cond, 1.0, 0.0).astype(BF16)


def iota(shape, dim):
    return lax.broadcasted_iota(I32, shape, dim)


def silu(v):
    return v / (1.0 + jnp.exp(-v))


def softplus(v):
    return jnp.maximum(v, 0.0) + jnp.log1p(jnp.exp(-jnp.abs(v)))


def attend(q_rows, keys, values, extra_keys, extra_values, bias, extra_bias):
    scores = nt(q_rows, keys) * SCALE + bias
    extra = nt(q_rows, extra_keys) * SCALE + extra_bias
    peak = jnp.maximum(
        jnp.max(scores, axis=1, keepdims=True), jnp.max(extra, axis=1, keepdims=True)
    )
    weight = jnp.exp(scores - peak)
    extra_weight = jnp.exp(extra - peak)
    total = jnp.sum(weight, axis=1, keepdims=True) + jnp.sum(extra_weight, axis=1, keepdims=True)
    out = nn(weight.astype(BF16), values) + nn(extra_weight.astype(BF16), extra_values)
    lane = iota((q_rows.shape[0], 128), 1)
    return out, jnp.where(lane < 64, peak, total)


def combine(near, far):
    near_peak, near_sum = near[:, 128:129], near[:, 192:193]
    far_peak, far_sum = far[:, 128:129], far[:, 192:193]
    peak = jnp.maximum(near_peak, far_peak)
    near_scale = jnp.exp(near_peak - peak)
    far_scale = jnp.exp(far_peak - peak)
    numer = near[:, :128] * near_scale + far[:, :128] * far_scale
    return numer / (near_sum * near_scale + far_sum * far_scale)


def tail_norm(tail):
    lane = iota(tail.shape, 1)
    square = tail * tail
    mean_b = jnp.sum(jnp.where(lane < 16, square, 0.0), axis=1, keepdims=True) / 16.0
    mean_c = jnp.sum(
        jnp.where((lane >= 16) & (lane < 32), square, 0.0), axis=1, keepdims=True
    ) / 16.0
    scale = jnp.where(lane < 16, lax.rsqrt(mean_b + EPS), lax.rsqrt(mean_c + EPS))
    return jnp.where(lane < 32, tail * scale, 0.0)


def by_quarter(blocks):
    quarter = iota(blocks[0].shape, 0) >> 2
    return jnp.where(
        quarter == 0,
        blocks[0],
        jnp.where(quarter == 1, blocks[1], jnp.where(quarter == 2, blocks[2], blocks[3])),
    )


def kernel(
    geo,
    src_ref_h,
    q_ref_h,
    nk_ref_h,
    x_ref_h,
    src_s_h,
    conv_ref_h,
    cw_ref_h,
    cb_ref_h,
    xw_h,
    page_ref_h,
    len_ref_h,
    pool_h,
    dtg_ref_h,
    dw_h,
    dtb_ref_h,
    bg_ref_h,
    cg_ref_h,
    skip_ref_h,
    a_ref_h,
    ssm_h,
    z_ref_h,
    attn_ref,
    mix_ref,
    src_ref,
    q_ref,
    nk_ref,
    x_ref,
    src_s,
    conv_ref,
    cw_ref,
    cb_ref,
    xw,
    page_ref,
    len_ref,
    pool,
    dtg_ref,
    dw,
    dtb_ref,
    bg_ref,
    cg_ref,
    skip_ref,
    a_ref,
    ssm,
    z_ref,
    mid,
    act,
    dts,
    mixed,
    dtl,
    tails,
    item_x,
    gather_x,
    stage_x,
    land_x,
    gather_q,
    stage_q,
    land_q,
    land_o,
    q_other,
    nk_other,
    part,
    part_land,
    half_send,
    half_land,
    norm_send,
    norm_land,
    near,
    away,
    far,
    late_send,
    late_land,
    late_half,
    late_half_land,
    late_acc,
    late_total,
    late_away,
    late_far,
    item_m,
    gather_m,
    stage_m,
    land_m,
    gather_a,
    stage_a,
    land_a,
    bias_ref,
    mask_ref,
    ssem,
    rsem,
    lsem,
    ready,
    zs,
    zr,
    ys,
    yr,
    ls,
    lr,
    hs,
    hr,
):
    nz, ny, nx = geo
    no = 2 * nx
    rpo = 64 // no
    n = src_ref.shape[1]
    rep, tp = lax.axis_index("rep"), lax.axis_index("tp")
    zi, yi = rep // ny, rep % ny
    core, zh, xi = tp % 2, (tp // 2) % 2, tp // 4
    own = xi * 2 + core
    tp_other = tp + 1 - 2 * core
    tp_half = tp + 2 - 4 * zh
    tp_odd = tp + 1 - core

    def o_tp(d):
        o = (own + d) % no
        return (o // 2) * 4 + zh * 2 + o % 2

    def z_rep(d):
        return ((zi + d) % nz) * ny + yi

    def y_rep(e):
        return zi * ny + (yi + e) % ny

    partners = [(z_rep(d), tp) for d in range(1, nz)]
    partners += [(z_rep(d), tp_other) for d in range(1, nz)]
    partners += [(y_rep(e), tp) for e in range(1, ny)]
    partners += [(y_rep(e), tp_other) for e in range(1, ny)]
    partners += [(rep, o_tp(d)) for d in range(1, no)]
    mirror = ((nz - 1 - zi) * ny + yi, tp_half)
    partners += [mirror]
    barrier = pltpu.get_barrier_semaphore()
    for device in partners:
        pl.semaphore_signal(
            barrier, inc=1, device_id=device, device_id_type=pl.DeviceIdType.MESH
        )

    loads = {}
    for k, (name, a, b) in enumerate(
        (
            ("src_ref", src_ref_h, src_ref),
            ("q_ref", q_ref_h, q_ref),
            ("nk_ref", nk_ref_h, nk_ref),
            ("x_ref", x_ref_h, x_ref),
            ("src_s", src_s_h, src_s),
            ("conv_ref", conv_ref_h, conv_ref),
            ("cw_ref", cw_ref_h, cw_ref),
            ("cb_ref", cb_ref_h, cb_ref),
            ("xw", xw_h, xw),
            ("page_ref", page_ref_h, page_ref),
            ("len_ref", len_ref_h, len_ref),
            ("pool", pool_h, pool),
            ("dtg_ref", dtg_ref_h, dtg_ref),
            ("dw", dw_h, dw),
            ("dtb_ref", dtb_ref_h, dtb_ref),
            ("bg_ref", bg_ref_h, bg_ref),
            ("cg_ref", cg_ref_h, cg_ref),
            ("skip_ref", skip_ref_h, skip_ref),
            ("a_ref", a_ref_h, a_ref),
            ("ssm", ssm_h, ssm),
            ("z_ref", z_ref_h, z_ref),
        )
    ):
        loads[name] = pltpu.make_async_copy(a, b, lsem.at[k])
        loads[name].start()

    def need(*names):
        for name in names:
            loads[name].wait()

    used = []

    def push(src, dst, device):
        k = len(used)
        copy = pltpu.make_async_remote_copy(
            src_ref=src,
            dst_ref=dst,
            send_sem=ssem.at[k],
            recv_sem=rsem.at[k],
            device_id=device,
            device_id_type=pl.DeviceIdType.MESH,
        )
        copy.start()
        used.append(copy)
        return copy

    def link(src, dst, send_sem, recv_sem, device):
        return pltpu.make_async_remote_copy(
            src_ref=src,
            dst_ref=dst,
            send_sem=send_sem,
            recv_sem=recv_sem,
            device_id=device,
            device_id_type=pl.DeviceIdType.MESH,
        )

    even, odd_core = pl.when(core == 0), pl.when(core == 1)

    def z_copy(k, item, gather, c, d):
        return link(item, gather.at[c, d], zs.at[k, d], zr.at[k, c, d], (z_rep(d), tp_odd))

    def y_copy(k, stage, land, c, e):
        return link(
            stage.at[c, e], land.at[e], ys.at[k, c, e], yr.at[k, e], (y_rep(e), tp_odd - 1 + c)
        )

    def late_copy(c, d):
        device = (rep, ((xi + d) % nx) * 4 + zh * 2 + 1)
        return link(late_send, late_land.at[c, d], ls.at[d], lr.at[c, d], device)

    def set_out(k, item, gather):
        for d in range(1, nz):
            z_copy(k, item, gather, core, d).start()

        @even
        def _():
            z_copy(k, item, gather, 0, 0).start()

        @odd_core
        def _():
            gather[1, 0] = item[...]

    def turn(k, item, gather, stage, land, chooser):
        @odd_core
        def _():
            for c in (1, 0):
                for d in range(nz):
                    if (c, d) != (1, 0):
                        z_copy(k, item, gather, c, d).wait_recv()
                chosen = nn(chooser, gather[c].reshape(nz * 16, 256)).astype(BF16)
                for e in range(ny):
                    stage[c, e] = chosen[e * 16 : (e + 1) * 16]
                    if (c, e) != (1, 0):
                        y_copy(k, stage, land, c, e).start()
                    else:
                        land[0] = chosen[0:16]

    def arrive(k, stage, land):
        for e in range(1, ny):
            y_copy(k, stage, land, 0, e).wait_recv()

        @even
        def _():
            y_copy(k, stage, land, 0, 0).wait_recv()

    def drain(k, item, gather, stage, land):
        for d in range(1, nz):
            z_copy(k, item, gather, core, d).wait_send()

        @even
        def _():
            z_copy(k, item, gather, 0, 0).wait_send()

        @odd_core
        def _():
            for c in range(2):
                for e in range(ny):
                    if (c, e) != (1, 0):
                        y_copy(k, stage, land, c, e).wait_send()

    need("src_ref")
    src = src_ref[...]
    lane_n = iota((1, n), 1)
    foreign = src != lane_n
    foreign16 = jnp.broadcast_to(hot(foreign), (16, n))
    slot_pick = hot(iota((128, n), 1) == rep * 16 + (iota((128, n), 0) & 15))
    f128 = nt(foreign16, slot_pick)
    before = hot(
        (iota((128, 128), 0) < 16) & (iota((128, 128), 0) < (iota((128, 128), 1) & 15))
    )
    k128 = nn(f128.astype(BF16), before)
    row = iota((16, 128), 0)
    col = iota((16, 128), 1)
    rank = ((row >> 1) & 1).astype(F32)
    place = (f128 > 0.5) & (k128 == rank)
    pack = hot(place & ((row >> 2) == ((col >> 4) & 3)) & ((row & 1) == (col >> 6)))
    pick16 = hot(place & (col < 16))[:, :16]

    need("q_ref", "nk_ref", "x_ref")
    blocks = []
    nothing = jnp.zeros((16, 256), BF16)
    for s in (2, 3):
        x_s = x_ref[s]
        q_s = q_ref[s]
        nk_s = nk_ref[s]
        for b in range(4):
            side = (
                q_s[:, b * 256 : (b + 1) * 256]
                if b < 2
                else (jnp.concatenate([nk_s, nothing[:, :128]], axis=1) if b == 2 else nothing)
            )
            blocks.append(jnp.concatenate([x_s[:, b * 256 : (b + 1) * 256], side], axis=1))
    item = nn(pack, jnp.concatenate(blocks, axis=0)).astype(BF16)
    item_x[...] = item[:, 0:256]
    gather_q[0] = item[:, 256:512]

    need("conv_ref", "cw_ref", "cb_ref")
    window = [conv_ref[w].astype(F32) for w in range(3)] + [x_ref[s].astype(F32) for s in range(4)]
    conv_last = window[2].astype(BF16)
    cw = cw_ref[...]
    cb = cb_ref[...]
    activ = []
    for s in range(4):
        total = window[s] * cw[0:1]
        for w in range(1, 4):
            total = total + window[s + w] * cw[w : w + 1]
        activ.append(silu(total + cb))
        act[s] = activ[s]
    activ_b = jnp.concatenate([v.astype(BF16) for v in activ], axis=0)
    need("xw")

    def project(rows):
        tail = jnp.concatenate([xw[512:544, :], jnp.zeros((96, 1024), BF16)], axis=0)
        return nt(rows, xw[0:512, :]), nt(rows, tail)

    main, tail = project(activ_b)
    for o in range(no):
        part[o, :, 0:512] = main[o * rpo : (o + 1) * rpo]
        part[o, :, 512:640] = tail[o * rpo : (o + 1) * rpo]
    pl.semaphore_wait(barrier, len(partners))
    pl.semaphore_signal(ready, inc=1, device_id=mirror, device_id_type=pl.DeviceIdType.MESH)

    set_out(0, item_x, gather_x)
    part_out = [
        push(part.at[(own + d) % no], part_land.at[d], (rep, o_tp(d))) for d in range(1, no)
    ]
    z_q = [push(gather_q.at[0], gather_q.at[d], (z_rep(d), tp)) for d in range(1, nz)]
    q_swap = push(q_ref, q_other, (rep, tp_other))
    nk_swap = push(nk_ref, nk_other, (rep, tp_other))

    same = iota((n, n), 0)
    lane_nn = iota((n, n), 1)
    rank16 = nn(foreign16, hot(((same >> 4) == (lane_nn >> 4)) & (same < lane_nn)))
    rank_there = nn(rank16.astype(BF16), hot(same == src))
    home = jnp.where(foreign, (lane_n >> 4) * 2 + rank16[0:1].astype(I32), -1)
    donor = jnp.where(foreign, (src >> 4) * 2 + rank_there[0:1].astype(I32), -1)
    to_row = iota((ny * 16, n), 0)
    to_code = (zi * ny + ((yi + (to_row >> 4)) & (ny - 1))) * 2 + ((to_row >> 1) & 1)
    from_row = iota((nz * 16, n), 0)
    from_code = (((zi - (from_row >> 4)) & (nz - 1)) * ny + yi) * 2 + ((from_row >> 1) & 1)
    r_ = iota((ny * 16, nz * 16), 0)
    c_ = iota((ny * 16, nz * 16), 1)
    alike = ((r_ >> 2) & 3 == (c_ >> 2) & 3) & ((r_ & 1) == (c_ & 1))
    select_in = hot(alike & (nt(hot(donor == to_code), hot(home == from_code)) > 0.5))
    select_out = hot(alike & (nt(hot(home == to_code), hot(donor == from_code)) > 0.5))

    def select(copies, chooser, gathered, staged, landing):
        for copy in copies:
            copy.wait_recv()
        width = gathered.shape[2]
        chosen = nn(chooser, gathered[...].reshape(nz * 16, width)).astype(BF16)
        for e in range(ny):
            staged[e] = chosen[e * 16 : (e + 1) * 16]
        landing[0] = chosen[0:16]
        return [push(staged.at[e], landing.at[e], (y_rep(e), tp)) for e in range(1, ny)]

    for copy in part_out:
        copy.wait_recv()
    summed = part[own]
    for d in range(1, no):
        summed = summed + part_land[d]
    blank = jnp.zeros((rpo, 128), F32)

    def pack_half(v):
        return jnp.concatenate(
            [
                jnp.concatenate([v[:, 0:256], v[:, 512:640]], axis=1),
                jnp.concatenate([v[:, 256:512], blank], axis=1),
            ],
            axis=0,
        ).astype(BF16)

    def unpack_half(v):
        v = v.astype(F32)
        return jnp.concatenate([v[:rpo, 0:256], v[rpo:, 0:256], v[:rpo, 256:384]], axis=1)

    half_send[...] = pack_half(summed)

    turn(0, item_x, gather_x, stage_x, land_x, select_in)
    pl.semaphore_wait(ready, 1)
    half = push(half_send, half_land, (rep, tp_half))

    y_q = select(z_q, select_in, gather_q, stage_q, land_q)
    y_q += [push(stage_q.at[e], land_o.at[e], (y_rep(e), tp_other)) for e in range(ny)]

    need("page_ref", "len_ref")
    own_lane = iota((16, n), 1) == rep * 16 + iota((16, n), 0)
    lengths = jnp.sum(jnp.where(own_lane, len_ref[...], 0), axis=1, keepdims=True)
    foreign_col = (
        jnp.sum(jnp.where(own_lane & foreign, 1.0, 0.0), axis=1, keepdims=True) > 0.5
    )
    table = page_ref[...]
    eye = iota((16, 16), 0) == iota((16, 16), 1)
    cache_lane = iota((16, 1024), 1)
    allowed = jnp.zeros((16, 1024), F32)
    for k in range(4):
        page = jnp.where(core == 0, table[2 * k : 2 * k + 1], table[2 * k + 1 : 2 * k + 2])
        page = jnp.sum(jnp.where(eye, page, 0), axis=1, keepdims=True)
        limit = lengths - (2 * k + core) * 16
        allowed = jnp.where(
            ((cache_lane >> 4) == page) & ((cache_lane & 15) < limit), 1.0, allowed
        )
    mask_ref[...] = allowed.astype(BF16)
    bias_ref[...] = jnp.where(allowed > 0.5, 0.0, MASKED)

    need("pool")
    q_swap.wait_recv()
    nk_swap.wait_recv()
    pages = pool[...].reshape(1024, 256)
    keys, values = pages[:, 0:128], pages[:, 128:256]
    pad64 = jnp.zeros((64, 128), BF16)
    new_keys = [nk_ref[s] for s in range(4)]
    new_values = [nk_other[s] for s in range(4)]
    extra_keys = jnp.concatenate(new_keys + [pad64], axis=0)
    extra_values = jnp.concatenate(new_values + [pad64], axis=0)
    row_q = iota((256, 128), 0)
    col_q = iota((256, 128), 1)
    extra_bias = jnp.where(
        ((row_q & 15) == (col_q & 15)) & ((col_q >> 4) <= (row_q >> 6)) & (core == 0), 0.0, MASKED
    )
    bias16 = bias_ref[...]
    bias = jnp.concatenate([bias16] * 16, axis=0)
    def attend_all(source, target):
        rows = jnp.concatenate(
            [source[s][:, h * 128 : (h + 1) * 128] for s in range(4) for h in range(4)], axis=0
        )
        out, stats = attend(rows, keys, values, extra_keys, extra_values, bias, extra_bias)
        target[:, 0:128] = out
        target[:, 128:256] = stats

    attend_all(q_other, away)
    partial = push(away, far, (rep, tp_other))

    arrive(0, stage_x, land_x)
    er = iota((128, ny * 16), 0)
    ec = iota((128, ny * 16), 1)
    wanted_step = jnp.where(er < 64, er & 1, 0)
    expand = hot(
        (((er >> 4) & 3) == ((ec >> 2) & 3))
        & (((er >> 1) & 1) == ((ec >> 1) & 1))
        & (wanted_step == (ec & 1))
    )
    arrived = nn(expand, land_x[...].reshape(ny * 16, 256))
    x_now = jnp.concatenate([arrived[b * 16 : (b + 1) * 16] for b in range(4)], axis=1)
    x_prev = jnp.concatenate(
        [arrived[64 + b * 16 : 64 + (b + 1) * 16] for b in range(4)], axis=1
    )
    last_row = nn(pick16, conv_last)
    x_zero = nn(pick16, x_ref[0])
    x_one = nn(pick16, x_ref[1])
    odd = (iota((16, 1024), 0) & 1) == 1
    total = jnp.where(odd, x_zero, last_row) * cw[0:1]
    total = total + jnp.where(odd, x_one, x_zero) * cw[1:2]
    total = total + jnp.where(odd, x_prev, x_one) * cw[2:3]
    total = total + x_now * cw[3:4]
    late_act = silu(total + cb)
    main, tail = project(late_act.astype(BF16))
    late_own = jnp.concatenate(
        [by_quarter([main[:, b * 128 : (b + 1) * 128] for b in range(4)]), tail], axis=1
    )
    late_send[...] = late_own.astype(BF16)
    for d in range(1, nx):
        late_copy(core, d).start()

    @even
    def _():
        late_copy(0, 0).start()


    attend_all(q_ref, near)

    late_swap = link(late_half, late_half_land, hs.at[0], hr.at[0], (rep, tp_half))
    late_over = link(late_total, late_total, hs.at[1], hr.at[1], (rep, tp_odd - 1))

    @odd_core
    def _():
        late_sum = late_own
        for c in range(2):
            for d in range(nx):
                if (c, d) != (1, 0):
                    late_copy(c, d).wait_recv()
                    late_sum = late_sum + late_land[c, d].astype(F32)
        late_acc[...] = late_sum
        late_half[...] = late_sum.astype(BF16)
        late_swap.start()

    need("dtg_ref")
    half.wait_recv()
    summed = summed + unpack_half(half_land[...])
    main = summed[:, 0:512]
    mean = jnp.sum(main * main, axis=1, keepdims=True) / 512.0
    low = main * lax.rsqrt(mean + EPS) * dtg_ref[...]
    normed = jnp.concatenate([low, tail_norm(summed[:, 512:640])], axis=1)
    packed = pack_half(normed)
    norm_send[...] = packed
    norm_out = [push(norm_send, norm_land.at[d], (rep, o_tp(d))) for d in range(1, no)]

    def take(o, v):
        v = unpack_half(v)
        start = pl.multiple_of(o * rpo, rpo)
        dtl[pl.ds(start, rpo), :] = v[:, 0:512]
        tails[pl.ds(start, rpo), :] = v[:, 512:640]

    take(own, packed)

    for copy in y_q:
        copy.wait_recv()
    arrived_q = nn(expand[0:64], land_q[...].reshape(ny * 16, 256))
    arrived_o = nn(expand[0:64], land_o[...].reshape(ny * 16, 256))
    q_late = jnp.concatenate(
        [
            v[(h // 2) * 16 : (h // 2) * 16 + 8, (h % 2) * 128 : (h % 2) * 128 + 128]
            for v in (arrived_q, arrived_o)
            for h in range(4)
        ],
        axis=0,
    ).astype(BF16)
    pad48 = jnp.zeros((48, 128), BF16)
    late_keys = jnp.concatenate(
        new_keys + [arrived_q[32:48, 0:128].astype(BF16), pad48], axis=0
    )
    late_values = jnp.concatenate(
        new_values + [arrived_o[32:48, 0:128].astype(BF16), pad48], axis=0
    )
    fits = (place & (col < 32)) | (
        (col >= 64)
        & (col < 68)
        & (((col >> 1) & 1) == ((row >> 1) & 1))
        & ((col & 1) <= (row & 1))
    )
    late_extra = jnp.where(fits & (core == 0), 0.0, MASKED)[0:8]
    late_bias = jnp.where(nn(pick16, mask_ref[...]) > 0.5, 0.0, MASKED)[0:8]
    out, stats = attend(
        q_late,
        keys,
        values,
        late_keys,
        late_values,
        jnp.concatenate([late_bias] * 8, axis=0),
        jnp.concatenate([late_extra] * 8, axis=0),
    )
    late_near = jnp.concatenate([out[0:32], stats[0:32]], axis=1)
    late_away[...] = jnp.concatenate([out[32:64], stats[32:64]], axis=1)
    late_partial = push(late_away, late_far, (rep, tp_other))

    for d, copy in enumerate(norm_out, 1):
        copy.wait_recv()
        take((own - d + no) % no, norm_land[d])
    need("dw", "dtb_ref", "bg_ref", "cg_ref", "skip_ref", "a_ref", "ssm")
    steps = softplus(nn(dtl[...].astype(BF16), dw[...]) + dtb_ref[...])
    for s in range(4):
        dts[s] = steps[s * 16 : (s + 1) * 16]
    b_gain = jnp.sum(jnp.where(eye, bg_ref[...], 0.0), axis=1, keepdims=True)
    c_gain = jnp.sum(jnp.where(eye, cg_ref[...], 0.0), axis=1, keepdims=True)
    skip = skip_ref[...]

    def columns(tail_row):
        b = jnp.sum(jnp.where(col == row, tail_row, 0.0), axis=1, keepdims=True) * b_gain
        c = jnp.sum(jnp.where(col == row + 16, tail_row, 0.0), axis=1, keepdims=True) * c_gain
        return b, c

    def advance(state, dt_row, act_row, tail_row):
        b, c = columns(tail_row)
        state = jnp.exp(-dt_row * a_ref[...]) * state + (dt_row * act_row) * b
        return state, jnp.sum(state * c, axis=0, keepdims=True) + skip * act_row

    def scan(first, held, keep):
        def body(i, carry):
            state = held[i]
            for s in (first, first + 1):
                state, out = advance(
                    state,
                    dts[s, pl.ds(i, 1), :],
                    act[s, pl.ds(i, 1), :],
                    tails[pl.ds(s * 16 + i, 1), :],
                )
                mixed[s, pl.ds(i, 1), :] = out
            if keep:
                mid[i] = state
            return carry

        lax.fori_loop(0, 16, body, 0)

    scan(0, ssm, True)

    late_partial.wait_recv()
    heads = combine(late_near, late_far[...]).astype(BF16)
    hr = iota((16, 32), 0)
    hc = iota((16, 32), 1)
    heads = nn(hot(((hr >> 2) == (hc >> 3)) & ((hr & 3) == (hc & 7))), heads)
    gather_a[0] = heads.astype(BF16)
    z_a = [push(gather_a.at[0], gather_a.at[d], (z_rep(d), tp)) for d in range(1, nz)]

    @odd_core
    def _():
        late_swap.wait_recv()
        late_total[...] = late_acc[...] + late_half_land[...].astype(F32)
        late_over.start()

    @even
    def _():
        late_over.wait_recv()

    late_sum = late_total[...]
    main = late_sum[:, 0:128]
    square = jnp.broadcast_to(jnp.sum(main * main, axis=1, keepdims=True), (16, 128))
    square = square + pltpu.roll(square, 8, 0)
    square = square + pltpu.roll(square, 4, 0)
    gain = dtg_ref[...]
    gains = by_quarter(
        [jnp.broadcast_to(gain[:, b * 128 : (b + 1) * 128], (16, 128)) for b in range(4)]
    )
    low = (main * lax.rsqrt(square / 512.0 + EPS) * gains).astype(BF16)
    wr = iota((64, 16), 0)
    wc = iota((64, 16), 1)
    spread = nn(hot(((wr >> 4) == (wc >> 2)) & ((wr & 3) == (wc & 3))), low)
    low = jnp.concatenate([spread[b * 16 : (b + 1) * 16] for b in range(4)], axis=1)
    late_dt = softplus(nn(low.astype(BF16), dw[...]) + dtb_ref[...])
    late_tail = tail_norm(late_sum[:, 128:256])

    need("src_s")
    base = rep * 16
    first = jnp.int32(-1)
    second = jnp.int32(0)
    for i in range(16):
        moves = src_s[base + i] != base + i
        second = jnp.where(moves & (first >= 0), i, second)
        first = jnp.where(moves & (first < 0), i, first)
    first = jnp.maximum(first, 0)
    rows = iota((16, 1024), 0) & 3
    late_mixed = jnp.zeros((16, 1024), F32)
    for r, slot in enumerate((first, second)):
        state = mid[slot]
        for s in range(2):
            m = r * 2 + s
            state, out = advance(
                state, late_dt[m : m + 1], late_act[m : m + 1], late_tail[m : m + 1]
            )
            late_mixed = jnp.where(rows == m, out, late_mixed)
    item_m[...] = by_quarter(
        [late_mixed[:, b * 256 : (b + 1) * 256] for b in range(4)]
    ).astype(BF16)
    set_out(1, item_m, gather_m)

    scan(2, mid, False)
    need("z_ref")
    partial.wait_recv()
    kept = []
    gates = []
    for s in range(4):
        gate = silu(z_ref[s].astype(F32))
        block = combine(near[s * 64 : (s + 1) * 64, :], far[s * 64 : (s + 1) * 64, :])
        block = jnp.concatenate([block[h * 16 : (h + 1) * 16] for h in range(4)], axis=1)
        if s < 2:
            attn_ref[s] = block.astype(BF16)
            mix_ref[s] = (mixed[s] * gate).astype(BF16)
        else:
            kept.append(block)
            gates.append((gate, mixed[s] * gate))

    own_code = rep * 2 + ((iota((ny * 16, n), 0) >> 1) & 1)
    fr = iota((128, ny * 16), 0)
    fc = iota((128, ny * 16), 1)
    put = hot(
        (((fr >> 4) & 3) == ((fc >> 2) & 3))
        & ((fr >> 6) == (fc & 1))
        & (nt(slot_pick, hot(home == own_code)) > 0.5)
    )
    turn(1, item_m, gather_m, stage_m, land_m, select_out)
    y_a = select(z_a, select_out, gather_a, stage_a, land_a)
    spots = [[s * 64 + b * 16 for b in range(4)] for s in range(2)]
    for copy in y_a:
        copy.wait_recv()
    attended = nn(put, land_a[...].reshape(ny * 16, 128))
    for s in range(2):
        back = jnp.concatenate([attended[p : p + 16] for p in spots[s]], axis=1)
        attn_ref[s + 2] = jnp.where(foreign_col, back, kept[s]).astype(BF16)
    arrive(1, stage_m, land_m)
    returned = nn(put, land_m[...].reshape(ny * 16, 256))
    for s in range(2):
        back = jnp.concatenate([returned[p : p + 16] for p in spots[s]], axis=1)
        gate, own_mix = gates[s]
        mix_ref[s + 2] = jnp.where(foreign_col, back * gate, own_mix).astype(BF16)

    for copy in used:
        copy.wait_send()
    drain(0, item_x, gather_x, stage_x, land_x)
    drain(1, item_m, gather_m, stage_m, land_m)
    for d in range(1, nx):
        late_copy(core, d).wait_send()

    @even
    def _():
        late_copy(0, 0).wait_send()

    @odd_core
    def _():
        late_swap.wait_send()
        late_over.wait_send()


def shards(
    geo,
    queries,
    new_kv,
    kv_pool,
    page_table,
    kv_lengths,
    slot_source,
    mamba_x,
    mamba_z,
    conv_state,
    ssm_state,
    x_proj_weight,
    dt_proj_weight,
    dt_bias,
    a_rate,
    skip_gain,
    conv_weight,
    conv_bias,
    dt_gain,
    b_gain,
    c_gain,
):
    nz, ny, nx = geo
    no = 2 * nx
    rpo = 64 // no
    copies = 2 * (nz - 1) + 2 * (ny - 1) + ny + 2 * (no - 1) + 5
    operands = (
        slot_source.reshape(1, -1),
        queries,
        new_kv,
        mamba_x,
        slot_source,
        conv_state.transpose(1, 0, 2),
        conv_weight,
        conv_bias.reshape(1, -1),
        x_proj_weight,
        page_table.T,
        kv_lengths.reshape(1, -1),
        kv_pool,
        dt_gain.reshape(1, -1),
        dt_proj_weight,
        dt_bias.reshape(1, -1),
        b_gain.reshape(1, -1),
        c_gain.reshape(1, -1),
        skip_gain.reshape(1, -1),
        a_rate,
        ssm_state,
        mamba_z,
    )
    vmem = pl.BlockSpec(memory_space=pltpu.VMEM)
    scratch = [
        pltpu.SMEM(v.shape, v.dtype) if k == 4 else pltpu.VMEM(v.shape, v.dtype)
        for k, v in enumerate(operands)
    ] + [
        pltpu.VMEM((16, 16, 1024), F32),
        pltpu.VMEM((4, 16, 1024), F32),
        pltpu.VMEM((4, 16, 1024), F32),
        pltpu.VMEM((4, 16, 1024), F32),
        pltpu.VMEM((64, 512), F32),
        pltpu.VMEM((64, 128), F32),
        pltpu.VMEM((16, 256), BF16),
        pltpu.VMEM((2, nz, 16, 256), BF16),
        pltpu.VMEM((2, ny, 16, 256), BF16),
        pltpu.VMEM((ny, 16, 256), BF16),
        pltpu.VMEM((nz, 16, 256), BF16),
        pltpu.VMEM((ny, 16, 256), BF16),
        pltpu.VMEM((ny, 16, 256), BF16),
        pltpu.VMEM((ny, 16, 256), BF16),
        pltpu.VMEM((4, 16, 512), BF16),
        pltpu.VMEM((4, 16, 128), BF16),
        pltpu.VMEM((no, rpo, 640), F32),
        pltpu.VMEM((no, rpo, 640), F32),
        pltpu.VMEM((2 * rpo, 384), BF16),
        pltpu.VMEM((2 * rpo, 384), BF16),
        pltpu.VMEM((2 * rpo, 384), BF16),
        pltpu.VMEM((no, 2 * rpo, 384), BF16),
        pltpu.VMEM((256, 256), F32),
        pltpu.VMEM((256, 256), F32),
        pltpu.VMEM((256, 256), F32),
        pltpu.VMEM((16, 256), BF16),
        pltpu.VMEM((2, nx, 16, 256), BF16),
        pltpu.VMEM((16, 256), BF16),
        pltpu.VMEM((16, 256), BF16),
        pltpu.VMEM((16, 256), F32),
        pltpu.VMEM((16, 256), F32),
        pltpu.VMEM((32, 256), F32),
        pltpu.VMEM((32, 256), F32),
        pltpu.VMEM((16, 256), BF16),
        pltpu.VMEM((2, nz, 16, 256), BF16),
        pltpu.VMEM((2, ny, 16, 256), BF16),
        pltpu.VMEM((ny, 16, 256), BF16),
        pltpu.VMEM((nz, 16, 128), BF16),
        pltpu.VMEM((ny, 16, 128), BF16),
        pltpu.VMEM((ny, 16, 128), BF16),
        pltpu.VMEM((16, 1024), F32),
        pltpu.VMEM((16, 1024), BF16),
        pltpu.SemaphoreType.DMA((copies,)),
        pltpu.SemaphoreType.DMA((copies,)),
        pltpu.SemaphoreType.DMA((len(operands),)),
        pltpu.SemaphoreType.REGULAR,
        pltpu.SemaphoreType.DMA((2, nz)),
        pltpu.SemaphoreType.DMA((2, 2, nz)),
        pltpu.SemaphoreType.DMA((2, 2, ny)),
        pltpu.SemaphoreType.DMA((2, ny)),
        pltpu.SemaphoreType.DMA((nx,)),
        pltpu.SemaphoreType.DMA((2, nx)),
        pltpu.SemaphoreType.DMA((2,)),
        pltpu.SemaphoreType.DMA((2,)),
    ]
    return pl.pallas_call(
        functools.partial(kernel, geo),
        out_shape=(
            pltpu.VMEM(queries.shape, BF16),
            pltpu.VMEM(mamba_x.shape, BF16),
        ),
        in_specs=[pl.BlockSpec(memory_space=pl.ANY)] * len(operands),
        out_specs=(vmem, vmem),
        scratch_shapes=scratch,
        compiler_params=pltpu.CompilerParams(
            collective_id=0, has_side_effects=True, vmem_limit_bytes=60 * 1024 * 1024
        ),
    )(*operands)


def solution(mesh):
    placed = (
        P(None, "rep", "tp"),
        P(None, "rep", "tp"),
        P("rep", "tp", None, None),
        P("rep", None),
        P(),
        P(),
        P(None, "rep", "tp"),
        P(None, "rep", "tp"),
        P("rep", None, "tp"),
        P("rep", None, "tp"),
        P(None, "tp"),
        P(None, "tp"),
        P("tp"),
        P(None, "tp"),
        P("tp"),
        P(None, "tp"),
        P("tp"),
        P(),
        P(),
        P(),
    )
    return jax.shard_map(
        functools.partial(shards, geometry(mesh)),
        mesh=mesh,
        in_specs=placed,
        out_specs=(P(None, "rep", "tp"), P(None, "rep", "tp")),
        check_vma=False,
    )
```

```python
import functools

import jax
import jax.numpy as jnp
from jax import lax
from jax.experimental import pallas as pl
from jax.experimental.pallas import tpu as pltpu
from jax.sharding import PartitionSpec as P

F32 = jnp.float32
BF16 = jnp.bfloat16
I32 = jnp.int32
EPS = 1e-06
MASKED = -1e30
SCALE = 128**-0.5


def geometry(mesh):
    rep, tp = mesh.shape["rep"], mesh.shape["tp"]
    ny = 4 if rep >= 16 else 2
    return (rep // ny, ny, tp // 4)


def nn(a, b):
    return lax.dot_general(a, b, (((1,), (0,)), ((), ())), preferred_element_type=F32)


def nt(a, b):
    return lax.dot_general(a, b, (((1,), (1,)), ((), ())), preferred_element_type=F32)


def hot(cond):
    return jnp.where(cond, 1.0, 0.0).astype(BF16)


def iota(shape, dim):
    return lax.broadcasted_iota(I32, shape, dim)


def silu(v):
    return v / (1.0 + jnp.exp(-v))


def softplus(v):
    return jnp.maximum(v, 0.0) + jnp.log1p(jnp.exp(-jnp.abs(v)))


def attend(q_rows, keys, values, extra_keys, extra_values, bias, extra_bias):
    scores = nt(q_rows, keys) * SCALE + bias
    extra = nt(q_rows, extra_keys) * SCALE + extra_bias
    peak = jnp.maximum(
        jnp.max(scores, axis=1, keepdims=True), jnp.max(extra, axis=1, keepdims=True)
    )
    weight = jnp.exp(scores - peak)
    extra_weight = jnp.exp(extra - peak)
    total = jnp.sum(weight, axis=1, keepdims=True) + jnp.sum(extra_weight, axis=1, keepdims=True)
    out = nn(weight.astype(BF16), values) + nn(extra_weight.astype(BF16), extra_values)
    lane = iota((q_rows.shape[0], 128), 1)
    return out, jnp.where(lane < 64, peak, total)


def combine(near, far):
    near_peak, near_sum = near[:, 128:129], near[:, 192:193]
    far_peak, far_sum = far[:, 128:129], far[:, 192:193]
    peak = jnp.maximum(near_peak, far_peak)
    near_scale = jnp.exp(near_peak - peak)
    far_scale = jnp.exp(far_peak - peak)
    numer = near[:, :128] * near_scale + far[:, :128] * far_scale
    return numer / (near_sum * near_scale + far_sum * far_scale)


def tail_norm(tail):
    lane = iota(tail.shape, 1)
    square = tail * tail
    mean_b = jnp.sum(jnp.where(lane < 16, square, 0.0), axis=1, keepdims=True) / 16.0
    mean_c = jnp.sum(
        jnp.where((lane >= 16) & (lane < 32), square, 0.0), axis=1, keepdims=True
    ) / 16.0
    scale = jnp.where(lane < 16, lax.rsqrt(mean_b + EPS), lax.rsqrt(mean_c + EPS))
    return jnp.where(lane < 32, tail * scale, 0.0)


def by_quarter(blocks):
    quarter = iota(blocks[0].shape, 0) >> 2
    return jnp.where(
        quarter == 0,
        blocks[0],
        jnp.where(quarter == 1, blocks[1], jnp.where(quarter == 2, blocks[2], blocks[3])),
    )


def kernel(
    geo,
    src_ref_h,
    q_ref_h,
    nk_ref_h,
    x_ref_h,
    src_s_h,
    conv_ref_h,
    cw_ref_h,
    cb_ref_h,
    xw_h,
    page_ref_h,
    len_ref_h,
    pool_h,
    dtg_ref_h,
    dw_h,
    dtb_ref_h,
    bg_ref_h,
    cg_ref_h,
    skip_ref_h,
    a_ref_h,
    ssm_h,
    z_ref_h,
    attn_ref,
    mix_ref,
    src_ref,
    q_ref,
    nk_ref,
    x_ref,
    src_s,
    conv_ref,
    cw_ref,
    cb_ref,
    xw,
    page_ref,
    len_ref,
    pool,
    dtg_ref,
    dw,
    dtb_ref,
    bg_ref,
    cg_ref,
    skip_ref,
    a_ref,
    ssm,
    z_ref,
    mid,
    act,
    dts,
    mixed,
    dtl,
    tails,
    gather_x,
    stage_x,
    land_x,
    gather_q,
    stage_q,
    land_q,
    land_o,
    q_other,
    nk_other,
    part,
    part_land,
    half_send,
    half_land,
    norm_send,
    norm_land,
    near,
    away,
    far,
    late_send,
    late_land,
    late_half,
    late_half_land,
    late_away,
    late_far,
    gather_m,
    stage_m,
    land_m,
    gather_a,
    stage_a,
    land_a,
    bias_ref,
    mask_ref,
    ssem,
    rsem,
    lsem,
    ready,
):
    nz, ny, nx = geo
    no = 2 * nx
    rpo = 64 // no
    n = src_ref.shape[1]
    rep, tp = lax.axis_index("rep"), lax.axis_index("tp")
    zi, yi = rep // ny, rep % ny
    core, zh, xi = tp % 2, (tp // 2) % 2, tp // 4
    own = xi * 2 + core
    tp_other = tp + 1 - 2 * core
    tp_half = tp + 2 - 4 * zh

    def o_tp(d):
        o = (own + d) % no
        return (o // 2) * 4 + zh * 2 + o % 2

    def z_rep(d):
        return ((zi + d) % nz) * ny + yi

    def y_rep(e):
        return zi * ny + (yi + e) % ny

    partners = [(z_rep(d), tp) for d in range(1, nz)]
    partners += [(y_rep(e), tp) for e in range(1, ny)]
    partners += [(y_rep(e), tp_other) for e in range(1, ny)]
    partners += [(rep, o_tp(d)) for d in range(1, no)]
    mirror = ((nz - 1 - zi) * ny + yi, tp_half)
    partners += [mirror]
    barrier = pltpu.get_barrier_semaphore()
    for device in partners:
        pl.semaphore_signal(
            barrier, inc=1, device_id=device, device_id_type=pl.DeviceIdType.MESH
        )

    loads = {}
    for k, (name, a, b) in enumerate(
        (
            ("src_ref", src_ref_h, src_ref),
            ("q_ref", q_ref_h, q_ref),
            ("nk_ref", nk_ref_h, nk_ref),
            ("x_ref", x_ref_h, x_ref),
            ("src_s", src_s_h, src_s),
            ("conv_ref", conv_ref_h, conv_ref),
            ("cw_ref", cw_ref_h, cw_ref),
            ("cb_ref", cb_ref_h, cb_ref),
            ("xw", xw_h, xw),
            ("page_ref", page_ref_h, page_ref),
            ("len_ref", len_ref_h, len_ref),
            ("pool", pool_h, pool),
            ("dtg_ref", dtg_ref_h, dtg_ref),
            ("dw", dw_h, dw),
            ("dtb_ref", dtb_ref_h, dtb_ref),
            ("bg_ref", bg_ref_h, bg_ref),
            ("cg_ref", cg_ref_h, cg_ref),
            ("skip_ref", skip_ref_h, skip_ref),
            ("a_ref", a_ref_h, a_ref),
            ("ssm", ssm_h, ssm),
            ("z_ref", z_ref_h, z_ref),
        )
    ):
        loads[name] = pltpu.make_async_copy(a, b, lsem.at[k])
        loads[name].start()

    def need(*names):
        for name in names:
            loads[name].wait()

    used = []

    def push(src, dst, device):
        k = len(used)
        copy = pltpu.make_async_remote_copy(
            src_ref=src,
            dst_ref=dst,
            send_sem=ssem.at[k],
            recv_sem=rsem.at[k],
            device_id=device,
            device_id_type=pl.DeviceIdType.MESH,
        )
        copy.start()
        used.append(copy)
        return copy

    def send_all(src, land, devices):
        return [push(src, land.at[d], device) for d, device in devices]

    far_z = sorted(range(1, nz), key=lambda d: min(d, nz - d))
    far_y = sorted(range(1, ny), key=lambda e: -min(e, ny - e))
    far_o = sorted(range(1, no), key=lambda d: -min(d, no - d))
    columns_z = [(d, (z_rep(d), tp)) for d in far_z]
    peers = [(d, (rep, o_tp(d))) for d in far_o]

    need("src_ref")
    src = src_ref[...]
    lane_n = iota((1, n), 1)
    foreign = src != lane_n
    foreign16 = jnp.broadcast_to(hot(foreign), (16, n))
    slot_pick = hot(iota((128, n), 1) == rep * 16 + (iota((128, n), 0) & 15))
    f128 = nt(foreign16, slot_pick)
    before = hot(
        (iota((128, 128), 0) < 16) & (iota((128, 128), 0) < (iota((128, 128), 1) & 15))
    )
    k128 = nn(f128.astype(BF16), before)
    row = iota((16, 128), 0)
    col = iota((16, 128), 1)
    rank = ((row >> 1) & 1).astype(F32)
    place = (f128 > 0.5) & (k128 == rank)
    pack = hot(place & ((row >> 2) == ((col >> 4) & 3)) & ((row & 1) == (col >> 6)))
    pick16 = hot(place & (col < 16))[:, :16]

    need("q_ref", "nk_ref", "x_ref")
    blocks = []
    nothing = jnp.zeros((16, 256), BF16)
    for s in (2, 3):
        x_s = x_ref[s]
        q_s = q_ref[s]
        nk_s = nk_ref[s]
        for b in range(4):
            side = (
                q_s[:, b * 256 : (b + 1) * 256]
                if b < 2
                else (jnp.concatenate([nk_s, nothing[:, :128]], axis=1) if b == 2 else nothing)
            )
            blocks.append(jnp.concatenate([x_s[:, b * 256 : (b + 1) * 256], side], axis=1))
    item = nn(pack, jnp.concatenate(blocks, axis=0)).astype(BF16)
    gather_x[0] = item[:, 0:256]
    gather_q[0] = item[:, 256:512]

    need("conv_ref", "cw_ref", "cb_ref")
    window = [conv_ref[w].astype(F32) for w in range(3)] + [x_ref[s].astype(F32) for s in range(4)]
    conv_last = window[2].astype(BF16)
    cw = cw_ref[...]
    cb = cb_ref[...]
    activ = []
    for s in range(4):
        total = window[s] * cw[0:1]
        for w in range(1, 4):
            total = total + window[s + w] * cw[w : w + 1]
        activ.append(silu(total + cb))
        act[s] = activ[s]
    activ_b = jnp.concatenate([v.astype(BF16) for v in activ], axis=0)
    need("xw")

    def project(rows):
        tail = jnp.concatenate([xw[512:544, :], jnp.zeros((96, 1024), BF16)], axis=0)
        return nt(rows, xw[0:512, :]), nt(rows, tail)

    main, tail = project(activ_b)
    for o in range(no):
        part[o, :, 0:512] = main[o * rpo : (o + 1) * rpo]
        part[o, :, 512:640] = tail[o * rpo : (o + 1) * rpo]
    pl.semaphore_wait(barrier, len(partners))
    pl.semaphore_signal(ready, inc=1, device_id=mirror, device_id_type=pl.DeviceIdType.MESH)

    z_x = send_all(gather_x.at[0], gather_x, columns_z)
    part_out = [
        push(part.at[(own + d) % no], part_land.at[d], (rep, o_tp(d))) for d in range(1, no)
    ]
    z_q = send_all(gather_q.at[0], gather_q, columns_z)
    q_swap = push(q_ref, q_other, (rep, tp_other))
    nk_swap = push(nk_ref, nk_other, (rep, tp_other))

    same = iota((n, n), 0)
    lane_nn = iota((n, n), 1)
    rank16 = nn(foreign16, hot(((same >> 4) == (lane_nn >> 4)) & (same < lane_nn)))
    rank_there = nn(rank16.astype(BF16), hot(same == src))
    home = jnp.where(foreign, (lane_n >> 4) * 2 + rank16[0:1].astype(I32), -1)
    donor = jnp.where(foreign, (src >> 4) * 2 + rank_there[0:1].astype(I32), -1)
    to_row = iota((ny * 16, n), 0)
    to_code = (zi * ny + ((yi + (to_row >> 4)) & (ny - 1))) * 2 + ((to_row >> 1) & 1)
    from_row = iota((nz * 16, n), 0)
    from_code = (((zi - (from_row >> 4)) & (nz - 1)) * ny + yi) * 2 + ((from_row >> 1) & 1)
    r_ = iota((ny * 16, nz * 16), 0)
    c_ = iota((ny * 16, nz * 16), 1)
    alike = ((r_ >> 2) & 3 == (c_ >> 2) & 3) & ((r_ & 1) == (c_ & 1))
    select_in = hot(alike & (nt(hot(donor == to_code), hot(home == from_code)) > 0.5))
    select_out = hot(alike & (nt(hot(home == to_code), hot(donor == from_code)) > 0.5))

    def select(copies, chooser, gathered, staged, landing):
        for copy in copies:
            copy.wait_recv()
        width = gathered.shape[2]
        chosen = nn(chooser, gathered[...].reshape(nz * 16, width)).astype(BF16)
        for e in range(ny):
            staged[e] = chosen[e * 16 : (e + 1) * 16]
        landing[0] = chosen[0:16]
        return [push(staged.at[e], landing.at[e], (y_rep(e), tp)) for e in far_y]

    for copy in part_out:
        copy.wait_recv()
    summed = part[own]
    for d in range(1, no):
        summed = summed + part_land[d]
    blank = jnp.zeros((rpo, 128), F32)

    def pack_half(v):
        return jnp.concatenate(
            [
                jnp.concatenate([v[:, 0:256], v[:, 512:640]], axis=1),
                jnp.concatenate([v[:, 256:512], blank], axis=1),
            ],
            axis=0,
        ).astype(BF16)

    def unpack_half(v):
        v = v.astype(F32)
        return jnp.concatenate([v[:rpo, 0:256], v[rpo:, 0:256], v[:rpo, 256:384]], axis=1)

    half_send[...] = pack_half(summed)

    y_x = select(z_x, select_in, gather_x, stage_x, land_x)
    pl.semaphore_wait(ready, 1)
    half = push(half_send, half_land, (rep, tp_half))

    y_q = select(z_q, select_in, gather_q, stage_q, land_q)
    y_q += [push(stage_q.at[e], land_o.at[e], (y_rep(e), tp_other)) for e in range(ny)]

    need("page_ref", "len_ref")
    own_lane = iota((16, n), 1) == rep * 16 + iota((16, n), 0)
    lengths = jnp.sum(jnp.where(own_lane, len_ref[...], 0), axis=1, keepdims=True)
    foreign_col = (
        jnp.sum(jnp.where(own_lane & foreign, 1.0, 0.0), axis=1, keepdims=True) > 0.5
    )
    table = page_ref[...]
    eye = iota((16, 16), 0) == iota((16, 16), 1)
    cache_lane = iota((16, 1024), 1)
    allowed = jnp.zeros((16, 1024), F32)
    for k in range(4):
        page = jnp.where(core == 0, table[2 * k : 2 * k + 1], table[2 * k + 1 : 2 * k + 2])
        page = jnp.sum(jnp.where(eye, page, 0), axis=1, keepdims=True)
        limit = lengths - (2 * k + core) * 16
        allowed = jnp.where(
            ((cache_lane >> 4) == page) & ((cache_lane & 15) < limit), 1.0, allowed
        )
    mask_ref[...] = allowed.astype(BF16)
    bias_ref[...] = jnp.where(allowed > 0.5, 0.0, MASKED)

    need("pool")
    q_swap.wait_recv()
    nk_swap.wait_recv()
    pages = pool[...].reshape(1024, 256)
    keys, values = pages[:, 0:128], pages[:, 128:256]
    pad64 = jnp.zeros((64, 128), BF16)
    new_keys = [nk_ref[s] for s in range(4)]
    new_values = [nk_other[s] for s in range(4)]
    extra_keys = jnp.concatenate(new_keys + [pad64], axis=0)
    extra_values = jnp.concatenate(new_values + [pad64], axis=0)
    row_q = iota((256, 128), 0)
    col_q = iota((256, 128), 1)
    extra_bias = jnp.where(
        ((row_q & 15) == (col_q & 15)) & ((col_q >> 4) <= (row_q >> 6)) & (core == 0), 0.0, MASKED
    )
    bias16 = bias_ref[...]
    bias = jnp.concatenate([bias16] * 16, axis=0)
    def attend_all(source, target):
        rows = jnp.concatenate(
            [source[s][:, h * 128 : (h + 1) * 128] for s in range(4) for h in range(4)], axis=0
        )
        out, stats = attend(rows, keys, values, extra_keys, extra_values, bias, extra_bias)
        target[:, 0:128] = out
        target[:, 128:256] = stats

    attend_all(q_other, away)
    partial = push(away, far, (rep, tp_other))

    er = iota((128, ny * 16), 0)
    ec = iota((128, ny * 16), 1)
    wanted_step = jnp.where(er < 64, er & 1, 0)
    expand = hot(
        (((er >> 4) & 3) == ((ec >> 2) & 3))
        & (((er >> 1) & 1) == ((ec >> 1) & 1))
        & (wanted_step == (ec & 1))
    )
    last_row = nn(pick16, conv_last)
    x_zero = nn(pick16, x_ref[0])
    x_one = nn(pick16, x_ref[1])
    odd = (iota((16, 1024), 0) & 1) == 1
    known = jnp.where(odd, x_zero, last_row) * cw[0:1]
    known = known + jnp.where(odd, x_one, x_zero) * cw[1:2]
    known = known + jnp.where(odd, 0.0, x_one) * cw[2:3]
    for copy in y_x:
        copy.wait_recv()
    arrived = nn(expand, land_x[...].reshape(ny * 16, 256))
    x_now = jnp.concatenate([arrived[b * 16 : (b + 1) * 16] for b in range(4)], axis=1)
    x_prev = jnp.concatenate(
        [arrived[64 + b * 16 : 64 + (b + 1) * 16] for b in range(4)], axis=1
    )
    total = known + jnp.where(odd, x_prev, 0.0) * cw[2:3] + x_now * cw[3:4]
    late_act = silu(total + cb)
    main, tail = project(late_act.astype(BF16))
    late_own = jnp.concatenate(
        [by_quarter([main[:, b * 128 : (b + 1) * 128] for b in range(4)]), tail], axis=1
    )
    late_send[...] = late_own.astype(BF16)
    late_out = send_all(late_send, late_land, peers)

    attend_all(q_ref, near)

    for copy in late_out:
        copy.wait_recv()
    late_sum = late_own
    for d in range(1, no):
        late_sum = late_sum + late_land[d].astype(F32)
    late_half[...] = late_sum.astype(BF16)
    late_swap = push(late_half, late_half_land, (rep, tp_half))

    need("dtg_ref")
    half.wait_recv()
    summed = summed + unpack_half(half_land[...])
    main = summed[:, 0:512]
    mean = jnp.sum(main * main, axis=1, keepdims=True) / 512.0
    low = main * lax.rsqrt(mean + EPS) * dtg_ref[...]
    normed = jnp.concatenate([low, tail_norm(summed[:, 512:640])], axis=1)
    packed = pack_half(normed)
    norm_send[...] = packed
    norm_out = [push(norm_send, norm_land.at[d], (rep, o_tp(d))) for d in range(1, no)]

    def take(o, v):
        v = unpack_half(v)
        start = pl.multiple_of(o * rpo, rpo)
        dtl[pl.ds(start, rpo), :] = v[:, 0:512]
        tails[pl.ds(start, rpo), :] = v[:, 512:640]

    take(own, packed)

    for copy in y_q:
        copy.wait_recv()
    arrived_q = nn(expand[0:64], land_q[...].reshape(ny * 16, 256))
    arrived_o = nn(expand[0:64], land_o[...].reshape(ny * 16, 256))
    q_late = jnp.concatenate(
        [
            v[(h // 2) * 16 : (h // 2) * 16 + 8, (h % 2) * 128 : (h % 2) * 128 + 128]
            for v in (arrived_q, arrived_o)
            for h in range(4)
        ],
        axis=0,
    ).astype(BF16)
    pad48 = jnp.zeros((48, 128), BF16)
    late_keys = jnp.concatenate(
        new_keys + [arrived_q[32:48, 0:128].astype(BF16), pad48], axis=0
    )
    late_values = jnp.concatenate(
        new_values + [arrived_o[32:48, 0:128].astype(BF16), pad48], axis=0
    )
    fits = (place & (col < 32)) | (
        (col >= 64)
        & (col < 68)
        & (((col >> 1) & 1) == ((row >> 1) & 1))
        & ((col & 1) <= (row & 1))
    )
    late_extra = jnp.where(fits & (core == 0), 0.0, MASKED)[0:8]
    late_bias = jnp.where(nn(pick16, mask_ref[...]) > 0.5, 0.0, MASKED)[0:8]
    out, stats = attend(
        q_late,
        keys,
        values,
        late_keys,
        late_values,
        jnp.concatenate([late_bias] * 8, axis=0),
        jnp.concatenate([late_extra] * 8, axis=0),
    )
    late_near = jnp.concatenate([out[0:32], stats[0:32]], axis=1)
    late_away[...] = jnp.concatenate([out[32:64], stats[32:64]], axis=1)
    late_partial = push(late_away, late_far, (rep, tp_other))

    for d, copy in zip(range(1, no), norm_out):
        copy.wait_recv()
        take((own - d + no) % no, norm_land[d])
    need("dw", "dtb_ref", "bg_ref", "cg_ref", "skip_ref", "a_ref", "ssm")
    steps = softplus(nn(dtl[...].astype(BF16), dw[...]) + dtb_ref[...])
    for s in range(4):
        dts[s] = steps[s * 16 : (s + 1) * 16]
    b_gain = jnp.sum(jnp.where(eye, bg_ref[...], 0.0), axis=1, keepdims=True)
    c_gain = jnp.sum(jnp.where(eye, cg_ref[...], 0.0), axis=1, keepdims=True)
    skip = skip_ref[...]

    def columns(tail_row):
        b = jnp.sum(jnp.where(col == row, tail_row, 0.0), axis=1, keepdims=True) * b_gain
        c = jnp.sum(jnp.where(col == row + 16, tail_row, 0.0), axis=1, keepdims=True) * c_gain
        return b, c

    def advance(state, dt_row, act_row, tail_row):
        b, c = columns(tail_row)
        state = jnp.exp(-dt_row * a_ref[...]) * state + (dt_row * act_row) * b
        return state, jnp.sum(state * c, axis=0, keepdims=True) + skip * act_row

    def scan(first, held, keep):
        def body(i, carry):
            state = held[i]
            for s in (first, first + 1):
                state, out = advance(
                    state,
                    dts[s, pl.ds(i, 1), :],
                    act[s, pl.ds(i, 1), :],
                    tails[pl.ds(s * 16 + i, 1), :],
                )
                mixed[s, pl.ds(i, 1), :] = out
            if keep:
                mid[i] = state
            return carry

        lax.fori_loop(0, 16, body, 0)

    scan(0, ssm, True)

    late_partial.wait_recv()
    heads = combine(late_near, late_far[...]).astype(BF16)
    hr = iota((16, 32), 0)
    hc = iota((16, 32), 1)
    heads = nn(hot(((hr >> 2) == (hc >> 3)) & ((hr & 3) == (hc & 7))), heads)
    gather_a[0] = heads.astype(BF16)
    z_a = [push(gather_a.at[0], gather_a.at[d], (z_rep(d), tp)) for d in range(1, nz)]

    need("src_s")
    gain = dtg_ref[...]
    gains = by_quarter(
        [jnp.broadcast_to(gain[:, b * 128 : (b + 1) * 128], (16, 128)) for b in range(4)]
    )
    wr = iota((64, 16), 0)
    wc = iota((64, 16), 1)
    widen = hot(((wr >> 4) == (wc >> 2)) & ((wr & 3) == (wc & 3)))
    base = rep * 16
    first = jnp.int32(-1)
    second = jnp.int32(0)
    for i in range(16):
        moves = src_s[base + i] != base + i
        second = jnp.where(moves & (first >= 0), i, second)
        first = jnp.where(moves & (first < 0), i, first)
    first = jnp.maximum(first, 0)
    rows = iota((16, 1024), 0) & 3
    states = [mid[first], mid[second]]
    late_swap.wait_recv()
    late_sum = late_sum + late_half_land[...].astype(F32)
    main = late_sum[:, 0:128]
    square = jnp.broadcast_to(jnp.sum(main * main, axis=1, keepdims=True), (16, 128))
    square = square + pltpu.roll(square, 8, 0)
    square = square + pltpu.roll(square, 4, 0)
    low = (main * lax.rsqrt(square / 512.0 + EPS) * gains).astype(BF16)
    spread = nn(widen, low)
    low = jnp.concatenate([spread[b * 16 : (b + 1) * 16] for b in range(4)], axis=1)
    late_dt = softplus(nn(low.astype(BF16), dw[...]) + dtb_ref[...])
    late_tail = tail_norm(late_sum[:, 128:256])

    late_mixed = jnp.zeros((16, 1024), F32)
    for r, state in enumerate(states):
        for s in range(2):
            m = r * 2 + s
            state, out = advance(
                state, late_dt[m : m + 1], late_act[m : m + 1], late_tail[m : m + 1]
            )
            late_mixed = jnp.where(rows == m, out, late_mixed)
    gather_m[0] = by_quarter(
        [late_mixed[:, b * 256 : (b + 1) * 256] for b in range(4)]
    ).astype(BF16)
    z_m = send_all(gather_m.at[0], gather_m, columns_z)

    scan(2, mid, False)
    need("z_ref")
    partial.wait_recv()
    kept = []
    gates = []
    for s in range(4):
        gate = silu(z_ref[s].astype(F32))
        block = combine(near[s * 64 : (s + 1) * 64, :], far[s * 64 : (s + 1) * 64, :])
        block = jnp.concatenate([block[h * 16 : (h + 1) * 16] for h in range(4)], axis=1)
        if s < 2:
            attn_ref[s] = block.astype(BF16)
            mix_ref[s] = (mixed[s] * gate).astype(BF16)
        else:
            kept.append(block)
            gates.append((gate, mixed[s] * gate))

    own_code = rep * 2 + ((iota((ny * 16, n), 0) >> 1) & 1)
    fr = iota((128, ny * 16), 0)
    fc = iota((128, ny * 16), 1)
    put = hot(
        (((fr >> 4) & 3) == ((fc >> 2) & 3))
        & ((fr >> 6) == (fc & 1))
        & (nt(slot_pick, hot(home == own_code)) > 0.5)
    )
    y_m = select(z_m, select_out, gather_m, stage_m, land_m)
    y_a = select(z_a, select_out, gather_a, stage_a, land_a)
    spots = [[s * 64 + b * 16 for b in range(4)] for s in range(2)]
    for copy in y_a:
        copy.wait_recv()
    attended = nn(put, land_a[...].reshape(ny * 16, 128))
    for s in range(2):
        back = jnp.concatenate([attended[p : p + 16] for p in spots[s]], axis=1)
        attn_ref[s + 2] = jnp.where(foreign_col, back, kept[s]).astype(BF16)
    for copy in y_m:
        copy.wait_recv()
    returned = nn(put, land_m[...].reshape(ny * 16, 256))
    for s in range(2):
        back = jnp.concatenate([returned[p : p + 16] for p in spots[s]], axis=1)
        gate, own_mix = gates[s]
        mix_ref[s + 2] = jnp.where(foreign_col, back * gate, own_mix).astype(BF16)

    for copy in used:
        copy.wait_send()


def shards(
    geo,
    queries,
    new_kv,
    kv_pool,
    page_table,
    kv_lengths,
    slot_source,
    mamba_x,
    mamba_z,
    conv_state,
    ssm_state,
    x_proj_weight,
    dt_proj_weight,
    dt_bias,
    a_rate,
    skip_gain,
    conv_weight,
    conv_bias,
    dt_gain,
    b_gain,
    c_gain,
):
    nz, ny, nx = geo
    no = 2 * nx
    rpo = 64 // no
    copies = 4 * (nz - 1) + 4 * (ny - 1) + ny + 3 * (no - 1) + 6
    operands = (
        slot_source.reshape(1, -1),
        queries,
        new_kv,
        mamba_x,
        slot_source,
        conv_state.transpose(1, 0, 2),
        conv_weight,
        conv_bias.reshape(1, -1),
        x_proj_weight,
        page_table.T,
        kv_lengths.reshape(1, -1),
        kv_pool,
        dt_gain.reshape(1, -1),
        dt_proj_weight,
        dt_bias.reshape(1, -1),
        b_gain.reshape(1, -1),
        c_gain.reshape(1, -1),
        skip_gain.reshape(1, -1),
        a_rate,
        ssm_state,
        mamba_z,
    )
    vmem = pl.BlockSpec(memory_space=pltpu.VMEM)
    scratch = [
        pltpu.SMEM(v.shape, v.dtype) if k == 4 else pltpu.VMEM(v.shape, v.dtype)
        for k, v in enumerate(operands)
    ] + [
        pltpu.VMEM((16, 16, 1024), F32),
        pltpu.VMEM((4, 16, 1024), F32),
        pltpu.VMEM((4, 16, 1024), F32),
        pltpu.VMEM((4, 16, 1024), F32),
        pltpu.VMEM((64, 512), F32),
        pltpu.VMEM((64, 128), F32),
        pltpu.VMEM((nz, 16, 256), BF16),
        pltpu.VMEM((ny, 16, 256), BF16),
        pltpu.VMEM((ny, 16, 256), BF16),
        pltpu.VMEM((nz, 16, 256), BF16),
        pltpu.VMEM((ny, 16, 256), BF16),
        pltpu.VMEM((ny, 16, 256), BF16),
        pltpu.VMEM((ny, 16, 256), BF16),
        pltpu.VMEM((4, 16, 512), BF16),
        pltpu.VMEM((4, 16, 128), BF16),
        pltpu.VMEM((no, rpo, 640), F32),
        pltpu.VMEM((no, rpo, 640), F32),
        pltpu.VMEM((2 * rpo, 384), BF16),
        pltpu.VMEM((2 * rpo, 384), BF16),
        pltpu.VMEM((2 * rpo, 384), BF16),
        pltpu.VMEM((no, 2 * rpo, 384), BF16),
        pltpu.VMEM((256, 256), F32),
        pltpu.VMEM((256, 256), F32),
        pltpu.VMEM((256, 256), F32),
        pltpu.VMEM((16, 256), BF16),
        pltpu.VMEM((no, 16, 256), BF16),
        pltpu.VMEM((16, 256), BF16),
        pltpu.VMEM((16, 256), BF16),
        pltpu.VMEM((32, 256), F32),
        pltpu.VMEM((32, 256), F32),
        pltpu.VMEM((nz, 16, 256), BF16),
        pltpu.VMEM((ny, 16, 256), BF16),
        pltpu.VMEM((ny, 16, 256), BF16),
        pltpu.VMEM((nz, 16, 128), BF16),
        pltpu.VMEM((ny, 16, 128), BF16),
        pltpu.VMEM((ny, 16, 128), BF16),
        pltpu.VMEM((16, 1024), F32),
        pltpu.VMEM((16, 1024), BF16),
        pltpu.SemaphoreType.DMA((copies,)),
        pltpu.SemaphoreType.DMA((copies,)),
        pltpu.SemaphoreType.DMA((len(operands),)),
        pltpu.SemaphoreType.REGULAR,
    ]
    return pl.pallas_call(
        functools.partial(kernel, geo),
        out_shape=(
            pltpu.VMEM(queries.shape, BF16),
            pltpu.VMEM(mamba_x.shape, BF16),
        ),
        in_specs=[pl.BlockSpec(memory_space=pl.ANY)] * len(operands),
        out_specs=(vmem, vmem),
        scratch_shapes=scratch,
        compiler_params=pltpu.CompilerParams(
            collective_id=0, has_side_effects=True, vmem_limit_bytes=60 * 1024 * 1024
        ),
    )(*operands)


def solution(mesh):
    placed = (
        P(None, "rep", "tp"),
        P(None, "rep", "tp"),
        P("rep", "tp", None, None),
        P("rep", None),
        P(),
        P(),
        P(None, "rep", "tp"),
        P(None, "rep", "tp"),
        P("rep", None, "tp"),
        P("rep", None, "tp"),
        P(None, "tp"),
        P(None, "tp"),
        P("tp"),
        P(None, "tp"),
        P("tp"),
        P(None, "tp"),
        P("tp"),
        P(),
        P(),
        P(),
    )
    return jax.shard_map(
        functools.partial(shards, geometry(mesh)),
        mesh=mesh,
        in_specs=placed,
        out_specs=(P(None, "rep", "tp"), P(None, "rep", "tp")),
        check_vma=False,
    )
```

```python
import functools

import jax
import jax.numpy as jnp
from jax import lax
from jax.experimental import pallas as pl
from jax.experimental.pallas import tpu as pltpu
from jax.sharding import PartitionSpec as P

F32 = jnp.float32
BF16 = jnp.bfloat16
I32 = jnp.int32
EPS = 1e-06
MASKED = -1e30
SCALE = 128**-0.5


def geometry(mesh):
    rep, tp = mesh.shape["rep"], mesh.shape["tp"]
    ny = 4 if rep >= 16 else 2
    return (rep // ny, ny, tp // 4)


def nn(a, b):
    return lax.dot_general(a, b, (((1,), (0,)), ((), ())), preferred_element_type=F32)


def nt(a, b):
    return lax.dot_general(a, b, (((1,), (1,)), ((), ())), preferred_element_type=F32)


def hot(cond):
    return jnp.where(cond, 1.0, 0.0).astype(BF16)


def iota(shape, dim):
    return lax.broadcasted_iota(I32, shape, dim)


def silu(v):
    return v / (1.0 + jnp.exp(-v))


def softplus(v):
    return jnp.maximum(v, 0.0) + jnp.log1p(jnp.exp(-jnp.abs(v)))


def attend(q_rows, keys, values, extra_keys, extra_values, bias, extra_bias):
    scores = nt(q_rows, keys) * SCALE + bias
    extra = nt(q_rows, extra_keys) * SCALE + extra_bias
    peak = jnp.maximum(
        jnp.max(scores, axis=1, keepdims=True), jnp.max(extra, axis=1, keepdims=True)
    )
    weight = jnp.exp(scores - peak)
    extra_weight = jnp.exp(extra - peak)
    total = jnp.sum(weight, axis=1, keepdims=True) + jnp.sum(extra_weight, axis=1, keepdims=True)
    out = nn(weight.astype(BF16), values) + nn(extra_weight.astype(BF16), extra_values)
    lane = iota((q_rows.shape[0], 128), 1)
    return out, jnp.where(lane < 64, peak, total)


def combine(near, far):
    near_peak, near_sum = near[:, 128:129], near[:, 192:193]
    far_peak, far_sum = far[:, 128:129], far[:, 192:193]
    peak = jnp.maximum(near_peak, far_peak)
    near_scale = jnp.exp(near_peak - peak)
    far_scale = jnp.exp(far_peak - peak)
    numer = near[:, :128] * near_scale + far[:, :128] * far_scale
    return numer / (near_sum * near_scale + far_sum * far_scale)


def tail_norm(tail):
    lane = iota(tail.shape, 1)
    square = tail * tail
    mean_b = jnp.sum(jnp.where(lane < 16, square, 0.0), axis=1, keepdims=True) / 16.0
    mean_c = jnp.sum(
        jnp.where((lane >= 16) & (lane < 32), square, 0.0), axis=1, keepdims=True
    ) / 16.0
    scale = jnp.where(lane < 16, lax.rsqrt(mean_b + EPS), lax.rsqrt(mean_c + EPS))
    return jnp.where(lane < 32, tail * scale, 0.0)


def by_quarter(blocks):
    quarter = iota(blocks[0].shape, 0) >> 2
    return jnp.where(
        quarter == 0,
        blocks[0],
        jnp.where(quarter == 1, blocks[1], jnp.where(quarter == 2, blocks[2], blocks[3])),
    )


def kernel(
    geo,
    src_ref_h,
    q_ref_h,
    nk_ref_h,
    x_ref_h,
    src_s_h,
    conv_ref_h,
    cw_ref_h,
    cb_ref_h,
    xw_h,
    page_ref_h,
    len_ref_h,
    pool_h,
    dtg_ref_h,
    dw_h,
    dtb_ref_h,
    bg_ref_h,
    cg_ref_h,
    skip_ref_h,
    a_ref_h,
    ssm_h,
    z_ref_h,
    attn_ref,
    mix_ref,
    src_ref,
    q_ref,
    nk_ref,
    x_ref,
    src_s,
    conv_ref,
    cw_ref,
    cb_ref,
    xw,
    page_ref,
    len_ref,
    pool,
    dtg_ref,
    dw,
    dtb_ref,
    bg_ref,
    cg_ref,
    skip_ref,
    a_ref,
    ssm,
    z_ref,
    mid,
    act,
    dts,
    mixed,
    dtl,
    tails,
    gather_x,
    stage_x,
    land_x,
    gather_q,
    stage_q,
    land_q,
    land_o,
    q_other,
    nk_other,
    part,
    part_land,
    half_send,
    half_land,
    norm_send,
    norm_land,
    near,
    away,
    far,
    late_send,
    late_land,
    late_half,
    late_half_land,
    late_away,
    late_far,
    gather_m,
    stage_m,
    land_m,
    gather_a,
    stage_a,
    land_a,
    bias_ref,
    mask_ref,
    ssem,
    rsem,
    lsem,
    ready,
):
    nz, ny, nx = geo
    no = 2 * nx
    rpo = 64 // no
    n = src_ref.shape[1]
    rep, tp = lax.axis_index("rep"), lax.axis_index("tp")
    zi, yi = rep // ny, rep % ny
    core, zh, xi = tp % 2, (tp // 2) % 2, tp // 4
    own = xi * 2 + core
    tp_other = tp + 1 - 2 * core
    tp_half = tp + 2 - 4 * zh

    def o_tp(d):
        o = (own + d) % no
        return (o // 2) * 4 + zh * 2 + o % 2

    def z_rep(d):
        return ((zi + d) % nz) * ny + yi

    def y_rep(e):
        return zi * ny + (yi + e) % ny

    partners = [(z_rep(d), tp) for d in range(1, nz)]
    partners += [(y_rep(e), tp) for e in range(1, ny)]
    partners += [(y_rep(e), tp_other) for e in range(1, ny)]
    partners += [(rep, o_tp(d)) for d in range(1, no)]
    mirror = ((nz - 1 - zi) * ny + yi, tp_half)
    partners += [mirror]
    barrier = pltpu.get_barrier_semaphore()
    for device in partners:
        pl.semaphore_signal(
            barrier, inc=1, device_id=device, device_id_type=pl.DeviceIdType.MESH
        )

    loads = {}
    for k, (name, a, b) in enumerate(
        (
            ("src_ref", src_ref_h, src_ref),
            ("q_ref", q_ref_h, q_ref),
            ("nk_ref", nk_ref_h, nk_ref),
            ("x_ref", x_ref_h, x_ref),
            ("src_s", src_s_h, src_s),
            ("conv_ref", conv_ref_h, conv_ref),
            ("cw_ref", cw_ref_h, cw_ref),
            ("cb_ref", cb_ref_h, cb_ref),
            ("xw", xw_h, xw),
            ("page_ref", page_ref_h, page_ref),
            ("len_ref", len_ref_h, len_ref),
            ("pool", pool_h, pool),
            ("dtg_ref", dtg_ref_h, dtg_ref),
            ("dw", dw_h, dw),
            ("dtb_ref", dtb_ref_h, dtb_ref),
            ("bg_ref", bg_ref_h, bg_ref),
            ("cg_ref", cg_ref_h, cg_ref),
            ("skip_ref", skip_ref_h, skip_ref),
            ("a_ref", a_ref_h, a_ref),
            ("ssm", ssm_h, ssm),
            ("z_ref", z_ref_h, z_ref),
        )
    ):
        loads[name] = pltpu.make_async_copy(a, b, lsem.at[k])
        loads[name].start()

    def need(*names):
        for name in names:
            loads[name].wait()

    used = []

    def push(src, dst, device):
        k = len(used)
        copy = pltpu.make_async_remote_copy(
            src_ref=src,
            dst_ref=dst,
            send_sem=ssem.at[k],
            recv_sem=rsem.at[k],
            device_id=device,
            device_id_type=pl.DeviceIdType.MESH,
        )
        copy.start()
        used.append(copy)
        return copy

    def send_all(src, land, devices):
        return [push(src, land.at[d], device) for d, device in devices]

    far_z = sorted(range(1, nz), key=lambda d: min(d, nz - d))
    far_y = sorted(range(1, ny), key=lambda e: -min(e, ny - e))
    far_o = sorted(range(1, no), key=lambda d: -min(d, no - d))
    columns_z = [(d, (z_rep(d), tp)) for d in far_z]
    peers = [(d, (rep, o_tp(d))) for d in far_o]

    need("src_ref")
    src = src_ref[...]
    lane_n = iota((1, n), 1)
    foreign = src != lane_n
    foreign16 = jnp.broadcast_to(hot(foreign), (16, n))
    slot_pick = hot(iota((128, n), 1) == rep * 16 + (iota((128, n), 0) & 15))
    f128 = nt(foreign16, slot_pick)
    before = hot(
        (iota((128, 128), 0) < 16) & (iota((128, 128), 0) < (iota((128, 128), 1) & 15))
    )
    k128 = nn(f128.astype(BF16), before)
    row = iota((16, 128), 0)
    col = iota((16, 128), 1)
    rank = ((row >> 1) & 1).astype(F32)
    place = (f128 > 0.5) & (k128 == rank)
    pack = hot(place & ((row >> 2) == ((col >> 4) & 3)) & ((row & 1) == (col >> 6)))
    pick16 = hot(place & (col < 16))[:, :16]

    need("q_ref", "nk_ref", "x_ref")
    blocks = []
    nothing = jnp.zeros((16, 256), BF16)
    for s in (2, 3):
        x_s = x_ref[s]
        q_s = q_ref[s]
        nk_s = nk_ref[s]
        for b in range(4):
            side = (
                q_s[:, b * 256 : (b + 1) * 256]
                if b < 2
                else (jnp.concatenate([nk_s, nothing[:, :128]], axis=1) if b == 2 else nothing)
            )
            blocks.append(jnp.concatenate([x_s[:, b * 256 : (b + 1) * 256], side], axis=1))
    item = nn(pack, jnp.concatenate(blocks, axis=0)).astype(BF16)
    gather_x[0] = item[:, 0:256]
    gather_q[0] = item[:, 256:512]

    need("conv_ref", "cw_ref", "cb_ref")
    window = [conv_ref[w].astype(F32) for w in range(3)] + [x_ref[s].astype(F32) for s in range(4)]
    conv_last = window[2].astype(BF16)
    cw = cw_ref[...]
    cb = cb_ref[...]
    activ = []
    for s in range(4):
        total = window[s] * cw[0:1]
        for w in range(1, 4):
            total = total + window[s + w] * cw[w : w + 1]
        activ.append(silu(total + cb))
        act[s] = activ[s]
    activ_b = jnp.concatenate([v.astype(BF16) for v in activ], axis=0)
    need("xw")

    def project(rows):
        tail = jnp.concatenate([xw[512:544, :], jnp.zeros((96, 1024), BF16)], axis=0)
        return nt(rows, xw[0:512, :]), nt(rows, tail)

    main, tail = project(activ_b)
    for o in range(no):
        part[o, :, 0:512] = main[o * rpo : (o + 1) * rpo]
        part[o, :, 512:640] = tail[o * rpo : (o + 1) * rpo]
    pl.semaphore_wait(barrier, len(partners))
    pl.semaphore_signal(ready, inc=1, device_id=mirror, device_id_type=pl.DeviceIdType.MESH)

    z_x = send_all(gather_x.at[0], gather_x, columns_z)
    part_out = [
        push(part.at[(own + d) % no], part_land.at[d], (rep, o_tp(d))) for d in range(1, no)
    ]
    z_q = send_all(gather_q.at[0], gather_q, columns_z)
    q_swap = push(q_ref, q_other, (rep, tp_other))
    nk_swap = push(nk_ref, nk_other, (rep, tp_other))

    same = iota((n, n), 0)
    lane_nn = iota((n, n), 1)
    rank16 = nn(foreign16, hot(((same >> 4) == (lane_nn >> 4)) & (same < lane_nn)))
    rank_there = nn(rank16.astype(BF16), hot(same == src))
    home = jnp.where(foreign, (lane_n >> 4) * 2 + rank16[0:1].astype(I32), -1)
    donor = jnp.where(foreign, (src >> 4) * 2 + rank_there[0:1].astype(I32), -1)
    to_row = iota((ny * 16, n), 0)
    to_code = (zi * ny + ((yi + (to_row >> 4)) & (ny - 1))) * 2 + ((to_row >> 1) & 1)
    from_row = iota((nz * 16, n), 0)
    from_code = (((zi - (from_row >> 4)) & (nz - 1)) * ny + yi) * 2 + ((from_row >> 1) & 1)
    r_ = iota((ny * 16, nz * 16), 0)
    c_ = iota((ny * 16, nz * 16), 1)
    alike = ((r_ >> 2) & 3 == (c_ >> 2) & 3) & ((r_ & 1) == (c_ & 1))
    select_in = hot(alike & (nt(hot(donor == to_code), hot(home == from_code)) > 0.5))
    select_out = hot(alike & (nt(hot(home == to_code), hot(donor == from_code)) > 0.5))

    def select(copies, chooser, gathered, staged, landing):
        for copy in copies:
            copy.wait_recv()
        width = gathered.shape[2]
        chosen = nn(chooser, gathered[...].reshape(nz * 16, width)).astype(BF16)
        for e in range(ny):
            staged[e] = chosen[e * 16 : (e + 1) * 16]
        landing[0] = chosen[0:16]
        return [push(staged.at[e], landing.at[e], (y_rep(e), tp)) for e in far_y]

    for copy in part_out:
        copy.wait_recv()
    summed = part[own]
    for d in range(1, no):
        summed = summed + part_land[d]
    blank = jnp.zeros((rpo, 128), F32)

    def pack_half(v):
        return jnp.concatenate(
            [
                jnp.concatenate([v[:, 0:256], v[:, 512:640]], axis=1),
                jnp.concatenate([v[:, 256:512], blank], axis=1),
            ],
            axis=0,
        ).astype(BF16)

    def unpack_half(v):
        v = v.astype(F32)
        return jnp.concatenate([v[:rpo, 0:256], v[rpo:, 0:256], v[:rpo, 256:384]], axis=1)

    half_send[...] = pack_half(summed)

    y_x = select(z_x, select_in, gather_x, stage_x, land_x)
    pl.semaphore_wait(ready, 1)
    half = push(half_send, half_land, (rep, tp_half))

    y_q = select(z_q, select_in, gather_q, stage_q, land_q)
    y_q += [push(stage_q.at[e], land_o.at[e], (y_rep(e), tp_other)) for e in range(ny)]

    need("page_ref", "len_ref")
    own_lane = iota((16, n), 1) == rep * 16 + iota((16, n), 0)
    lengths = jnp.sum(jnp.where(own_lane, len_ref[...], 0), axis=1, keepdims=True)
    foreign_col = (
        jnp.sum(jnp.where(own_lane & foreign, 1.0, 0.0), axis=1, keepdims=True) > 0.5
    )
    table = page_ref[...]
    eye = iota((16, 16), 0) == iota((16, 16), 1)
    cache_lane = iota((16, 1024), 1)
    allowed = jnp.zeros((16, 1024), F32)
    for k in range(4):
        page = jnp.where(core == 0, table[2 * k : 2 * k + 1], table[2 * k + 1 : 2 * k + 2])
        page = jnp.sum(jnp.where(eye, page, 0), axis=1, keepdims=True)
        limit = lengths - (2 * k + core) * 16
        allowed = jnp.where(
            ((cache_lane >> 4) == page) & ((cache_lane & 15) < limit), 1.0, allowed
        )
    mask_ref[...] = allowed.astype(BF16)
    bias_ref[...] = jnp.where(allowed > 0.5, 0.0, MASKED)

    need("pool")
    q_swap.wait_recv()
    nk_swap.wait_recv()
    pages = pool[...].reshape(1024, 256)
    keys, values = pages[:, 0:128], pages[:, 128:256]
    pad64 = jnp.zeros((64, 128), BF16)
    new_keys = [nk_ref[s] for s in range(4)]
    new_values = [nk_other[s] for s in range(4)]
    extra_keys = jnp.concatenate(new_keys + [pad64], axis=0)
    extra_values = jnp.concatenate(new_values + [pad64], axis=0)
    row_q = iota((256, 128), 0)
    col_q = iota((256, 128), 1)
    extra_bias = jnp.where(
        ((row_q & 15) == (col_q & 15)) & ((col_q >> 4) <= (row_q >> 6)) & (core == 0), 0.0, MASKED
    )
    bias16 = bias_ref[...]
    bias = jnp.concatenate([bias16] * 16, axis=0)
    def attend_all(source, target):
        rows = jnp.concatenate(
            [source[s][:, h * 128 : (h + 1) * 128] for s in range(4) for h in range(4)], axis=0
        )
        out, stats = attend(rows, keys, values, extra_keys, extra_values, bias, extra_bias)
        target[:, 0:128] = out
        target[:, 128:256] = stats

    attend_all(q_other, away)
    partial = push(away, far, (rep, tp_other))

    er = iota((128, ny * 16), 0)
    ec = iota((128, ny * 16), 1)
    wanted_step = jnp.where(er < 64, er & 1, 0)
    expand = hot(
        (((er >> 4) & 3) == ((ec >> 2) & 3))
        & (((er >> 1) & 1) == ((ec >> 1) & 1))
        & (wanted_step == (ec & 1))
    )
    last_row = nn(pick16, conv_last)
    x_zero = nn(pick16, x_ref[0])
    x_one = nn(pick16, x_ref[1])
    odd = (iota((16, 1024), 0) & 1) == 1
    known = jnp.where(odd, x_zero, last_row) * cw[0:1]
    known = known + jnp.where(odd, x_one, x_zero) * cw[1:2]
    known = known + jnp.where(odd, 0.0, x_one) * cw[2:3]
    for copy in y_x:
        copy.wait_recv()
    arrived = nn(expand, land_x[...].reshape(ny * 16, 256))
    x_now = jnp.concatenate([arrived[b * 16 : (b + 1) * 16] for b in range(4)], axis=1)
    x_prev = jnp.concatenate(
        [arrived[64 + b * 16 : 64 + (b + 1) * 16] for b in range(4)], axis=1
    )
    total = known + jnp.where(odd, x_prev, 0.0) * cw[2:3] + x_now * cw[3:4]
    late_act = silu(total + cb)
    main, tail = project(late_act.astype(BF16))
    late_own = jnp.concatenate(
        [by_quarter([main[:, b * 128 : (b + 1) * 128] for b in range(4)]), tail], axis=1
    )
    late_send[...] = late_own.astype(BF16)
    late_out = send_all(late_send, late_land, peers)

    attend_all(q_ref, near)

    for copy in late_out:
        copy.wait_recv()
    late_sum = late_own
    for d in range(1, no):
        late_sum = late_sum + late_land[d].astype(F32)
    late_half[...] = late_sum.astype(BF16)
    late_swap = push(late_half, late_half_land, (rep, tp_half))

    need("dtg_ref")
    half.wait_recv()
    summed = summed + unpack_half(half_land[...])
    main = summed[:, 0:512]
    mean = jnp.sum(main * main, axis=1, keepdims=True) / 512.0
    low = main * lax.rsqrt(mean + EPS) * dtg_ref[...]
    normed = jnp.concatenate([low, tail_norm(summed[:, 512:640])], axis=1)
    packed = pack_half(normed)
    norm_send[...] = packed
    norm_out = [push(norm_send, norm_land.at[d], (rep, o_tp(d))) for d in range(1, no)]

    def take(o, v):
        v = unpack_half(v)
        start = pl.multiple_of(o * rpo, rpo)
        dtl[pl.ds(start, rpo), :] = v[:, 0:512]
        tails[pl.ds(start, rpo), :] = v[:, 512:640]

    take(own, packed)

    for copy in y_q:
        copy.wait_recv()
    arrived_q = nn(expand[0:64], land_q[...].reshape(ny * 16, 256))
    arrived_o = nn(expand[0:64], land_o[...].reshape(ny * 16, 256))
    q_late = jnp.concatenate(
        [
            v[(h // 2) * 16 : (h // 2) * 16 + 8, (h % 2) * 128 : (h % 2) * 128 + 128]
            for v in (arrived_q, arrived_o)
            for h in range(4)
        ],
        axis=0,
    ).astype(BF16)
    pad48 = jnp.zeros((48, 128), BF16)
    late_keys = jnp.concatenate(
        new_keys + [arrived_q[32:48, 0:128].astype(BF16), pad48], axis=0
    )
    late_values = jnp.concatenate(
        new_values + [arrived_o[32:48, 0:128].astype(BF16), pad48], axis=0
    )
    fits = (place & (col < 32)) | (
        (col >= 64)
        & (col < 68)
        & (((col >> 1) & 1) == ((row >> 1) & 1))
        & ((col & 1) <= (row & 1))
    )
    late_extra = jnp.where(fits & (core == 0), 0.0, MASKED)[0:8]
    late_bias = jnp.where(nn(pick16, mask_ref[...]) > 0.5, 0.0, MASKED)[0:8]
    out, stats = attend(
        q_late,
        keys,
        values,
        late_keys,
        late_values,
        jnp.concatenate([late_bias] * 8, axis=0),
        jnp.concatenate([late_extra] * 8, axis=0),
    )
    late_near = jnp.concatenate([out[0:32], stats[0:32]], axis=1)
    late_away[...] = jnp.concatenate([out[32:64], stats[32:64]], axis=1)
    late_partial = push(late_away, late_far, (rep, tp_other))

    for d, copy in zip(range(1, no), norm_out):
        copy.wait_recv()
        take((own - d + no) % no, norm_land[d])
    need("dw", "dtb_ref", "bg_ref", "cg_ref", "skip_ref", "a_ref", "ssm")
    steps = softplus(nn(dtl[...].astype(BF16), dw[...]) + dtb_ref[...])
    for s in range(4):
        dts[s] = steps[s * 16 : (s + 1) * 16]
    b_gain = jnp.sum(jnp.where(eye, bg_ref[...], 0.0), axis=1, keepdims=True)
    c_gain = jnp.sum(jnp.where(eye, cg_ref[...], 0.0), axis=1, keepdims=True)
    skip = skip_ref[...]

    def columns(tail_row):
        b = jnp.sum(jnp.where(col == row, tail_row, 0.0), axis=1, keepdims=True) * b_gain
        c = jnp.sum(jnp.where(col == row + 16, tail_row, 0.0), axis=1, keepdims=True) * c_gain
        return b, c

    def advance(state, dt_row, act_row, tail_row):
        b, c = columns(tail_row)
        state = jnp.exp(-dt_row * a_ref[...]) * state + (dt_row * act_row) * b
        return state, jnp.sum(state * c, axis=0, keepdims=True) + skip * act_row

    def scan(first, held, keep):
        def body(i, carry):
            state = held[i]
            for s in (first, first + 1):
                state, out = advance(
                    state,
                    dts[s, pl.ds(i, 1), :],
                    act[s, pl.ds(i, 1), :],
                    tails[pl.ds(s * 16 + i, 1), :],
                )
                mixed[s, pl.ds(i, 1), :] = out
            if keep:
                mid[i] = state
            return carry

        lax.fori_loop(0, 16, body, 0)

    scan(0, ssm, True)

    late_partial.wait_recv()
    heads = combine(late_near, late_far[...]).astype(BF16)
    hr = iota((16, 32), 0)
    hc = iota((16, 32), 1)
    heads = nn(hot(((hr >> 2) == (hc >> 3)) & ((hr & 3) == (hc & 7))), heads)
    gather_a[0] = heads.astype(BF16)
    z_a = [push(gather_a.at[0], gather_a.at[d], (z_rep(d), tp)) for d in range(1, nz)]

    need("src_s")
    gain = dtg_ref[...]
    gains = by_quarter(
        [jnp.broadcast_to(gain[:, b * 128 : (b + 1) * 128], (16, 128)) for b in range(4)]
    )
    wr = iota((64, 16), 0)
    wc = iota((64, 16), 1)
    widen = hot(((wr >> 4) == (wc >> 2)) & ((wr & 3) == (wc & 3)))
    base = rep * 16
    first = jnp.int32(-1)
    second = jnp.int32(0)
    for i in range(16):
        moves = src_s[base + i] != base + i
        second = jnp.where(moves & (first >= 0), i, second)
        first = jnp.where(moves & (first < 0), i, first)
    first = jnp.maximum(first, 0)
    rows = iota((16, 1024), 0) & 3
    states = [mid[first], mid[second]]
    late_swap.wait_recv()
    late_sum = late_sum + late_half_land[...].astype(F32)
    main = late_sum[:, 0:128]
    square = jnp.broadcast_to(jnp.sum(main * main, axis=1, keepdims=True), (16, 128))
    square = square + pltpu.roll(square, 8, 0)
    square = square + pltpu.roll(square, 4, 0)
    low = (main * lax.rsqrt(square / 512.0 + EPS) * gains).astype(BF16)
    spread = nn(widen, low)
    low = jnp.concatenate([spread[b * 16 : (b + 1) * 16] for b in range(4)], axis=1)
    late_dt = softplus(nn(low.astype(BF16), dw[...]) + dtb_ref[...])
    late_tail = tail_norm(late_sum[:, 128:256])

    late_mixed = jnp.zeros((16, 1024), F32)
    for s in range(2):
        for r in range(2):
            m = r * 2 + s
            states[r], out = advance(
                states[r], late_dt[m : m + 1], late_act[m : m + 1], late_tail[m : m + 1]
            )
            late_mixed = jnp.where(rows == m, out, late_mixed)
    gather_m[0] = by_quarter(
        [late_mixed[:, b * 256 : (b + 1) * 256] for b in range(4)]
    ).astype(BF16)
    z_m = send_all(gather_m.at[0], gather_m, columns_z)

    scan(2, mid, False)
    need("z_ref")
    partial.wait_recv()
    kept = []
    gates = []
    for s in range(4):
        gate = silu(z_ref[s].astype(F32))
        block = combine(near[s * 64 : (s + 1) * 64, :], far[s * 64 : (s + 1) * 64, :])
        block = jnp.concatenate([block[h * 16 : (h + 1) * 16] for h in range(4)], axis=1)
        if s < 2:
            attn_ref[s] = block.astype(BF16)
            mix_ref[s] = (mixed[s] * gate).astype(BF16)
        else:
            kept.append(block)
            gates.append((gate, mixed[s] * gate))

    own_code = rep * 2 + ((iota((ny * 16, n), 0) >> 1) & 1)
    fr = iota((128, ny * 16), 0)
    fc = iota((128, ny * 16), 1)
    put = hot(
        (((fr >> 4) & 3) == ((fc >> 2) & 3))
        & ((fr >> 6) == (fc & 1))
        & (nt(slot_pick, hot(home == own_code)) > 0.5)
    )
    y_m = select(z_m, select_out, gather_m, stage_m, land_m)
    y_a = select(z_a, select_out, gather_a, stage_a, land_a)
    spots = [[s * 64 + b * 16 for b in range(4)] for s in range(2)]
    for copy in y_a:
        copy.wait_recv()
    attended = nn(put, land_a[...].reshape(ny * 16, 128))
    for s in range(2):
        back = jnp.concatenate([attended[p : p + 16] for p in spots[s]], axis=1)
        attn_ref[s + 2] = jnp.where(foreign_col, back, kept[s]).astype(BF16)
    for copy in y_m:
        copy.wait_recv()
    returned = nn(put, land_m[...].reshape(ny * 16, 256))
    for s in range(2):
        back = jnp.concatenate([returned[p : p + 16] for p in spots[s]], axis=1)
        gate, own_mix = gates[s]
        mix_ref[s + 2] = jnp.where(foreign_col, back * gate, own_mix).astype(BF16)

    for copy in used:
        copy.wait_send()


def shards(
    geo,
    queries,
    new_kv,
    kv_pool,
    page_table,
    kv_lengths,
    slot_source,
    mamba_x,
    mamba_z,
    conv_state,
    ssm_state,
    x_proj_weight,
    dt_proj_weight,
    dt_bias,
    a_rate,
    skip_gain,
    conv_weight,
    conv_bias,
    dt_gain,
    b_gain,
    c_gain,
):
    nz, ny, nx = geo
    no = 2 * nx
    rpo = 64 // no
    copies = 4 * (nz - 1) + 4 * (ny - 1) + ny + 3 * (no - 1) + 6
    operands = (
        slot_source.reshape(1, -1),
        queries,
        new_kv,
        mamba_x,
        slot_source,
        conv_state.transpose(1, 0, 2),
        conv_weight,
        conv_bias.reshape(1, -1),
        x_proj_weight,
        page_table.T,
        kv_lengths.reshape(1, -1),
        kv_pool,
        dt_gain.reshape(1, -1),
        dt_proj_weight,
        dt_bias.reshape(1, -1),
        b_gain.reshape(1, -1),
        c_gain.reshape(1, -1),
        skip_gain.reshape(1, -1),
        a_rate,
        ssm_state,
        mamba_z,
    )
    vmem = pl.BlockSpec(memory_space=pltpu.VMEM)
    scratch = [
        pltpu.SMEM(v.shape, v.dtype) if k == 4 else pltpu.VMEM(v.shape, v.dtype)
        for k, v in enumerate(operands)
    ] + [
        pltpu.VMEM((16, 16, 1024), F32),
        pltpu.VMEM((4, 16, 1024), F32),
        pltpu.VMEM((4, 16, 1024), F32),
        pltpu.VMEM((4, 16, 1024), F32),
        pltpu.VMEM((64, 512), F32),
        pltpu.VMEM((64, 128), F32),
        pltpu.VMEM((nz, 16, 256), BF16),
        pltpu.VMEM((ny, 16, 256), BF16),
        pltpu.VMEM((ny, 16, 256), BF16),
        pltpu.VMEM((nz, 16, 256), BF16),
        pltpu.VMEM((ny, 16, 256), BF16),
        pltpu.VMEM((ny, 16, 256), BF16),
        pltpu.VMEM((ny, 16, 256), BF16),
        pltpu.VMEM((4, 16, 512), BF16),
        pltpu.VMEM((4, 16, 128), BF16),
        pltpu.VMEM((no, rpo, 640), F32),
        pltpu.VMEM((no, rpo, 640), F32),
        pltpu.VMEM((2 * rpo, 384), BF16),
        pltpu.VMEM((2 * rpo, 384), BF16),
        pltpu.VMEM((2 * rpo, 384), BF16),
        pltpu.VMEM((no, 2 * rpo, 384), BF16),
        pltpu.VMEM((256, 256), F32),
        pltpu.VMEM((256, 256), F32),
        pltpu.VMEM((256, 256), F32),
        pltpu.VMEM((16, 256), BF16),
        pltpu.VMEM((no, 16, 256), BF16),
        pltpu.VMEM((16, 256), BF16),
        pltpu.VMEM((16, 256), BF16),
        pltpu.VMEM((32, 256), F32),
        pltpu.VMEM((32, 256), F32),
        pltpu.VMEM((nz, 16, 256), BF16),
        pltpu.VMEM((ny, 16, 256), BF16),
        pltpu.VMEM((ny, 16, 256), BF16),
        pltpu.VMEM((nz, 16, 128), BF16),
        pltpu.VMEM((ny, 16, 128), BF16),
        pltpu.VMEM((ny, 16, 128), BF16),
        pltpu.VMEM((16, 1024), F32),
        pltpu.VMEM((16, 1024), BF16),
        pltpu.SemaphoreType.DMA((copies,)),
        pltpu.SemaphoreType.DMA((copies,)),
        pltpu.SemaphoreType.DMA((len(operands),)),
        pltpu.SemaphoreType.REGULAR,
    ]
    return pl.pallas_call(
        functools.partial(kernel, geo),
        out_shape=(
            pltpu.VMEM(queries.shape, BF16),
            pltpu.VMEM(mamba_x.shape, BF16),
        ),
        in_specs=[pl.BlockSpec(memory_space=pl.ANY)] * len(operands),
        out_specs=(vmem, vmem),
        scratch_shapes=scratch,
        compiler_params=pltpu.CompilerParams(
            collective_id=0, has_side_effects=True, vmem_limit_bytes=60 * 1024 * 1024
        ),
    )(*operands)


def solution(mesh):
    placed = (
        P(None, "rep", "tp"),
        P(None, "rep", "tp"),
        P("rep", "tp", None, None),
        P("rep", None),
        P(),
        P(),
        P(None, "rep", "tp"),
        P(None, "rep", "tp"),
        P("rep", None, "tp"),
        P("rep", None, "tp"),
        P(None, "tp"),
        P(None, "tp"),
        P("tp"),
        P(None, "tp"),
        P("tp"),
        P(None, "tp"),
        P("tp"),
        P(),
        P(),
        P(),
    )
    return jax.shard_map(
        functools.partial(shards, geometry(mesh)),
        mesh=mesh,
        in_specs=placed,
        out_specs=(P(None, "rep", "tp"), P(None, "rep", "tp")),
        check_vma=False,
    )
```
